32 devices in a mesh: dp: 8 (over z, y), fsdp: 4 (over x, core).
Axes of the slice: x: 2, y: 2, z: 4, core: 2. Of those that a mesh axis runs over, the one named last changes fastest.
Arguments:
- tokens: bfloat16 [8192, 960], P(('dp', 'fsdp')), may hold values from -6 to 6
- cotangent: bfloat16 [8192, 960], P(('dp', 'fsdp')), may hold values from -6 to 6
- sequence_ids: int32 [32], P('dp'), may hold values from 0 to 31, as said below
- span_position: int32 [32], P('dp'), may hold values from 0 to 3, as said below
- attention_norm: bfloat16 [960], P('fsdp'), may hold values from 0.5 to 1.5
- query_weight: bfloat16 [960, 960], P('fsdp'), may hold values from -0.1875 to 0.1875
- key_matrix: bfloat16 [960, 320], P('fsdp'), may hold values from -0.1875 to 0.1875
- value_matrix: bfloat16 [960, 320], P('fsdp'), may hold values from -0.1875 to 0.1875
- output_weight: bfloat16 [960, 960], P('fsdp'), may hold values from -0.5 to 0.5
- feedforward_norm: bfloat16 [960], P('fsdp'), may hold values from 0.5 to 1.5
- gate_weight: bfloat16 [960, 2560], P('fsdp'), may hold values from -0.1875 to 0.1875
- up_weight: bfloat16 [960, 2560], P('fsdp'), may hold values from -0.1875 to 0.1875
- down_weight: bfloat16 [2560, 960], P('fsdp'), may hold values from -0.125 to 0.125
Outputs:
- activations: bfloat16 [8192, 960], P(('dp', 'fsdp'))
- input_grad: bfloat16 [8192, 960], P(('dp', 'fsdp'))
- attention_norm_grad: float32 [960], P('fsdp')
- query_grad: float32 [960, 960], P('fsdp')
- key_grad: float32 [960, 320], P('fsdp')
- value_grad: float32 [960, 320], P('fsdp')
- output_grad: float32 [960, 960], P('fsdp')
- feedforward_norm_grad: float32 [960], P('fsdp')
- gate_grad: float32 [960, 2560], P('fsdp')
- up_grad: float32 [960, 2560], P('fsdp')
- down_grad: float32 [2560, 960], P('fsdp')
The draws below stay inside these ranges and needn't reach their ends.
Inputs may be any that keep to these rules, and one draw needn't show every extreme that they name: `sequence_ids`: spans with equal ids lie in one group of 4 consecutive spans (one index of dp). A group holds either one sequence of 4 spans or 4 sequences of one span each; every draw has a group with one sequence of 4 spans. `span_position`: within a sequence the spans carry the places 0 to its number of spans - 1, each once, in any order over its group; a sequence of one span has place 0.
All inputs are finite; a program needn't handle non-finite values.
Results may differ from the reference program's by a relative error of at most 0.024.
Values may be sent and summed in bfloat16 or wider, within the bound.
No kernel may reach another device: no remote copies, remote signals or barrier semaphores. Data moves between devices by JAX's collectives and lax.ppermute only.
A program may use at most 192 MiB of HBM per device.

```python
import jax
import jax.numpy as jnp
from jax import lax

MODEL_WIDTH = 960
QUERY_HEADS = 15
KEY_VALUE_HEADS = 5
HEAD_SIZE = 64
FF = 2560
SPAN = 256
SPANS = 32
TOKENS = 8192
N_DP = 8
N_FSDP = 4


def span_layout(key):
    group_kind = jax.random.randint(jax.random.fold_in(key, 11), (N_DP,), 0, 4)
    forced = jax.random.randint(jax.random.fold_in(key, 12), (), 0, N_DP)
    groups = jnp.arange(N_DP, dtype=jnp.int32)
    members = jnp.arange(N_FSDP, dtype=jnp.int32)
    single = (group_kind > 0) | (groups == forced)
    scores = jax.random.randint(jax.random.fold_in(key, 13), (N_DP, N_FSDP), 0, 1 << 20) * N_FSDP + members[None, :]
    order_rank = jnp.argsort(jnp.argsort(scores, axis=1, stable=True), axis=1, stable=True).astype(jnp.int32)
    positions = jnp.where(single[:, None], order_rank, 0)
    whole_label = jnp.where(groups == 0, 0, N_FSDP - 1)
    labels = groups[:, None] * N_FSDP + jnp.where(single[:, None], whole_label[:, None], members[None, :])
    return (labels.reshape(N_DP * N_FSDP).astype(jnp.int32), positions.reshape(N_DP * N_FSDP).astype(jnp.int32))


def draw_sequence_ids(key, part):
    return span_layout(key)[0]


def draw_span_position(key, part):
    return span_layout(key)[1]


def steps_of(own_key, extent, shards, low, largest):
    loudness, own = 1.0, jax.random.fold_in(own_key, 6)
    for position, parts in shards:
        steps = jnp.exp(jax.random.uniform(jax.random.fold_in(own, position), (parts,), jnp.float32, low / len(shards), largest / len(shards)))
        loudness = loudness * jnp.repeat(steps, extent[position] // parts).reshape([-1 if axis == position else 1 for axis in range(len(extent))])
    return loudness


def centred(stream_key, extent, spread, limit, split=(), kind=jnp.bfloat16):
    gain = steps_of(stream_key, extent, split, -0.22, 0.18) if split else 1.0
    values = jax.random.normal(stream_key, extent, jnp.float32) * spread * gain
    return jnp.minimum(jnp.maximum(values, -limit), limit).astype(kind)


def setup_inputs(seed: int = 0) -> dict:
    key_of = jax.random.split(jax.random.key(seed), 14)
    tokens = centred(key_of[0], (TOKENS, MODEL_WIDTH), 1.0, 6.0, ((0, 32),))
    cotangent = centred(key_of[1], (TOKENS, MODEL_WIDTH), 1.0, 6.0, ((0, 32),))
    sequence_ids = draw_sequence_ids(jax.random.fold_in(key_of[13], 71), 0)
    span_position = draw_span_position(jax.random.fold_in(key_of[13], 71), 0)
    attention_norm = jnp.clip(1.0 + 0.1 * jax.random.normal(key_of[4], (MODEL_WIDTH,), jnp.float32), 0.5, 1.5).astype(jnp.bfloat16)
    query_weight = centred(key_of[5], (MODEL_WIDTH, QUERY_HEADS * HEAD_SIZE), MODEL_WIDTH ** -0.5, 0.1875, ((0, 4),))
    key_matrix = centred(key_of[6], (MODEL_WIDTH, KEY_VALUE_HEADS * HEAD_SIZE), MODEL_WIDTH ** -0.5, 0.1875, ((0, 4),))
    value_matrix = centred(key_of[7], (MODEL_WIDTH, KEY_VALUE_HEADS * HEAD_SIZE), MODEL_WIDTH ** -0.5, 0.1875, ((0, 4),))
    output_weight = centred(key_of[8], (QUERY_HEADS * HEAD_SIZE, MODEL_WIDTH), (MODEL_WIDTH // 8) ** -0.5, 0.5, ((0, 4),))
    feedforward_norm = jnp.clip(1.0 + 0.1 * jax.random.normal(key_of[9], (MODEL_WIDTH,), jnp.float32), 0.5, 1.5).astype(jnp.bfloat16)
    gate_weight = centred(key_of[10], (MODEL_WIDTH, FF), MODEL_WIDTH ** -0.5, 0.1875, ((0, 4),))
    up_weight = centred(key_of[11], (MODEL_WIDTH, FF), MODEL_WIDTH ** -0.5, 0.1875, ((0, 4),))
    down_weight = centred(key_of[12], (FF, MODEL_WIDTH), FF ** -0.5, 0.125, ((0, 4),))
    return {"tokens": tokens, "cotangent": cotangent, "sequence_ids": sequence_ids, "span_position": span_position, "attention_norm": attention_norm, "query_weight": query_weight, "key_matrix": key_matrix, "value_matrix": value_matrix, "output_weight": output_weight, "feedforward_norm": feedforward_norm, "gate_weight": gate_weight, "up_weight": up_weight, "down_weight": down_weight}


@jax.custom_vjp
def lower_precision(v):
    return lax.optimization_barrier(v.astype(jnp.bfloat16)).astype(jnp.float32)

@jax.custom_vjp
def lower_precision_reverse(v):
    return v

def low_keep(v):
    return (lower_precision(v), None)

def low_pass(kept, grad):
    return (grad,)

def back_keep(v):
    return (v, None)

def back_low(kept, grad):
    return (lower_precision(grad),)
lower_precision.defvjp(low_keep, low_pass)
lower_precision_reverse.defvjp(back_keep, back_low)
epsilon = 1e-05
rope_base = 10000.0
masked = -1e+30

def product_result(left_side, right_side):
    return jnp.dot(left_side, right_side, precision=lax.Precision.HIGHEST)

def rmsnorm(hidden, norm_gain):
    return hidden * lax.rsqrt(lax.optimization_barrier(jnp.mean(hidden * hidden, axis=-1, keepdims=True)) + epsilon) * norm_gain

def apply_rotation(vector, token_positions):
    half_dim = vector.shape[-1] // 2
    frequency = rope_base ** (-jnp.arange(half_dim, dtype=jnp.float32) / half_dim)
    angles = token_positions.astype(jnp.float32)[:, None] * frequency[None, :]
    cosine_table = jnp.cos(angles)[:, None, :]
    sine_table = jnp.sin(angles)[:, None, :]
    first_half = vector[..., :half_dim]
    second = vector[..., half_dim:]
    return jnp.concatenate([first_half * cosine_table - second * sine_table, second * cosine_table + first_half * sine_table], axis=-1)

def layer_block(hidden, params, token_positions, allowed):
    attention_norm, query_weight, key_matrix, value_matrix, output_weight, feedforward_norm, gate_weight, up_weight, down_weight = params
    token_count = hidden.shape[0]
    normalized_input = lower_precision(rmsnorm(hidden, attention_norm))
    query_rows = lower_precision_reverse(product_result(normalized_input, query_weight)).reshape(token_count, QUERY_HEADS, HEAD_SIZE)
    query_rows = lower_precision(apply_rotation(query_rows, token_positions)).reshape(token_count, KEY_VALUE_HEADS, QUERY_HEADS // KEY_VALUE_HEADS, HEAD_SIZE)
    rotated_keys = lower_precision(apply_rotation(lower_precision_reverse(product_result(normalized_input, key_matrix)).reshape(token_count, KEY_VALUE_HEADS, HEAD_SIZE), token_positions))
    value_rows = lower_precision(lower_precision_reverse(product_result(normalized_input, value_matrix))).reshape(token_count, KEY_VALUE_HEADS, HEAD_SIZE)
    scores = jnp.einsum('qhgd,khd->hgqk', query_rows, rotated_keys, precision=lax.Precision.HIGHEST)
    scores = jnp.where(allowed, lower_precision_reverse(scores * HEAD_SIZE ** (-0.5)), masked)
    row_peak = lax.optimization_barrier(jnp.max(scores, axis=-1, keepdims=True))
    raised = jnp.exp(scores - row_peak)
    softened = lower_precision(raised / lax.optimization_barrier(jnp.sum(raised, axis=-1, keepdims=True)))
    attended_rows = jnp.einsum('hgqk,khd->qhgd', softened, value_rows, precision=lax.Precision.HIGHEST)
    attended_rows = lower_precision_reverse(lower_precision(attended_rows.reshape(token_count, QUERY_HEADS * HEAD_SIZE)))
    middle = hidden + lower_precision_reverse(product_result(attended_rows, output_weight))
    normed_ffn = lower_precision(rmsnorm(middle, feedforward_norm))
    gating = lower_precision_reverse(product_result(normed_ffn, gate_weight))
    upward = lower_precision_reverse(product_result(normed_ffn, up_weight))
    activation = lower_precision(gating * jax.nn.sigmoid(gating) * upward)
    return middle + lower_precision_reverse(product_result(activation, down_weight))

def reference(tokens, cotangent, sequence_ids, span_position, attention_norm, query_weight, key_matrix, value_matrix, output_weight, feedforward_norm, gate_weight, up_weight, down_weight):
    group_rows = SPAN * N_FSDP
    params = tuple((weight.astype(jnp.float32) for weight in (attention_norm, query_weight, key_matrix, value_matrix, output_weight, feedforward_norm, gate_weight, up_weight, down_weight)))
    offsets = jnp.arange(SPAN, dtype=jnp.int32)
    token_positions = (span_position.astype(jnp.int32)[:, None] * SPAN + offsets[None, :]).reshape(N_DP, group_rows)
    owners = jnp.broadcast_to(sequence_ids.astype(jnp.int32)[:, None], (SPANS, SPAN)).reshape(N_DP, group_rows)
    starting = tokens.astype(jnp.float32).reshape(N_DP, group_rows, MODEL_WIDTH)

    def forward(starting, params):
        checked_block = jax.checkpoint(layer_block)

        def one_group(entries):
            hidden, place_row, owner_row = entries
            allowed = (owner_row[:, None] == owner_row[None, :]) & (place_row[None, :] <= place_row[:, None])
            after = checked_block(hidden, params, place_row, allowed)
            return checked_block(after, params, place_row, allowed)
        return lax.map(one_group, (starting, token_positions, owners))
    finish, pullback = jax.vjp(forward, starting, params)
    starting_grad, param_grads = pullback(cotangent.astype(jnp.float32).reshape(N_DP, group_rows, MODEL_WIDTH))
    return (finish.reshape(TOKENS, MODEL_WIDTH).astype(jnp.bfloat16), starting_grad.reshape(TOKENS, MODEL_WIDTH).astype(jnp.bfloat16), param_grads[0], param_grads[1], param_grads[2], param_grads[3], param_grads[4], param_grads[5], param_grads[6], param_grads[7], param_grads[8])
```

```python
import jax
import jax.numpy as jnp
from jax import lax
from jax.sharding import PartitionSpec as P

QUERY_HEADS = 15
KEY_VALUE_HEADS = 5
HEAD_SIZE = 64


epsilon = 1e-05
rope_base = 10000.0
masked = -1e30


def matrix_product(left_side, right_side):
    return jnp.dot(left_side, right_side, preferred_element_type=jnp.float32)


def first_trans(left_side, right_side):
    return lax.dot_general(
        left_side, right_side, (((0,), (0,)), ((), ())), preferred_element_type=jnp.float32
    )


def second_trans(left_side, right_side):
    return lax.dot_general(
        left_side, right_side, (((1,), (1,)), ((), ())), preferred_element_type=jnp.float32
    )


def rotation(token_positions, half_dim):
    frequency = rope_base ** (-jnp.arange(half_dim, dtype=jnp.float32) / half_dim)
    angles = token_positions.astype(jnp.float32)[:, None] * frequency[None, :]
    return (jnp.cos(angles)[:, None, :], jnp.sin(angles)[:, None, :])


def apply_rotation(vector, cosine_table, sine_table):
    half_dim = vector.shape[-1] // 2
    first_half = vector[..., :half_dim]
    second = vector[..., half_dim:]
    return jnp.concatenate(
        [
            first_half * cosine_table - second * sine_table,
            second * cosine_table + first_half * sine_table,
        ],
        axis=-1,
    )


def normalize(hidden):
    return hidden * lax.rsqrt(jnp.mean(hidden * hidden, axis=-1, keepdims=True) + epsilon)


def norm_back(grad_unit, unitized, hidden):
    factor = lax.rsqrt(jnp.mean(hidden * hidden, axis=-1, keepdims=True) + epsilon)
    return factor * (grad_unit - unitized * jnp.mean(grad_unit * unitized, axis=-1, keepdims=True))


def unchanged(carried):
    return carried


def split_slab(key_rows_block):
    key_total_width = KEY_VALUE_HEADS * HEAD_SIZE
    row_number = key_rows_block.shape[0]
    return (
        key_rows_block[:, :key_total_width].reshape(row_number, KEY_VALUE_HEADS, HEAD_SIZE),
        key_rows_block[:, key_total_width:].reshape(row_number, KEY_VALUE_HEADS, HEAD_SIZE),
    )


def raw_scores(query_rows, keys_part, allowed):
    scores = jnp.einsum(
        "qhgd,khd->hgqk", query_rows, keys_part, preferred_element_type=jnp.float32
    ) * HEAD_SIZE ** (-0.5)
    return jnp.where(allowed, scores, masked)


def attention_inputs(hidden, complete_weights, cosine_table, sine_table):
    row_number = hidden.shape[0]
    unitized = normalize(hidden)
    normalized_input = (unitized * complete_weights[0]).astype(jnp.bfloat16)
    query_rows = apply_rotation(
        matrix_product(normalized_input, complete_weights[1]).reshape(
            row_number, QUERY_HEADS, HEAD_SIZE
        ),
        cosine_table,
        sine_table,
    )
    query_rows = query_rows.astype(jnp.bfloat16).reshape(
        row_number, KEY_VALUE_HEADS, QUERY_HEADS // KEY_VALUE_HEADS, HEAD_SIZE
    )
    rotated_keys = apply_rotation(
        matrix_product(normalized_input, complete_weights[2]).reshape(
            row_number, KEY_VALUE_HEADS, HEAD_SIZE
        ),
        cosine_table,
        sine_table,
    )
    rotated_keys = rotated_keys.astype(jnp.bfloat16).reshape(
        row_number, KEY_VALUE_HEADS * HEAD_SIZE
    )
    value_rows = matrix_product(normalized_input, complete_weights[3]).astype(jnp.bfloat16)
    return (
        unitized,
        normalized_input,
        query_rows,
        jnp.concatenate([rotated_keys, value_rows], axis=1),
    )


def feedforward_front(middle, complete_weights):
    unit_ffn = normalize(middle)
    normed_ffn = (unit_ffn * complete_weights[5]).astype(jnp.bfloat16)
    gating = matrix_product(normed_ffn, complete_weights[6])
    upward = matrix_product(normed_ffn, complete_weights[7])
    sigmoid_gate = jax.nn.sigmoid(gating)
    activation = (gating * sigmoid_gate * upward).astype(jnp.bfloat16)
    return (unit_ffn, normed_ffn, gating, upward, sigmoid_gate, activation)


def attention_forward(query_rows, gathered, layout):
    visible, allowed = layout
    row_number = query_rows.shape[0]
    statistics_shape = (KEY_VALUE_HEADS, QUERY_HEADS // KEY_VALUE_HEADS, row_number, 1)
    row_peak = jnp.full(statistics_shape, masked, jnp.float32)
    row_total = jnp.zeros(statistics_shape, jnp.float32)
    for member in range(len(visible)):
        key_rows_block = gathered[member * row_number : (member + 1) * row_number]

        def update(carried, key_rows_block=key_rows_block, mask_here=allowed[member]):
            old_peak, old_total = carried
            scores = raw_scores(query_rows, split_slab(key_rows_block)[0], mask_here)
            new_peak = jnp.maximum(old_peak, jnp.max(scores, axis=-1, keepdims=True))
            new_total = old_total * jnp.exp(old_peak - new_peak) + jnp.sum(
                jnp.exp(scores - new_peak), axis=-1, keepdims=True
            )
            return (new_peak, new_total)

        row_peak, row_total = lax.cond(visible[member], update, unchanged, (row_peak, row_total))
    attended_rows = jnp.zeros(
        (row_number, KEY_VALUE_HEADS, QUERY_HEADS // KEY_VALUE_HEADS, HEAD_SIZE), jnp.float32
    )
    for member in range(len(visible)):
        key_rows_block = gathered[member * row_number : (member + 1) * row_number]

        def accumulate(running, key_rows_block=key_rows_block, mask_here=allowed[member]):
            keys_part, values_part = split_slab(key_rows_block)
            softened = (
                jnp.exp(raw_scores(query_rows, keys_part, mask_here) - row_peak) / row_total
            ).astype(jnp.bfloat16)
            return running + jnp.einsum(
                "hgqk,khd->qhgd", softened, values_part, preferred_element_type=jnp.float32
            )

        attended_rows = lax.cond(visible[member], accumulate, unchanged, attended_rows)
    return (attended_rows.reshape(row_number, QUERY_HEADS * HEAD_SIZE), row_peak, row_total)


def attention_backward(query_rows, gathered, layout, row_peak, row_total, attended_gradient):
    visible, allowed = layout
    row_number = query_rows.shape[0]
    head_gradient = attended_gradient.reshape(
        row_number, KEY_VALUE_HEADS, QUERY_HEADS // KEY_VALUE_HEADS, HEAD_SIZE
    )
    score_scale = HEAD_SIZE ** (-0.5)

    def probabilities(key_rows_block, mask_here):
        keys_part, values_part = split_slab(key_rows_block)
        softened = jnp.exp(raw_scores(query_rows, keys_part, mask_here) - row_peak) / row_total
        grad_prob = jnp.einsum(
            "qhgd,khd->hgqk", head_gradient, values_part, preferred_element_type=jnp.float32
        )
        return (keys_part, softened, grad_prob)

    row_difference = jnp.zeros(
        (KEY_VALUE_HEADS, QUERY_HEADS // KEY_VALUE_HEADS, row_number, 1), jnp.float32
    )
    for member in range(len(visible)):
        key_rows_block = gathered[member * row_number : (member + 1) * row_number]

        def delta_add(running, key_rows_block=key_rows_block, mask_here=allowed[member]):
            parts = probabilities(key_rows_block, mask_here)
            return running + jnp.sum(parts[2] * parts[1], axis=-1, keepdims=True)

        row_difference = lax.cond(visible[member], delta_add, unchanged, row_difference)
    query_gradient = jnp.zeros(
        (row_number, KEY_VALUE_HEADS, QUERY_HEADS // KEY_VALUE_HEADS, HEAD_SIZE), jnp.float32
    )
    empty_buffer = jnp.zeros((row_number, KEY_VALUE_HEADS, HEAD_SIZE), jnp.float32)
    pieces = []
    for member in range(len(visible)):
        key_rows_block = gathered[member * row_number : (member + 1) * row_number]

        def member_grads(running, key_rows_block=key_rows_block, mask_here=allowed[member]):
            keys_part, softened, grad_prob = probabilities(key_rows_block, mask_here)
            grad_score = (softened * (grad_prob - row_difference)).astype(
                jnp.bfloat16
            ) * score_scale
            key_gradient = jnp.einsum(
                "hgqk,qhgd->khd", grad_score, query_rows, preferred_element_type=jnp.float32
            )
            value_gradient = jnp.einsum(
                "hgqk,qhgd->khd",
                softened.astype(jnp.bfloat16),
                head_gradient,
                preferred_element_type=jnp.float32,
            )
            moved = running + jnp.einsum(
                "hgqk,khd->qhgd", grad_score, keys_part, preferred_element_type=jnp.float32
            )
            return (moved, key_gradient, value_gradient)

        def skipped(running):
            return (running, empty_buffer, empty_buffer)

        query_gradient, key_gradient, value_gradient = lax.cond(
            visible[member], member_grads, skipped, query_gradient
        )
        pieces.append(
            jnp.concatenate(
                [
                    key_gradient.reshape(row_number, KEY_VALUE_HEADS * HEAD_SIZE),
                    value_gradient.reshape(row_number, KEY_VALUE_HEADS * HEAD_SIZE),
                ],
                axis=1,
            )
        )
    return (query_gradient, jnp.concatenate(pieces, axis=0))


def flip(value, axis_name, distance):
    size = lax.axis_size(axis_name)
    return lax.ppermute(value, axis_name, [(i, i ^ distance) for i in range(size)])


def pick(condition, when_true, when_false):
    return jnp.where(condition, when_true, when_false)


def quarters(value):
    width = value.shape[1] // 4
    return [value[:, i * width : (i + 1) * width] for i in range(4)]


def order_by(bit, own, other):
    return (pick(bit == 1, other, own), pick(bit == 1, own, other))


def gather_direct(shard):
    core = lax.axis_index("fsdp") % 2
    chip = lax.axis_index("fsdp") // 2
    beside = flip(shard, "fsdp", 1)
    across = flip(shard, "fsdp", 2)
    diagonal = flip(across, "fsdp", 1)
    near = order_by(core, shard, beside)
    far = order_by(core, across, diagonal)
    low = [pick(chip == 1, f, n) for n, f in zip(near, far)]
    high = [pick(chip == 1, n, f) for n, f in zip(near, far)]
    return jnp.concatenate(low + high, axis=0)


def gather_shared(shard):
    core = lax.axis_index("fsdp") % 2
    chip = lax.axis_index("fsdp") // 2
    first = lax.axis_index("dp") % 2
    second = (lax.axis_index("dp") // 2) % 2
    beside = flip(shard, "fsdp", 1)
    parts = quarters(shard)
    mine = pick(second == 1, pick(first == 1, parts[3], parts[2]), pick(first == 1, parts[1], parts[0]))
    got = flip(mine, "fsdp", 2)
    half = got.shape[1] // 2
    left, right = got[:, :half], got[:, half:]
    left_y = flip(left, "dp", 1)
    right_z = flip(right, "dp", 2)
    left_pair = order_by(first, left, left_y)
    right_pair = order_by(second, right, right_z)
    left_row = jnp.concatenate(left_pair, axis=1)
    right_row = jnp.concatenate(right_pair, axis=1)
    left_far = flip(left_row, "dp", 2)
    right_far = flip(right_row, "dp", 1)
    left_rows = order_by(second, left_row, left_far)
    right_rows = order_by(first, right_row, right_far)
    pieces = []
    for b2 in range(2):
        for b1 in range(2):
            pieces.append(left_rows[b2][:, b1 * half : (b1 + 1) * half])
            pieces.append(right_rows[b1][:, b2 * half : (b2 + 1) * half])
    across = jnp.concatenate(pieces, axis=1)
    diagonal = flip(across, "fsdp", 1)
    near = order_by(core, shard, beside)
    far = order_by(core, across, diagonal)
    low = [pick(chip == 1, f, n) for n, f in zip(near, far)]
    high = [pick(chip == 1, n, f) for n, f in zip(near, far)]
    return jnp.concatenate(low + high, axis=0)


def gather_rows(block):
    core = lax.axis_index("fsdp") % 2
    chip = lax.axis_index("fsdp") // 2
    beside = flip(block, "fsdp", 1)
    across = flip(block, "fsdp", 2)
    diagonal = flip(across, "fsdp", 1)
    near = order_by(core, block, beside)
    far = order_by(core, across, diagonal)
    low = [pick(chip == 1, f, n) for n, f in zip(near, far)]
    high = [pick(chip == 1, n, f) for n, f in zip(near, far)]
    return jnp.concatenate(low + high, axis=0)


def add_short(one, other):
    return (one.astype(jnp.float32) + other.astype(jnp.float32)).astype(jnp.bfloat16)


def scatter_group(blocks):
    core = lax.axis_index("fsdp") % 2
    chip = lax.axis_index("fsdp") // 2
    keep = [pick(core == 1, row[1], row[0]) for row in blocks]
    send = [pick(core == 1, row[0], row[1]) for row in blocks]
    got = flip(jnp.concatenate(send, axis=0), "fsdp", 1)
    rows = keep[0].shape[0]
    summed = [add_short(keep[0], got[:rows]), add_short(keep[1], got[rows:])]
    got = flip(pick(chip == 1, summed[0], summed[1]), "fsdp", 2)
    return add_short(pick(chip == 1, summed[1], summed[0]), got)


def reduce_rows(blocks):
    size = lax.axis_size("dp")
    index = lax.axis_index("dp")
    first = index % 2
    second = (index // 2) % 2
    own = scatter_group(blocks)
    width = own.shape[1] // 2
    got = flip(pick(first == 1, own[:, :width], own[:, width:]), "dp", 1)
    own = add_short(pick(first == 1, own[:, width:], own[:, :width]), got)
    width = width // 2
    got = flip(pick(second == 1, own[:, :width], own[:, width:]), "dp", 2)
    own = add_short(pick(second == 1, own[:, width:], own[:, :width]), got)
    distance = 4
    while distance < size:
        own = add_short(own, flip(own, "dp", distance))
        distance *= 2
    own = jnp.concatenate(order_by(second, own, flip(own, "dp", 2)), axis=1)
    own = jnp.concatenate(order_by(first, own, flip(own, "dp", 1)), axis=1)
    return own.astype(jnp.float32)


def blocks_of(total):
    rows = total.shape[0] // 4
    total = total.astype(jnp.bfloat16)
    return [[total[(2 * a + b) * rows : (2 * a + b + 1) * rows] for b in range(2)] for a in range(2)]


def forward_run(hidden, complete_weights, cosine_table, sine_table, layout):
    unitized, normalized_input, query_rows, key_rows_block = attention_inputs(
        hidden, complete_weights, cosine_table, sine_table
    )
    gathered = gather_rows(key_rows_block)
    attended_rows, row_peak, row_total = attention_forward(query_rows, gathered, layout)
    attended_rows = attended_rows.astype(jnp.bfloat16)
    middle = hidden + matrix_product(attended_rows, complete_weights[4])
    activation = feedforward_front(middle, complete_weights)[5]
    return (
        middle + matrix_product(activation, complete_weights[8]),
        attended_rows,
        row_peak,
        row_total,
        gathered,
    )


def backward_run(
    hidden,
    attended_rows,
    row_peak,
    row_total,
    gathered,
    grad_after,
    complete_weights,
    cosine_table,
    sine_table,
    layout,
):
    (
        attention_norm,
        query_weight,
        key_matrix,
        value_matrix,
        output_weight,
        feedforward_norm,
        gate_weight,
        up_weight,
        down_weight,
    ) = complete_weights
    row_number = hidden.shape[0]
    key_total_width = KEY_VALUE_HEADS * HEAD_SIZE
    unitized, normalized_input, query_rows, key_rows_block = attention_inputs(
        hidden, complete_weights, cosine_table, sine_table
    )
    middle = hidden + matrix_product(attended_rows, output_weight)
    unit_ffn, normed_ffn, gating, upward, sigmoid_gate, activation = feedforward_front(
        middle, complete_weights
    )
    grad_branch = grad_after.astype(jnp.bfloat16)
    grad_inner = second_trans(grad_branch, down_weight)
    grad_gating = (
        grad_inner * upward * (sigmoid_gate * (1.0 + gating * (1.0 - sigmoid_gate)))
    ).astype(jnp.bfloat16)
    grad_upward = (grad_inner * (gating * sigmoid_gate)).astype(jnp.bfloat16)
    grad_normed_ffn = second_trans(grad_gating, gate_weight) + second_trans(grad_upward, up_weight)
    ffn_gain_grad = jnp.sum(grad_normed_ffn * unit_ffn, axis=0)
    grad_middle = grad_after + norm_back(grad_normed_ffn * feedforward_norm, unit_ffn, middle)
    grad_mixed = grad_middle.astype(jnp.bfloat16)
    attended_gradient = second_trans(grad_mixed, output_weight).astype(jnp.bfloat16)
    query_gradient, key_terms = attention_backward(
        query_rows, gathered, layout, row_peak, row_total, attended_gradient
    )
    diagonal_terms = scatter_group(blocks_of(key_terms)).astype(jnp.float32)
    grad_queries = (
        apply_rotation(
            query_gradient.reshape(row_number, QUERY_HEADS, HEAD_SIZE), cosine_table, -sine_table
        )
        .astype(jnp.bfloat16)
        .reshape(row_number, QUERY_HEADS * HEAD_SIZE)
    )
    key_gradient = (
        apply_rotation(
            diagonal_terms[:, :key_total_width].reshape(row_number, KEY_VALUE_HEADS, HEAD_SIZE),
            cosine_table,
            -sine_table,
        )
        .astype(jnp.bfloat16)
        .reshape(row_number, key_total_width)
    )
    value_gradient = diagonal_terms[:, key_total_width:].astype(jnp.bfloat16)
    grad_normed = (
        second_trans(grad_queries, query_weight)
        + second_trans(key_gradient, key_matrix)
        + second_trans(value_gradient, value_matrix)
    )
    attn_gain_grad = jnp.sum(grad_normed * unitized, axis=0)
    grad_hidden = grad_middle + norm_back(grad_normed * attention_norm, unitized, hidden)
    factors = (
        (normalized_input, jnp.concatenate([grad_queries, key_gradient, value_gradient], axis=1)),
        (attended_rows, grad_mixed),
        (normed_ffn, jnp.concatenate([grad_gating, grad_upward], axis=1)),
        (activation, grad_branch),
        (attn_gain_grad, ffn_gain_grad),
    )
    return (grad_hidden, factors)


def body(
    tokens,
    cotangent,
    sequence_ids,
    span_position,
    attention_norm,
    query_weight,
    key_matrix,
    value_matrix,
    output_weight,
    feedforward_norm,
    gate_weight,
    up_weight,
    down_weight,
):
    width = output_weight.shape[1]
    key_total_width = key_matrix.shape[1]
    ffn_width = gate_weight.shape[1]
    first_end = width + key_total_width
    second_end = first_end + key_total_width
    attention_weights = gather_shared(
        jnp.concatenate([query_weight, key_matrix, value_matrix, output_weight], axis=1)
    )
    gains = gather_rows(jnp.stack([attention_norm, feedforward_norm], axis=1))
    ffn_weights = gather_shared(jnp.concatenate([gate_weight, up_weight], axis=1))
    complete_weights = (
        gains[:, 0],
        attention_weights[:, :width],
        attention_weights[:, width:first_end],
        attention_weights[:, first_end:second_end],
        attention_weights[:, second_end:],
        gains[:, 1],
        ffn_weights[:, :ffn_width],
        ffn_weights[:, ffn_width:],
        gather_direct(down_weight),
    )
    row_number = tokens.shape[0]
    member_count = lax.axis_size("fsdp")
    itself = lax.axis_index("fsdp")
    own_sequence = sequence_ids[itself]
    own_place = span_position[itself]
    offsets = jnp.arange(row_number, dtype=jnp.int32)
    query_places = own_place * row_number + offsets
    cosine_table, sine_table = rotation(query_places, HEAD_SIZE // 2)
    visible = []
    allowed = []
    for member in range(member_count):
        visible.append(
            (sequence_ids[member] == own_sequence) & (span_position[member] <= own_place)
        )
        allowed.append(
            (span_position[member] * row_number + offsets)[None, :] <= query_places[:, None]
        )
    layout = (visible, allowed)
    hidden = tokens.astype(jnp.float32)
    stored = []
    for repeat in range(2):
        finish, attended_rows, row_peak, row_total, gathered = forward_run(
            hidden, complete_weights, cosine_table, sine_table, layout
        )
        stored.append((hidden, attended_rows, row_peak, row_total, gathered))
        hidden = finish
    activations = hidden.astype(jnp.bfloat16)
    grad_hidden = cotangent.astype(jnp.float32)
    factors = []
    for repeat in (1, 0):
        stored_hidden, attended_rows, row_peak, row_total, gathered = stored[repeat]
        grad_hidden, run_factors = backward_run(
            stored_hidden,
            attended_rows,
            row_peak,
            row_total,
            gathered,
            grad_hidden,
            complete_weights,
            cosine_table,
            sine_table,
            layout,
        )
        factors.append(run_factors)

    def both(entry):
        left = jnp.concatenate([run[entry][0] for run in factors], axis=0)
        right = jnp.concatenate([run[entry][1] for run in factors], axis=0)
        return first_trans(left, right)

    ffn_width = gate_weight.shape[1]
    width = output_weight.shape[1]
    key_total_width = key_matrix.shape[1]
    down_grad = reduce_rows(blocks_of(both(3)))
    gate_up = both(2)
    gate_grad = reduce_rows(blocks_of(gate_up[:, :ffn_width]))
    up_grad = reduce_rows(blocks_of(gate_up[:, ffn_width:]))
    shard_rows = query_weight.shape[0]
    attention_grad = jnp.concatenate([both(0), both(1)], axis=1).astype(jnp.bfloat16)
    gains = [factors[0][4][i] + factors[1][4][i] for i in range(2)]
    extra = jnp.stack(gains).reshape(2, 4, shard_rows).transpose(1, 0, 2).reshape(4, 1, 2 * shard_rows)
    extra = jnp.pad(extra, ((0, 0), (0, 15), (0, attention_grad.shape[1] - 2 * shard_rows)))
    extra = extra.astype(jnp.bfloat16)
    rows = attention_grad.shape[0] // 4
    blocks = [
        [
            jnp.concatenate(
                [attention_grad[(2 * a + b) * rows : (2 * a + b + 1) * rows], extra[2 * a + b]], axis=0
            )
            for b in range(2)
        ]
        for a in range(2)
    ]
    mixed = reduce_rows(blocks)
    first_end = width + key_total_width
    second_end = first_end + key_total_width
    return (
        activations,
        grad_hidden.astype(jnp.bfloat16),
        mixed[rows, :shard_rows],
        mixed[:rows, :width],
        mixed[:rows, width:first_end],
        mixed[:rows, first_end:second_end],
        mixed[:rows, second_end:],
        mixed[rows, shard_rows : 2 * shard_rows],
        gate_grad,
        up_grad,
        down_grad,
    )


def solution(mesh):
    return jax.shard_map(
        body,
        mesh=mesh,
        in_specs=(
            P(("dp", "fsdp"), None),
            P(("dp", "fsdp"), None),
            P("dp"),
            P("dp"),
            P("fsdp"),
            P("fsdp", None),
            P("fsdp", None),
            P("fsdp", None),
            P("fsdp", None),
            P("fsdp"),
            P("fsdp", None),
            P("fsdp", None),
            P("fsdp", None),
        ),
        out_specs=(
            P(("dp", "fsdp"), None),
            P(("dp", "fsdp"), None),
            P("fsdp"),
            P("fsdp", None),
            P("fsdp", None),
            P("fsdp", None),
            P("fsdp", None),
            P("fsdp"),
            P("fsdp", None),
            P("fsdp", None),
            P("fsdp", None),
        ),
        check_vma=False,
    )
```

```python
import functools

import jax
import jax.numpy as jnp
from jax import lax
from jax.experimental import pallas as pl
from jax.experimental.pallas import tpu as pltpu
from jax.sharding import PartitionSpec as P

QUERY_HEADS = 15
KEY_VALUE_HEADS = 5
HEAD_SIZE = 64
SHARING = QUERY_HEADS // KEY_VALUE_HEADS
HALF = HEAD_SIZE // 2

epsilon = 1e-05
rope_base = 10000.0
masked = -1e30
score_scale = HEAD_SIZE ** (-0.5)

bf16 = jnp.bfloat16
f32 = jnp.float32
VMEM_BYTES = 56 * 1024 * 1024
GAIN_ROWS = 16


def nn(left, right):
    return jnp.dot(left, right, preferred_element_type=f32)


def nt(left, right):
    return lax.dot_general(left, right, (((1,), (1,)), ((), ())), preferred_element_type=f32)


def in_vmem():
    return pl.BlockSpec(memory_space=pltpu.VMEM)


def in_smem():
    return pl.BlockSpec(memory_space=pltpu.SMEM)


def anywhere():
    return pl.BlockSpec(memory_space=pl.ANY)


def params():
    return pltpu.CompilerParams(vmem_limit_bytes=VMEM_BYTES)


def shape(dims, dtype):
    return jax.ShapeDtypeStruct(dims, dtype)


def cost(flops, bytes_accessed):
    return pl.CostEstimate(flops=int(flops), bytes_accessed=int(bytes_accessed), transcendentals=0)


def inverse_rms(hidden):
    return lax.rsqrt(jnp.mean(hidden * hidden, axis=-1, keepdims=True) + epsilon)


def pack_kernel(
    bits_ref, query_ref, key_ref, value_ref, out_ref, gate_hbm, up_hbm, packed_ref, mine_ref, gate_ref,
    up_ref, sems,
):
    half = gate_ref.shape[1]
    loads = [
        pltpu.make_async_copy(
            source.at[:, pl.ds(pl.multiple_of(bits_ref[i] * half, 128), half)], target, sems.at[i]
        )
        for i, (source, target) in enumerate(((gate_hbm, gate_ref), (up_hbm, up_ref)))
    ]
    for load in loads:
        load.start()
    packed_ref[...] = jnp.concatenate(
        [
            query_ref[...].astype(f32),
            key_ref[...].astype(f32).T,
            value_ref[...].astype(f32).T,
            out_ref[...].astype(f32),
        ],
        axis=1,
    ).astype(bf16)
    wide = mine_ref.shape[1]
    mine_ref[...] = packed_ref[:, pl.ds(pl.multiple_of(bits_ref[0] * wide, 128), wide)]
    for load in loads:
        load.wait()


def pack(bits, query, key_t, value_t, out, gate, up):
    rows, width = query.shape
    columns = 2 * width + 2 * key_t.shape[0]
    return pl.pallas_call(
        pack_kernel,
        out_shape=(
            shape((rows, columns), bf16),
            shape((rows, columns // 2), bf16),
        )
        + (shape((rows, gate.shape[1] // 2), bf16),) * 2,
        in_specs=[in_smem()] + [in_vmem()] * 4 + [anywhere()] * 2,
        out_specs=(in_vmem(),) * 4,
        scratch_shapes=[pltpu.SemaphoreType.DMA((2,))],
        compiler_params=params(),
        cost_estimate=cost(0, 8 * rows * columns),
        name="pack",
    )(bits, query, key_t, value_t, out, gate, up)


def piece_copies(plan, bits_ref, sources, target_ref, sems):
    me = bits_ref[2]
    copies = []
    for i, (which, member, column, part, bit) in enumerate(plan):
        source = sources[which]
        height, width = source.shape
        if column is None:
            turned = pl.ds(pl.multiple_of((me ^ member) * width, 128), width)
            if part is None:
                rows = pl.ds(0, height)
            else:
                rows = pl.ds(pl.multiple_of((bits_ref[bit] ^ part) * height, 16), height)
            target = target_ref.at[rows, turned]
        else:
            rows = pl.ds(pl.multiple_of((me ^ member) * height, 16), height)
            if part is None:
                columns = pl.ds(column, width)
            else:
                columns = pl.ds(
                    pl.multiple_of(column + (bits_ref[bit] ^ part) * width, 128), width
                )
            target = target_ref.at[rows, columns]
        copies.append(pltpu.make_async_copy(source, target, sems.at[i]))
    return copies


def shared_plan(first, column, bit):
    return (
        (first, 0, column, None, bit),
        (first + 1, 1, column, None, bit),
        (first + 2, 2, column, 0, bit),
        (first + 3, 2, column, 1, bit),
        (first + 4, 3, column, 0, bit),
        (first + 5, 3, column, 1, bit),
    )


def enter_body(hidden, gain_ref, cos_ref, sin_ref, ready, normed_ref, q_ref, kv_ref, w_ref):
    width = hidden.shape[1]
    key_width = kv_ref.shape[0] // 2
    mixed_width = width + key_width
    wide = width + 2 * key_width + HEAD_SIZE
    normed = (hidden * inverse_rms(hidden) * gain_ref[...]).astype(bf16)
    normed_ref[...] = normed
    cos, sin = cos_ref[...], sin_ref[...]
    ready()
    mixed = nn(normed, w_ref[:, :mixed_width]).T
    for head in range(QUERY_HEADS + KEY_VALUE_HEADS):
        low = head * HEAD_SIZE
        first = mixed[low : low + HALF]
        second = mixed[low + HALF : low + HEAD_SIZE]
        top = first * cos - second * sin
        bottom = second * cos + first * sin
        if head < QUERY_HEADS:
            q_ref[low : low + HALF, :] = (top * score_scale).astype(bf16)
            q_ref[low + HALF : low + HEAD_SIZE, :] = (bottom * score_scale).astype(bf16)
        else:
            low = low - width
            kv_ref[low : low + HALF, :] = top.astype(bf16)
            kv_ref[low + HALF : low + HEAD_SIZE, :] = bottom.astype(bf16)
    values = nn(normed, w_ref[:, mixed_width:wide]).T
    kv_ref[key_width:, :] = values[:key_width].astype(bf16)


def enter_first_kernel(plan, count, index_ref, h_ref, gain_ref, cos_ref, sin_ref, *refs):
    sources = refs[:count]
    hidden_ref, normed_ref, q_ref, kv_ref, w_hbm, w_ref, sems, out_sem = refs[count:]
    copies = piece_copies(plan, index_ref, sources, w_ref, sems)
    for copy in copies:
        copy.start()
    hidden = h_ref[...].astype(f32).T
    hidden_ref[...] = hidden
    out = pltpu.make_async_copy(w_ref, w_hbm, out_sem)

    def ready():
        for copy in copies:
            copy.wait()
        out.start()

    enter_body(hidden, gain_ref, cos_ref, sin_ref, ready, normed_ref, q_ref, kv_ref, w_ref)
    out.wait()


def enter_first(index, hidden_t, gain, cos, sin, plan, sources):
    width, rows = hidden_t.shape
    key_width = KEY_VALUE_HEADS * HEAD_SIZE
    columns = 2 * (width + key_width)
    return pl.pallas_call(
        functools.partial(enter_first_kernel, plan, len(sources)),
        out_shape=(
            shape((rows, width), f32),
            shape((rows, width), bf16),
            shape((width, rows), bf16),
            shape((2 * key_width, rows), bf16),
            shape((width, columns), bf16),
        ),
        in_specs=[in_smem()] + [in_vmem()] * 4 + [anywhere()] * len(sources),
        out_specs=(in_vmem(),) * 4 + (anywhere(),),
        scratch_shapes=[
            pltpu.VMEM((width, columns), bf16),
            pltpu.SemaphoreType.DMA((len(plan),)),
            pltpu.SemaphoreType.DMA,
        ],
        compiler_params=params(),
        cost_estimate=cost(4 * rows * width * width, width * columns * 4),
        name="enter_first",
    )(index, hidden_t, gain, cos, sin, *sources)


def enter_kernel(h_ref, gain_ref, cos_ref, sin_ref, w_hbm, normed_ref, q_ref, kv_ref, w_ref, sem):
    load = pltpu.make_async_copy(w_hbm.at[:, pl.ds(0, w_ref.shape[1])], w_ref, sem)
    load.start()
    enter_body(
        h_ref[...], gain_ref, cos_ref, sin_ref, load.wait, normed_ref, q_ref, kv_ref, w_ref
    )


def enter(hidden, gain, cos, sin, weights_a):
    rows, width = hidden.shape
    key_width = KEY_VALUE_HEADS * HEAD_SIZE
    wide = width + 2 * key_width + HEAD_SIZE
    return pl.pallas_call(
        enter_kernel,
        out_shape=(
            shape((rows, width), bf16),
            shape((width, rows), bf16),
            shape((2 * key_width, rows), bf16),
        ),
        in_specs=[in_vmem()] * 4 + [anywhere()],
        out_specs=(in_vmem(),) * 3,
        scratch_shapes=[pltpu.VMEM((width, wide), bf16), pltpu.SemaphoreType.DMA],
        compiler_params=params(),
        cost_estimate=cost(2 * rows * width * wide, width * wide * 2 + rows * width * 10),
        name="enter",
    )(hidden, gain, cos, sin, weights_a)


def stacked_heads(ref, group):
    parts = []
    for j in range(SHARING):
        low = (group * SHARING + j) * HEAD_SIZE
        parts.append(ref[low : low + HEAD_SIZE, :])
    return jnp.concatenate(parts, axis=1)


def key_block(ref, group):
    return ref[group * HEAD_SIZE : (group + 1) * HEAD_SIZE, :]


def value_block(ref, group):
    key_width = KEY_VALUE_HEADS * HEAD_SIZE
    return ref[key_width + group * HEAD_SIZE : key_width + (group + 1) * HEAD_SIZE, :]


def causal(rows):
    keys = lax.broadcasted_iota(jnp.int32, (rows, SHARING * rows), 0)
    queries = lax.broadcasted_iota(jnp.int32, (rows, SHARING * rows), 1) % rows
    return keys <= queries


def forward_kernel(plans, counts, *refs):
    (visible_ref, index_ref, h_ref, q_ref, kv0_ref, kv1_ref, kv2_ref, kv3_ref, gain_ref, a_hbm) = refs[:10]
    gu_sources = refs[10 : 10 + counts[0]]
    dn_sources = refs[10 + counts[0] : 10 + counts[0] + counts[1]]
    refs = refs[10 + counts[0] + counts[1] :]
    (out_ref, att_ref, att_t_ref, lse_ref, middle_ref, nf_ref, gating_ref, upward_ref, inner_ref) = refs[:9]
    refs = refs[9:]
    first = plans is not None
    if first:
        gu_hbm, dn_hbm = refs[:2]
        refs = refs[2:]
    (wo_ref, gu_ref, dn_ref, acc_ref, m_ref, l_ref, wo_sem, gu_sems, dn_sems) = refs
    rows, width = h_ref.shape
    ffn = inner_ref.shape[1]
    wo_wide = wo_ref.shape[1]
    wo_load = pltpu.make_async_copy(
        a_hbm.at[:, pl.ds(a_hbm.shape[1] - wo_wide, wo_wide)], wo_ref, wo_sem
    )
    if first:
        gu_loads = piece_copies(plans[0], index_ref, gu_sources, gu_ref, gu_sems)
        dn_loads = piece_copies(plans[1], index_ref, dn_sources, dn_ref, dn_sems)
    else:
        gu_loads = [pltpu.make_async_copy(gu_sources[0], gu_ref, gu_sems.at[0])]
        dn_loads = [pltpu.make_async_copy(dn_sources[0], dn_ref, dn_sems.at[0])]
    for load in [wo_load] + gu_loads + dn_loads:
        load.start()

    allowed = causal(rows)
    for group in range(KEY_VALUE_HEADS):
        scores = nn(key_block(kv0_ref, group).T, stacked_heads(q_ref, group))
        scores = jnp.where(allowed, scores, masked)
        peak = jnp.max(scores, axis=0, keepdims=True)
        raised = jnp.exp(scores - peak)
        m_ref[group : group + 1, :] = peak
        l_ref[group : group + 1, :] = jnp.sum(raised, axis=0, keepdims=True)
        acc_ref[group] = nn(value_block(kv0_ref, group), raised.astype(bf16))
    for member, kv_ref in ((1, kv1_ref), (2, kv2_ref), (3, kv3_ref)):

        @pl.when(visible_ref[member] == 1)
        def _(kv_ref=kv_ref):
            for group in range(KEY_VALUE_HEADS):
                scores = nn(key_block(kv_ref, group).T, stacked_heads(q_ref, group))
                old = m_ref[group : group + 1, :]
                peak = jnp.maximum(old, jnp.max(scores, axis=0, keepdims=True))
                raised = jnp.exp(scores - peak)
                fade = jnp.exp(old - peak)
                m_ref[group : group + 1, :] = peak
                l_ref[group : group + 1, :] = l_ref[group : group + 1, :] * fade + jnp.sum(
                    raised, axis=0, keepdims=True
                )
                acc_ref[group] = acc_ref[group] * fade + nn(
                    value_block(kv_ref, group), raised.astype(bf16)
                )

    total = l_ref[...]
    lse_ref[...] = m_ref[...] + jnp.log(total)
    for group in range(KEY_VALUE_HEADS):
        mean = acc_ref[group] / total[group : group + 1, :]
        for j in range(SHARING):
            low = (group * SHARING + j) * HEAD_SIZE
            att_t_ref[low : low + HEAD_SIZE, :] = mean[:, j * rows : (j + 1) * rows].astype(bf16)
    attended = att_t_ref[...].T
    att_ref[...] = attended
    wo_load.wait()
    middle = h_ref[...] + nn(attended, wo_ref[...])[:, wo_wide - width :]
    middle_ref[...] = middle
    normed = (middle * inverse_rms(middle) * gain_ref[...]).astype(bf16)
    nf_ref[...] = normed
    for load in gu_loads:
        load.wait()
    if first:
        gu_out = pltpu.make_async_copy(gu_ref, gu_hbm, gu_sems.at[0])
        gu_out.start()
    step = 512
    for low in range(0, ffn, step):
        gating = nn(normed, gu_ref[:, low : low + step])
        upward = nn(normed, gu_ref[:, ffn + low : ffn + low + step])
        gating_ref[:, low : low + step] = gating.astype(bf16)
        upward_ref[:, low : low + step] = upward.astype(bf16)
        inner_ref[:, low : low + step] = (gating * jax.nn.sigmoid(gating) * upward).astype(bf16)
    for load in dn_loads:
        load.wait()
    if first:
        dn_out = pltpu.make_async_copy(dn_ref, dn_hbm, dn_sems.at[0])
        dn_out.start()
    finished = middle + nt(inner_ref[...], dn_ref[...])
    if first:
        out_ref[...] = finished
        gu_out.wait()
        dn_out.wait()
    else:
        out_ref[...] = finished.T.astype(bf16)


def forward_block(visible, index, hidden, q, kvs, gain, weights_a, gu, dn, plans=None):
    rows, width = hidden.shape
    ffn = gu[0].shape[1] if plans is not None else gu[0].shape[1] // 2
    wo_wide = width + HEAD_SIZE
    lanes = SHARING * rows
    counts = (len(gu), len(dn))
    first = plans is not None
    whole = (shape((width, 2 * ffn), bf16), shape((width, ffn), bf16))
    return pl.pallas_call(
        functools.partial(forward_kernel, plans, counts),
        out_shape=(
            shape((rows, width), f32) if first else shape((width, rows), bf16),
            shape((rows, width), bf16),
            shape((width, rows), bf16),
            shape((KEY_VALUE_HEADS, lanes), f32),
            shape((rows, width), f32),
            shape((rows, width), bf16),
            shape((rows, ffn), bf16),
            shape((rows, ffn), bf16),
            shape((rows, ffn), bf16),
        )
        + (whole if first else ()),
        in_specs=[in_smem()] * 2 + [in_vmem()] * 7 + [anywhere()] * (1 + sum(counts)),
        out_specs=(in_vmem(),) * 9 + ((anywhere(),) * 2 if first else ()),
        scratch_shapes=[
            pltpu.VMEM((width, wo_wide), bf16),
            pltpu.VMEM((width, 2 * ffn), bf16),
            pltpu.VMEM((width, ffn), bf16),
            pltpu.VMEM((KEY_VALUE_HEADS, HEAD_SIZE, lanes), f32),
            pltpu.VMEM((KEY_VALUE_HEADS, lanes), f32),
            pltpu.VMEM((KEY_VALUE_HEADS, lanes), f32),
            pltpu.SemaphoreType.DMA,
            pltpu.SemaphoreType.DMA((len(plans[0]) if first else 1,)),
            pltpu.SemaphoreType.DMA((len(plans[1]) if first else 1,)),
        ],
        compiler_params=params(),
        cost_estimate=cost(2 * rows * width * (4 * ffn), 3 * width * ffn * 2 + rows * ffn * 8),
        name="forward_first" if first else "forward_last",
    )(visible, index, hidden, q, *kvs, gain, weights_a, *gu, *dn)


def feed_back_kernel(
    g_ref,
    middle_ref,
    gating_ref,
    upward_ref,
    gain_ref,
    a_hbm,
    gu_hbm,
    dn_hbm,
    gb_ref,
    dgu_ref,
    dmid_ref,
    gm_ref,
    do_ref,
    dgain_ref,
    wo_ref,
    gu_ref,
    dn_ref,
    sum_ref,
    sems,
):
    rows, width = middle_ref.shape
    ffn = gating_ref.shape[1]
    wo_wide = wo_ref.shape[1]
    loads = [
        pltpu.make_async_copy(dn_hbm, dn_ref, sems.at[0]),
        pltpu.make_async_copy(gu_hbm, gu_ref, sems.at[1]),
        pltpu.make_async_copy(
            a_hbm.at[:, pl.ds(a_hbm.shape[1] - wo_wide, wo_wide)], wo_ref, sems.at[2]
        ),
    ]
    for load in loads:
        load.start()
    grad = g_ref[...] if g_ref.shape[0] == rows else g_ref[...].astype(f32).T
    short = grad.astype(bf16)
    gb_ref[...] = short
    loads[0].wait()
    step = 512
    for low in range(0, ffn, step):
        part = slice(low, low + step)
        behind = slice(ffn + low, ffn + low + step)
        d_inner = nn(short, dn_ref[:, part])
        gating = gating_ref[:, part].astype(f32)
        upward = upward_ref[:, part].astype(f32)
        gate = jax.nn.sigmoid(gating)
        d_gating = (d_inner * upward * (gate * (1.0 + gating * (1.0 - gate)))).astype(bf16)
        d_upward = (d_inner * (gating * gate)).astype(bf16)
        dgu_ref[:, part] = d_gating
        dgu_ref[:, behind] = d_upward
        if low == 0:
            loads[1].wait()
            sum_ref[...] = nt(d_gating, gu_ref[:, part]) + nt(d_upward, gu_ref[:, behind])
        else:
            sum_ref[...] += nt(d_gating, gu_ref[:, part]) + nt(d_upward, gu_ref[:, behind])
    d_normed = sum_ref[...]
    middle = middle_ref[...]
    factor = inverse_rms(middle)
    unit = middle * factor
    dgain_ref[...] = jnp.sum(d_normed * unit, axis=0, keepdims=True)
    scaled = d_normed * gain_ref[...]
    d_middle = grad + factor * (scaled - unit * jnp.mean(scaled * unit, axis=-1, keepdims=True))
    dmid_ref[...] = d_middle
    padded = jnp.concatenate(
        [jnp.zeros((rows, wo_wide - width), f32), d_middle], axis=1
    ).astype(bf16)
    gm_ref[...] = padded
    loads[2].wait()
    do_ref[...] = nt(padded, wo_ref[...]).T.astype(bf16)


def feed_back(grad, middle, gating, upward, gain, weights):
    rows, width = middle.shape
    weights_a, weights_gu, weights_dn = weights
    ffn = weights_dn.shape[1]
    wo_wide = width + HEAD_SIZE
    return pl.pallas_call(
        feed_back_kernel,
        out_shape=(
            shape((rows, width), bf16),
            shape((rows, 2 * ffn), bf16),
            shape((rows, width), f32),
            shape((rows, wo_wide), bf16),
            shape((width, rows), bf16),
            shape((1, width), f32),
        ),
        in_specs=[in_vmem()] * 5 + [anywhere()] * 3,
        out_specs=(in_vmem(),) * 6,
        scratch_shapes=[
            pltpu.VMEM((width, wo_wide), bf16),
            pltpu.VMEM((width, 2 * ffn), bf16),
            pltpu.VMEM((width, ffn), bf16),
            pltpu.VMEM((rows, width), f32),
            pltpu.SemaphoreType.DMA((3,)),
        ],
        compiler_params=params(),
        cost_estimate=cost(2 * rows * width * (4 * ffn), 3 * width * ffn * 2 + rows * ffn * 8),
        name="feed_back",
    )(grad, middle, gating, upward, gain, weights_a, weights_gu, weights_dn)


def attend_back_kernel(
    visible_ref,
    q_ref,
    do_ref,
    att_ref,
    lse_ref,
    cos_ref,
    sin_ref,
    kv0_ref,
    kv1_ref,
    kv2_ref,
    kv3_ref,
    dq_ref,
    dkv0_ref,
    dkv1_ref,
    dkv2_ref,
    dkv3_ref,
    acc_ref,
    row_ref,
):
    rows = q_ref.shape[1]
    key_width = KEY_VALUE_HEADS * HEAD_SIZE
    allowed = causal(rows)
    for group in range(KEY_VALUE_HEADS):
        row_ref[group : group + 1, :] = jnp.sum(
            stacked_heads(do_ref, group).astype(f32) * stacked_heads(att_ref, group).astype(f32),
            axis=0,
            keepdims=True,
        )

    def one(group, kv_ref, dkv_ref, own):
        queries = stacked_heads(q_ref, group)
        d_out = stacked_heads(do_ref, group)
        keys = key_block(kv_ref, group)
        scores = nn(keys.T, queries)
        if own:
            scores = jnp.where(allowed, scores, masked)
        probs = jnp.exp(scores - lse_ref[group : group + 1, :])
        d_probs = nn(value_block(kv_ref, group).T, d_out)
        d_scores = (probs * (d_probs - row_ref[group : group + 1, :])).astype(bf16)
        dkv_ref[group * HEAD_SIZE : (group + 1) * HEAD_SIZE, :] = nt(queries, d_scores).astype(bf16)
        dkv_ref[key_width + group * HEAD_SIZE : key_width + (group + 1) * HEAD_SIZE, :] = nt(
            d_out, probs.astype(bf16)
        ).astype(bf16)
        moved = nn(keys, d_scores)
        if own:
            acc_ref[group] = moved
        else:
            acc_ref[group] += moved

    for group in range(KEY_VALUE_HEADS):
        one(group, kv0_ref, dkv0_ref, True)
    for member, kv_ref, dkv_ref in (
        (1, kv1_ref, dkv1_ref),
        (2, kv2_ref, dkv2_ref),
        (3, kv3_ref, dkv3_ref),
    ):

        @pl.when(visible_ref[member] == 1)
        def _(kv_ref=kv_ref, dkv_ref=dkv_ref):
            for group in range(KEY_VALUE_HEADS):
                one(group, kv_ref, dkv_ref, False)

        @pl.when(visible_ref[member] == 0)
        def _(dkv_ref=dkv_ref):
            dkv_ref[...] = jnp.zeros_like(dkv_ref)

    cos, sin = cos_ref[...], sin_ref[...]
    for group in range(KEY_VALUE_HEADS):
        for j in range(SHARING):
            low = (group * SHARING + j) * HEAD_SIZE
            lanes = slice(j * rows, (j + 1) * rows)
            first = acc_ref[group, :HALF, lanes] * score_scale
            second = acc_ref[group, HALF:, lanes] * score_scale
            dq_ref[low : low + HALF, :] = (first * cos + second * sin).astype(bf16)
            dq_ref[low + HALF : low + HEAD_SIZE, :] = (second * cos - first * sin).astype(bf16)


def attend_back(visible, q, d_out, att_t, lse, cos, sin, kvs):
    width, rows = q.shape
    key_rows = kvs[0].shape[0]
    lanes = SHARING * rows
    return pl.pallas_call(
        attend_back_kernel,
        out_shape=(shape((width, rows), bf16),) + (shape((key_rows, rows), bf16),) * 4,
        in_specs=[in_smem()] + [in_vmem()] * 10,
        out_specs=(in_vmem(),) * 5,
        scratch_shapes=[
            pltpu.VMEM((KEY_VALUE_HEADS, HEAD_SIZE, lanes), f32),
            pltpu.VMEM((KEY_VALUE_HEADS, lanes), f32),
        ],
        compiler_params=params(),
        cost_estimate=cost(2 * rows * width * 4 * rows * 10, 10 * width * rows * 2),
        name="attend_back",
    )(visible, q, d_out, att_t, lse, cos, sin, *kvs)


def leave_kernel(
    h_ref,
    dmid_ref,
    dq_ref,
    own_ref,
    got_ref,
    gain_ref,
    cos_ref,
    sin_ref,
    w_hbm,
    g_ref,
    dqkv_ref,
    dgain_ref,
    w_ref,
    turned_ref,
    sem,
):
    width, rows = dq_ref.shape
    key_width = own_ref.shape[0] // 2
    wide = w_ref.shape[1]
    load = pltpu.make_async_copy(w_hbm.at[:, pl.ds(0, wide)], w_ref, sem)
    load.start()
    cos, sin = cos_ref[...], sin_ref[...]
    turned_ref[:width, :] = dq_ref[...]
    summed = own_ref[...].astype(f32) + got_ref[...].astype(f32)
    for head in range(KEY_VALUE_HEADS):
        low = head * HEAD_SIZE
        first = summed[low : low + HALF]
        second = summed[low + HALF : low + HEAD_SIZE]
        base = width + low
        turned_ref[base : base + HALF, :] = (first * cos + second * sin).astype(bf16)
        turned_ref[base + HALF : base + HEAD_SIZE, :] = (second * cos - first * sin).astype(bf16)
    turned_ref[width + key_width : width + 2 * key_width, :] = summed[key_width:].astype(bf16)
    turned_ref[width + 2 * key_width :, :] = jnp.zeros((wide - width - 2 * key_width, rows), bf16)
    d_mixed = turned_ref[...].T
    dqkv_ref[...] = d_mixed
    load.wait()
    d_normed = nt(d_mixed, w_ref[...])
    hidden = h_ref[...]
    factor = inverse_rms(hidden)
    unit = hidden * factor
    dgain_ref[...] = jnp.sum(d_normed * unit, axis=0, keepdims=True)
    scaled = d_normed * gain_ref[...]
    grad = dmid_ref[...] + factor * (
        scaled - unit * jnp.mean(scaled * unit, axis=-1, keepdims=True)
    )
    g_ref[...] = grad if g_ref.dtype == f32 else grad.T.astype(bf16)


def leave(hidden, d_middle, dq, own, got, gain, cos, sin, weights_a):
    rows, width = hidden.shape
    key_width = KEY_VALUE_HEADS * HEAD_SIZE
    wide = width + 2 * key_width + HEAD_SIZE
    return pl.pallas_call(
        leave_kernel,
        out_shape=(
            shape((rows, width), f32),
            shape((rows, wide), bf16),
            shape((1, width), f32),
        ),
        in_specs=[in_vmem()] * 8 + [anywhere()],
        out_specs=(in_vmem(),) * 3,
        scratch_shapes=[
            pltpu.VMEM((width, wide), bf16),
            pltpu.VMEM((wide, rows), bf16),
            pltpu.SemaphoreType.DMA,
        ],
        compiler_params=params(),
        cost_estimate=cost(2 * rows * width * wide, width * wide * 2 + rows * width * 14),
        name="leave",
    )(hidden, d_middle, dq, own, got, gain, cos, sin, weights_a)


def grad_parts(place_ref, right, keep_ref, send_ref, xt_ref):
    block, step = keep_ref.shape[2:]
    core, chip, quarter = place_ref[0], place_ref[1], place_ref[2]
    for part in range(4):
        columns = right(part * step, (part + 1) * step)
        for away in range(2):
            for out_ref, which in ((keep_ref, core), (send_ref, 1 - core)):
                start = pl.multiple_of((2 * (chip ^ away) + which) * block, 16)
                out_ref[away, part ^ quarter] = nn(
                    xt_ref[pl.ds(start, block), :], columns
                ).astype(bf16)


def feed_back_gate_kernel(*refs):
    (place_ref, g_ref, middle_ref, gating_ref, upward_ref, gain_ref, nf2_ref, nf_ref, dgu2_ref,
     a_hbm, gu_hbm, dn_hbm, dmid_ref, gm_ref, do_ref, dgain_ref, keep_ref, send_ref, keep2_ref,
     send2_ref, gb_ref, dgu_ref, wo_ref, gu_ref, dn_ref, sum_ref, xt_ref, sems) = refs
    feed_back_kernel(
        g_ref, middle_ref, gating_ref, upward_ref, gain_ref, a_hbm, gu_hbm, dn_hbm, gb_ref, dgu_ref,
        dmid_ref, gm_ref, do_ref, dgain_ref, wo_ref, gu_ref, dn_ref, sum_ref, sems,
    )

    rows = nf_ref.shape[0]
    ffn = gating_ref.shape[1]
    xt_ref[:, :rows] = nf2_ref[...].T
    xt_ref[:, rows:] = nf_ref[...].T
    for base, out_refs in ((0, (keep_ref, send_ref)), (ffn, (keep2_ref, send2_ref))):

        def right(low, high, base=base):
            return jnp.concatenate(
                [dgu2_ref[:, base + low : base + high], dgu_ref[:, base + low : base + high]], axis=0
            )

        grad_parts(place_ref, right, *out_refs, xt_ref)


def feed_back_gate(place, grad, middle, gating, upward, gain, nf2, nf, dgu2, weights):
    rows, width = grad.shape
    weights_a, weights_gu, weights_dn = weights
    ffn = weights_dn.shape[1]
    wo_wide = width + HEAD_SIZE
    return pl.pallas_call(
        feed_back_gate_kernel,
        out_shape=(
            shape((rows, width), f32),
            shape((rows, wo_wide), bf16),
            shape((width, rows), bf16),
            shape((1, width), f32),
        )
        + (shape((2, 4, width // 4, ffn // 4), bf16),) * 4,
        in_specs=[in_smem()] + [in_vmem()] * 8 + [anywhere()] * 3,
        out_specs=(in_vmem(),) * 8,
        scratch_shapes=[
            pltpu.VMEM((rows, width), bf16),
            pltpu.VMEM((rows, 2 * ffn), bf16),
            pltpu.VMEM((width, wo_wide), bf16),
            pltpu.VMEM((width, 2 * ffn), bf16),
            pltpu.VMEM((width, ffn), bf16),
            pltpu.VMEM((rows, width), f32),
            pltpu.VMEM((width, 2 * rows), bf16),
            pltpu.SemaphoreType.DMA((3,)),
        ],
        compiler_params=params(),
        cost_estimate=cost(2 * rows * width * (8 * ffn), 3 * width * ffn * 2 + rows * ffn * 8),
        name="feed_back_gate",
    )(place, grad, middle, gating, upward, gain, nf2, nf, dgu2, weights_a, weights_gu, weights_dn)


def leave_mixed_kernel(*refs):
    (place_ref, h_ref, dmid_ref, dq_ref, own_ref, got_ref, gain_ref, cos_ref, sin_ref, n1_ref, n2_ref,
     d1_ref, a1_ref, a2_ref, m1_ref, m2_ref, attention_gain_ref, ffn_gain_ref, ffn_gain2_ref, w_hbm,
     g_ref, keep_ref, send_ref, d2_ref, dgain_ref, w_ref, turned_ref, nt_ref, at_ref, gains_ref,
     sem) = refs
    leave_kernel(
        h_ref, dmid_ref, dq_ref, own_ref, got_ref, gain_ref, cos_ref, sin_ref, w_hbm, g_ref, d2_ref,
        dgain_ref, w_ref, turned_ref, sem,
    )
    gains = (attention_gain_ref[...] + dgain_ref[...], ffn_gain_ref[...] + ffn_gain2_ref[...])
    attention_grad_kernel(
        place_ref, n1_ref, n2_ref, d1_ref, d2_ref, a1_ref, a2_ref, m1_ref, m2_ref, gains, keep_ref,
        send_ref, nt_ref, at_ref, gains_ref,
    )


def leave_mixed(
    place, hidden, d_middle, dq, own, got, gain, cos, sin, normed, dqkv2, att, gm, gain_grads, weights_a
):
    rows, width = hidden.shape
    key_width = KEY_VALUE_HEADS * HEAD_SIZE
    wide = width + 2 * key_width + HEAD_SIZE
    block = width // 4 + GAIN_ROWS
    columns = 2 * width + 2 * key_width
    return pl.pallas_call(
        leave_mixed_kernel,
        out_shape=(shape((width, rows), bf16),)
        + (shape((2, 4, block, columns // 4), bf16),) * 2,
        in_specs=[in_smem()] + [in_vmem()] * 18 + [anywhere()],
        out_specs=(in_vmem(),) * 3,
        scratch_shapes=[
            pltpu.VMEM((rows, wide), bf16),
            pltpu.VMEM((1, width), f32),
            pltpu.VMEM((width, wide), bf16),
            pltpu.VMEM((wide, rows), bf16),
            pltpu.VMEM((width, 2 * rows), bf16),
            pltpu.VMEM((width, 2 * rows), bf16),
            pltpu.VMEM((GAIN_ROWS, columns), f32),
            pltpu.SemaphoreType.DMA,
        ],
        compiler_params=params(),
        cost_estimate=cost(6 * rows * width * wide, width * wide * 2 + rows * width * 14),
        name="leave_mixed",
    )(place, hidden, d_middle, dq, own, got, gain, cos, sin, *normed, dqkv2, *att, *gm, *gain_grads,
      weights_a)


def down_grad_kernel(place_ref, g2_ref, g_ref, inner2_ref, inner_ref, keep_ref, send_ref, gt_ref):
    rows = g2_ref.shape[0]
    height, step = keep_ref.shape[2:]
    gt_ref[:, :rows] = g2_ref[...].T
    gt_ref[:, rows:] = g_ref[...].astype(bf16).T
    core, chip, quarter = place_ref[0], place_ref[1], place_ref[2]
    for away in range(2):
        for out_ref, which in ((keep_ref, core), (send_ref, 1 - core)):
            columns = pl.ds(pl.multiple_of((2 * (chip ^ away) + which) * step, 128), step)
            right = jnp.concatenate([inner2_ref[:, columns], inner_ref[:, columns]], axis=0)
            for part in range(4):
                out_ref[away, part ^ quarter] = nn(
                    gt_ref[part * height : (part + 1) * height, :], right
                ).astype(bf16)


def down_grad_parts(place, g2, g, inner2, inner):
    rows, width = g.shape
    ffn = inner.shape[1]
    return pl.pallas_call(
        down_grad_kernel,
        out_shape=(shape((2, 4, width // 4, ffn // 4), bf16),) * 2,
        in_specs=[in_smem()] + [in_vmem()] * 4,
        out_specs=(in_vmem(),) * 2,
        scratch_shapes=[pltpu.VMEM((width, 2 * rows), bf16)],
        compiler_params=params(),
        cost_estimate=cost(4 * rows * width * ffn, width * ffn * 2),
        name="down_grad",
    )(place, g2, g, inner2, inner)


def attention_grad_kernel(
    place_ref, n1_ref, n2_ref, d1_ref, d2_ref, a1_ref, a2_ref, m1_ref, m2_ref, gains,
    keep_ref, send_ref, nt_ref, at_ref, gains_ref,
):
    rows = n1_ref.shape[0]
    block = n1_ref.shape[1] // 4
    wide = d1_ref.shape[1]
    edge = wide - 128
    step = keep_ref.shape[3]
    nt_ref[:, :rows] = n1_ref[...].T
    nt_ref[:, rows:] = n2_ref[...].T
    at_ref[:, :rows] = a1_ref[...].T
    at_ref[:, rows:] = a2_ref[...].T
    half = GAIN_ROWS // 2
    gains_ref[...] = jnp.zeros_like(gains_ref)
    for i, gain in enumerate(gains):
        gains_ref[i * half : (i + 1) * half, : gain.shape[1]] = jnp.broadcast_to(
            gain, (half, gain.shape[1])
        )
    core, chip, quarter = place_ref[0], place_ref[1], place_ref[2]
    d_mixed = jnp.concatenate([d1_ref[...], d2_ref[...]], axis=0)
    d_out = jnp.concatenate([m1_ref[...], m2_ref[...]], axis=0)
    for away in range(2):
        for out_ref, which in ((keep_ref, core), (send_ref, 1 - core)):
            member = 2 * (chip ^ away) + which
            start = pl.multiple_of(member * block, 16)
            normed = nt_ref[pl.ds(start, block), :]
            attended = at_ref[pl.ds(start, block), :]
            for part in range(4):
                low, high = part * step, (part + 1) * step
                pieces = []
                if low < edge:
                    pieces.append(nn(normed, d_mixed[:, low : min(high, edge)]))
                if low <= edge < high:
                    pieces.append(nn(normed, d_mixed[:, edge:]) + nn(attended, d_out[:, :128]))
                if high > wide:
                    base = wide - 128
                    pieces.append(nn(attended, d_out[:, max(low, wide) - base : high - base]))
                piece = pieces[0] if len(pieces) == 1 else jnp.concatenate(pieces, axis=1)
                out_ref[away, part ^ quarter, :block, :] = piece.astype(bf16)
                out_ref[away, part ^ quarter, block:, :] = gains_ref[:, low:high].astype(bf16)


def finish_kernel(place_ref, p0_ref, p1_ref, p2_ref, p3_ref, out_ref):
    part = pl.program_id(0)
    for i, ref in enumerate((p0_ref, p1_ref, p2_ref, p3_ref)):

        @pl.when(part == i)
        def _(ref=ref):
            out_ref[...] = ref[...].astype(f32)


def finish(place, pieces, by_rows):
    height, step = pieces[0].shape
    whole = pl.BlockSpec((height, step), lambda i, place: (0, 0))
    if by_rows:
        dims, index = (4 * height, step), lambda i, place: (i ^ place[2], 0)
    else:
        dims, index = (height, 4 * step), lambda i, place: (0, i ^ place[2])
    return pl.pallas_call(
        finish_kernel,
        grid_spec=pltpu.PrefetchScalarGridSpec(
            num_scalar_prefetch=1,
            grid=(4,),
            in_specs=[whole] * 4,
            out_specs=pl.BlockSpec((height, step), index),
        ),
        out_shape=shape(dims, f32),
        compiler_params=params(),
        cost_estimate=cost(0, 24 * height * step),
        name="finish",
    )(place, *pieces)


def finish_mixed_kernel(
    place_ref, p0_ref, p1_ref, p2_ref, p3_ref, query_ref, key_ref, value_ref, out_ref, gain_ref,
    mixed_ref,
):
    quarter = place_ref[2]
    block, width = query_ref.shape
    key_width = key_ref.shape[0]
    step = p0_ref.shape[1]
    for i, ref in enumerate((p0_ref, p1_ref, p2_ref, p3_ref)):
        start = pl.multiple_of((quarter ^ i) * step, 128)
        mixed_ref[:, pl.ds(start, step)] = ref[...].astype(f32)
    first_end = width + key_width
    second_end = first_end + key_width
    query_ref[...] = mixed_ref[:block, :width]
    key_ref[...] = mixed_ref[:block, width:first_end].T
    value_ref[...] = mixed_ref[:block, first_end:second_end].T
    out_ref[...] = mixed_ref[:block, second_end:]
    gain_ref[...] = mixed_ref[block:, : gain_ref.shape[1]]


def finish_mixed(place, pieces, width, key_width):
    height, step = pieces[0].shape
    block = height - GAIN_ROWS
    return pl.pallas_call(
        finish_mixed_kernel,
        out_shape=(
            shape((block, width), f32),
            shape((key_width, block), f32),
            shape((key_width, block), f32),
            shape((block, width), f32),
            shape((GAIN_ROWS, width + HEAD_SIZE), f32),
        ),
        in_specs=[in_smem()] + [in_vmem()] * 4,
        out_specs=(in_vmem(),) * 5,
        scratch_shapes=[pltpu.VMEM((height, 4 * step), f32)],
        compiler_params=params(),
        cost_estimate=cost(0, 24 * height * step),
        name="finish_mixed",
    )(place, *pieces)


def flip(value, axis_name, distance):
    size = lax.axis_size(axis_name)
    return lax.ppermute(value, axis_name, [(i, i ^ distance) for i in range(size)])


def pick(condition, when_true, when_false):
    return jnp.where(condition, when_true, when_false)


def order_by(bit, own, other):
    return (pick(bit == 1, other, own), pick(bit == 1, own, other))


def exchange_kv(block):
    beside = flip(block, "fsdp", 1)
    across = flip(block, "fsdp", 2)
    diagonal = flip(across, "fsdp", 1)
    return (block, beside, across, diagonal)


def fold_kv(pieces):
    rows = pieces[0].shape[0]
    got = flip(jnp.concatenate([pieces[1], pieces[3]], axis=0), "fsdp", 1)
    return total(pieces[0], got[:rows]), total(pieces[2], got[rows:])


def return_kv(pieces):
    own, across = fold_kv(pieces)
    return own, flip(across, "fsdp", 2)


def total(*terms):
    result = terms[0].astype(f32)
    for term in terms[1:]:
        result = result + term.astype(f32)
    return result.astype(bf16)


class Order:
    def __init__(self, *token):
        self.token = token

    def tie(self, *values):
        tied = lax.optimization_barrier(self.token + values)[len(self.token) :]
        return tied[0] if len(tied) == 1 else tied

    def done(self, value):
        self.token = (value,)
        return value

    def done_all(self, *values):
        self.token = values
        return values


class Reduction:
    def __init__(self, order, keep, send):
        self.order = order
        self.keep = keep
        self.core = flip(order.tie(send), "fsdp", 1)

    def chip(self):
        self.core = self.order.tie(self.core)
        high = total(self.keep[1, 2:], self.core[1, 2:])
        low = total(self.keep[1, :2], self.core[1, :2])
        high, low = self.order.done_all(high, low)
        self.high = flip(high, "fsdp", 2)
        self.low = flip(low, "fsdp", 2)

    def first(self, both=False):
        if both:
            self.high, self.low = self.order.tie(self.high, self.low)
        else:
            self.high = self.order.tie(self.high)
        out = total(self.keep[0, 2:], self.core[0, 2:], self.high)
        self.got = flip(self.order.done(out), "dp", 1)

    def rest(self):
        self.low = self.order.done(self.order.tie(self.low))

    def second(self):
        self.got, self.low = self.order.tie(self.got, self.low)
        self.terms = (self.keep[0, :2], self.core[0, :2], self.low, self.got)
        self.got = flip(self.order.done(total(*[term[1] for term in self.terms])), "dp", 2)

    def third(self):
        size = lax.axis_size("dp")
        own = total(*[term[0] for term in self.terms], self.order.tie(self.got))
        distance = 4
        while 2 * distance < size:
            own = total(own, flip(own, "dp", distance))
            distance *= 2
        self.own = self.order.done(own)
        self.got = flip(own, "dp", distance) if distance < size else jnp.zeros_like(own)

    def back(self):
        self.own = self.order.done(total(self.own, self.order.tie(self.got)))
        self.beside = flip(self.own, "dp", 2)
        self.pieces = [self.own, self.beside, flip(self.own, "dp", 1)]

    def back_again(self):
        self.beside = self.order.done(self.order.tie(self.beside))
        self.pieces.append(flip(self.beside, "dp", 1))

    def end(self):
        return self.order.tie(*self.pieces)


def rotation(token_positions):
    frequency = rope_base ** (-jnp.arange(HALF, dtype=f32) / HALF)
    angles = frequency[:, None] * token_positions.astype(f32)[None, :]
    return jnp.cos(angles), jnp.sin(angles)


def body(
    tokens,
    cotangent,
    sequence_ids,
    span_position,
    attention_norm,
    query_weight,
    key_matrix,
    value_matrix,
    output_weight,
    feedforward_norm,
    gate_weight,
    up_weight,
    down_weight,
):
    rows, width = tokens.shape
    key_width = key_matrix.shape[1]
    ffn = gate_weight.shape[1]
    itself = lax.axis_index("fsdp")
    outer = lax.axis_index("dp")
    quarter = 2 * (outer % 2) + (outer // 2) % 2
    place = jnp.stack([itself % 2, itself // 2, quarter]).astype(jnp.int32)

    outer = lax.axis_index("dp")
    bits = jnp.stack([outer % 2, (outer // 2) % 2, itself]).astype(jnp.int32)
    packed, *mine = pack(
        bits, query_weight, key_matrix.T, value_matrix.T, output_weight, gate_weight, up_weight
    )
    down_t = down_weight.T
    half = width // 2
    mine.append(pick(outer % 2 == 1, down_t[half:], down_t[:half]))
    gains = jnp.stack([attention_norm, feedforward_norm], axis=0)
    gains = [flip(gains, "fsdp", distance) if distance else gains for distance in range(4)]
    mine = Order(*gains).tie(*mine)
    far = [flip(piece, "fsdp", 2) for piece in mine]
    shards = (packed, gate_weight, up_weight, down_t)
    near = [flip(shard, "fsdp", 1) for shard in shards]
    sequence_ids, span_position = Order(*mine).tie(sequence_ids, span_position)
    places = jnp.arange(rows, dtype=jnp.int32) + span_position[itself] * rows
    cos, sin = rotation(places)
    others = itself ^ jnp.arange(4)
    visible = (
        (sequence_ids[others] == sequence_ids[itself])
        & (span_position[others] <= span_position[itself])
    ).astype(jnp.int32)

    beside = order_by(itself % 2, gains[0], gains[1])
    away = order_by(itself % 2, gains[2], gains[3])
    chip = itself // 2 == 1
    gains = jnp.concatenate(
        [pick(chip, a, n) for a, n in zip(away, beside)]
        + [pick(chip, n, a) for a, n in zip(away, beside)],
        axis=1,
    ).astype(f32)
    attention_gain, ffn_gain = gains[:1], gains[1:]
    order = Order(cos, sin, visible, attention_gain, ffn_gain)
    share = ((1, 0), (1, 0), (2, 1), (1, 0))

    def shared(i):
        got = order.done(order.tie(far[i]))
        return got, flip(got, "dp", share[i][0])

    def gathered(i, got, other):
        return [shards[i], near[i], got, other, flip(got, "fsdp", 1), flip(other, "fsdp", 1)]

    shared_a = shared(0)
    order.done_all(*order.tie(*shared_a))
    shared_gate = shared(1)
    sources_a = gathered(0, *shared_a)
    order.done_all(*order.tie(*near), *sources_a)
    tokens_t = order.tie(tokens.T)
    hidden, normed, q, kv, weights_a = enter_first(
        bits, tokens_t, attention_gain, cos, sin, shared_plan(0, 0, 0), tuple(sources_a)
    )
    order.done(kv)
    shared_up = shared(2)
    shared_gate = order.done_all(*order.tie(*shared_gate))
    kvs = exchange_kv(kv)
    shared_down = shared(3)
    order.done_all(*order.tie(*shared_up))
    sources_gu = gathered(1, *shared_gate) + gathered(2, *shared_up)
    sources_dn = gathered(3, *order.tie(*shared_down))
    plan_gu = shared_plan(0, 0, 0) + shared_plan(6, ffn, 1)
    plan_dn = shared_plan(0, None, 0)
    finished, att, att_t, lse, middle, nf, gating, upward, inner, weights_gu, weights_dn = forward_block(
        visible, bits, hidden, q, kvs, ffn_gain, weights_a, tuple(sources_gu), tuple(sources_dn),
        (plan_gu, plan_dn),
    )
    weights = (weights_a, weights_gu, weights_dn)
    saved = [(hidden, normed, q, kvs, att, att_t, lse, middle, nf, gating, upward, inner)]
    hidden = finished
    normed, q, kv = enter(hidden, attention_gain, cos, sin, weights_a)
    kvs = exchange_kv(kv)
    activations, att, att_t, lse, middle, nf, gating, upward, inner = forward_block(
        visible, bits, hidden, q, kvs, ffn_gain, weights_a, (weights_gu,), (weights_dn,)
    )
    saved.append((hidden, normed, q, kvs, att, att_t, lse, middle, nf, gating, upward, inner))

    hidden, normed2, q, kvs, att2, att_t, lse, middle, nf2, gating, upward, inner2 = saved[1]
    gb2, dgu2, d_middle, gm2, d_out, ffn_gain_grad2 = feed_back(
        cotangent.T, middle, gating, upward, ffn_gain, weights
    )
    dq, *dkvs = attend_back(visible, q, d_out, att_t, lse, cos, sin, kvs)
    own, got = return_kv(dkvs)
    grad, dqkv2, attention_gain_grad2 = leave(
        hidden, d_middle, dq, own, got, attention_gain, cos, sin, weights_a
    )

    hidden, normed, q, kvs, att, att_t, lse, middle, nf, gating, upward, inner = saved[0]
    order = Order(grad)
    down = Reduction(order, *down_grad_parts(place, gb2, grad, inner2, inner))
    down.chip()
    d_middle, gm, d_out, ffn_gain_grad, *rest = feed_back_gate(
        place, order.tie(grad), middle, gating, upward, ffn_gain, nf2, nf, dgu2, weights
    )
    order.done(d_middle)
    down.first(both=True)
    gate = Reduction(order, *rest[:2])
    gate.chip()
    up = Reduction(order, *rest[2:])
    dq, *dkvs = attend_back(visible, order.tie(q), d_out, att_t, lse, cos, sin, kvs)
    order.done(dq)
    gate.first()
    down.second()
    own, across = fold_kv(order.tie(*dkvs))
    order.done(across)
    gate.rest()
    across = order.tie(across)
    got = flip(across, "fsdp", 2)
    order.done(across)
    up.chip()
    d_middle, got = order.tie(d_middle, got)
    grad, *mixed = leave_mixed(
        place,
        hidden,
        d_middle,
        dq,
        own,
        got,
        attention_gain,
        cos,
        sin,
        (normed2, normed),
        dqkv2,
        (att2, att),
        (gm2, gm),
        (attention_gain_grad2, ffn_gain_grad2, ffn_gain_grad),
        weights_a,
    )
    order.done(grad)
    up.first()
    mixed = Reduction(order, *mixed)
    gate.second()
    down.third()
    mixed.chip()
    up.second()
    gate.third()
    down.back()
    mixed.first()
    down.back_again()
    gate.back()
    up.third()
    gate.back_again()
    down_grad = order.done(finish(place, down.end(), True))
    up.back()
    mixed.second()
    up.back_again()
    gate_grad = order.done(finish(place, gate.end(), False))
    mixed.third()
    up_grad = order.done(finish(place, up.end(), False))
    mixed.back()
    mixed.back_again()
    query_grad, key_grad, value_grad, output_grad, gain_grads = finish_mixed(
        place, mixed.end(), width, key_width
    )
    shard_rows = attention_norm.shape[0]
    gain_grads = lax.dynamic_slice_in_dim(gain_grads, itself * shard_rows, shard_rows, axis=1)
    return (
        activations.T,
        grad.T,
        gain_grads[0],
        query_grad,
        key_grad.T,
        value_grad.T,
        output_grad,
        gain_grads[GAIN_ROWS // 2],
        gate_grad,
        up_grad,
        down_grad.T,
    )


def solution(mesh):
    return jax.shard_map(
        body,
        mesh=mesh,
        in_specs=(
            P(("dp", "fsdp"), None),
            P(("dp", "fsdp"), None),
            P("dp"),
            P("dp"),
            P("fsdp"),
            P("fsdp", None),
            P("fsdp", None),
            P("fsdp", None),
            P("fsdp", None),
            P("fsdp"),
            P("fsdp", None),
            P("fsdp", None),
            P("fsdp", None),
        ),
        out_specs=(
            P(("dp", "fsdp"), None),
            P(("dp", "fsdp"), None),
            P("fsdp"),
            P("fsdp", None),
            P("fsdp", None),
            P("fsdp", None),
            P("fsdp", None),
            P("fsdp"),
            P("fsdp", None),
            P("fsdp", None),
            P("fsdp", None),
        ),
        check_vma=False,
    )
```

```python
import functools

import jax
import jax.numpy as jnp
from jax import lax
from jax.experimental import pallas as pl
from jax.experimental.pallas import tpu as pltpu
from jax.sharding import PartitionSpec as P

QUERY_HEADS = 15
KEY_VALUE_HEADS = 5
HEAD_SIZE = 64
SHARING = QUERY_HEADS // KEY_VALUE_HEADS
HALF = HEAD_SIZE // 2

epsilon = 1e-05
rope_base = 10000.0
masked = -1e30
score_scale = HEAD_SIZE ** (-0.5)

bf16 = jnp.bfloat16
f32 = jnp.float32
GAIN_ROWS = 16
FFN_MEBIBYTES = 30


def nn(left, right):
    return jnp.dot(left, right, preferred_element_type=f32)


def nt(left, right):
    return lax.dot_general(left, right, (((1,), (1,)), ((), ())), preferred_element_type=f32)


def in_vmem():
    return pl.BlockSpec(memory_space=pltpu.VMEM)


def in_smem():
    return pl.BlockSpec(memory_space=pltpu.SMEM)


def anywhere():
    return pl.BlockSpec(memory_space=pl.ANY)


def params(mebibytes=20):
    return pltpu.CompilerParams(vmem_limit_bytes=mebibytes * 1024 * 1024)


def shape(dims, dtype):
    return jax.ShapeDtypeStruct(dims, dtype)


def kept(array):
    return pltpu.with_memory_space_constraint(array, pltpu.VMEM)


def in_hbm(array):
    return pltpu.with_memory_space_constraint(array, pltpu.HBM)


def cost(flops, bytes_accessed):
    return pl.CostEstimate(flops=int(flops), bytes_accessed=int(bytes_accessed), transcendentals=0)


def inverse_rms(hidden):
    return lax.rsqrt(jnp.mean(hidden * hidden, axis=-1, keepdims=True) + epsilon)


def pack_kernel(
    bits_ref, query_hbm, key_hbm, value_hbm, out_hbm, gate_hbm, up_hbm, packed_hbm, mine_hbm,
    mine_gate_hbm, mine_up_hbm, query_ref, key_ref, value_ref, out_ref, gate_ref, up_ref, packed_ref,
    mine_ref, sems,
):
    half = gate_ref.shape[1]
    loads = [
        pltpu.make_async_copy(source, target, sems.at[i])
        for i, (source, target) in enumerate(
            (
                (query_hbm, query_ref),
                (key_hbm, key_ref),
                (value_hbm, value_ref),
                (out_hbm, out_ref),
                (gate_hbm.at[:, pl.ds(pl.multiple_of(bits_ref[0] * half, 128), half)], gate_ref),
                (up_hbm.at[:, pl.ds(pl.multiple_of(bits_ref[1] * half, 128), half)], up_ref),
            )
        )
    ]
    for load in loads:
        load.start()
    for load in loads[:4]:
        load.wait()
    packed_ref[...] = jnp.concatenate(
        [
            query_ref[...].astype(f32),
            key_ref[...].astype(f32).T,
            value_ref[...].astype(f32).T,
            out_ref[...].astype(f32),
        ],
        axis=1,
    ).astype(bf16)
    wide = mine_ref.shape[1]
    mine_ref[...] = packed_ref[:, pl.ds(pl.multiple_of(bits_ref[0] * wide, 128), wide)]
    for load in loads[4:]:
        load.wait()
    stores = [
        pltpu.make_async_copy(source, target, sems.at[i])
        for i, (source, target) in enumerate(
            (
                (mine_ref, mine_hbm),
                (gate_ref, mine_gate_hbm),
                (up_ref, mine_up_hbm),
                (packed_ref, packed_hbm),
            )
        )
    ]
    for store in stores:
        store.start()
    for store in stores:
        store.wait()


def pack(bits, query, key_t, value_t, out, gate, up):
    rows, width = query.shape
    columns = 2 * width + 2 * key_t.shape[0]
    ffn = gate.shape[1]
    return pl.pallas_call(
        pack_kernel,
        out_shape=(
            pltpu.HBM((rows, columns), bf16),
            pltpu.HBM((rows, columns // 2), bf16),
            pltpu.HBM((rows, ffn // 2), bf16),
            pltpu.HBM((rows, ffn // 2), bf16),
        ),
        in_specs=[in_smem()] + [anywhere()] * 6,
        out_specs=(anywhere(),) * 4,
        scratch_shapes=[
            pltpu.VMEM((rows, width), bf16),
            pltpu.VMEM(key_t.shape, bf16),
            pltpu.VMEM(value_t.shape, bf16),
            pltpu.VMEM((rows, width), bf16),
            pltpu.VMEM((rows, ffn // 2), bf16),
            pltpu.VMEM((rows, ffn // 2), bf16),
            pltpu.VMEM((rows, columns), bf16),
            pltpu.VMEM((rows, columns // 2), bf16),
            pltpu.SemaphoreType.DMA((6,)),
        ],
        compiler_params=params(),
        cost_estimate=cost(0, 8 * rows * columns),
        name="pack",
    )(bits, *[in_hbm(part) for part in (query, key_t, value_t, out, gate, up)])


def piece_copies(plan, bits_ref, sources, target_ref, sems):
    me = bits_ref[2]
    copies = []
    for i, (which, member, column, part, bit) in enumerate(plan):
        source = sources[which]
        height, width = source.shape
        if column is None:
            turned = pl.ds(pl.multiple_of((me ^ member) * width, 128), width)
            if part is None:
                rows = pl.ds(0, height)
            else:
                rows = pl.ds(pl.multiple_of((bits_ref[bit] ^ part) * height, 16), height)
            target = target_ref.at[rows, turned]
        else:
            rows = pl.ds(pl.multiple_of((me ^ member) * height, 16), height)
            if part is None:
                columns = pl.ds(column, width)
            else:
                columns = pl.ds(
                    pl.multiple_of(column + (bits_ref[bit] ^ part) * width, 128), width
                )
            target = target_ref.at[rows, columns]
        copies.append(pltpu.make_async_copy(source, target, sems.at[i]))
    return copies


def shared_plan(first, column, bit):
    return (
        (first, 0, column, None, bit),
        (first + 1, 1, column, None, bit),
        (first + 2, 2, column, 0, bit),
        (first + 3, 2, column, 1, bit),
        (first + 4, 3, column, 0, bit),
        (first + 5, 3, column, 1, bit),
    )


def enter_body(hidden, gain_ref, cos_ref, sin_ref, ready, normed_ref, q_ref, kv_ref, w_ref):
    width = hidden.shape[1]
    key_width = kv_ref.shape[0] // 2
    mixed_width = width + key_width
    wide = width + 2 * key_width + HEAD_SIZE
    normed = (hidden * inverse_rms(hidden) * gain_ref[...]).astype(bf16)
    normed_ref[...] = normed
    cos, sin = cos_ref[...], sin_ref[...]
    ready()
    mixed = nn(normed, w_ref[:, :mixed_width]).T
    for head in range(QUERY_HEADS + KEY_VALUE_HEADS):
        low = head * HEAD_SIZE
        first = mixed[low : low + HALF]
        second = mixed[low + HALF : low + HEAD_SIZE]
        top = first * cos - second * sin
        bottom = second * cos + first * sin
        if head < QUERY_HEADS:
            q_ref[low : low + HALF, :] = (top * score_scale).astype(bf16)
            q_ref[low + HALF : low + HEAD_SIZE, :] = (bottom * score_scale).astype(bf16)
        else:
            low = low - width
            kv_ref[low : low + HALF, :] = top.astype(bf16)
            kv_ref[low + HALF : low + HEAD_SIZE, :] = bottom.astype(bf16)
    values = nn(normed, w_ref[:, mixed_width:wide]).T
    kv_ref[key_width:, :] = values[:key_width].astype(bf16)


def enter_first_kernel(plan, count, index_ref, h_ref, gain_ref, cos_ref, sin_ref, *refs):
    sources = refs[:count]
    hidden_ref, normed_ref, q_ref, kv_ref, w_ref, sems = refs[count:]
    copies = piece_copies(plan, index_ref, sources, w_ref, sems)
    for copy in copies:
        copy.start()
    hidden = h_ref[...].astype(f32).T
    hidden_ref[...] = hidden

    def ready():
        for copy in copies:
            copy.wait()

    enter_body(hidden, gain_ref, cos_ref, sin_ref, ready, normed_ref, q_ref, kv_ref, w_ref)


def enter_first(index, hidden_t, gain, cos, sin, plan, sources):
    width, rows = hidden_t.shape
    key_width = KEY_VALUE_HEADS * HEAD_SIZE
    columns = 2 * (width + key_width)
    return pl.pallas_call(
        functools.partial(enter_first_kernel, plan, len(sources)),
        out_shape=(
            shape((rows, width), f32),
            shape((rows, width), bf16),
            shape((width, rows), bf16),
            shape((2 * key_width, rows), bf16),
            pltpu.VMEM((width, columns), bf16),
        ),
        in_specs=[in_smem()] + [in_vmem()] * 4 + [anywhere()] * len(sources),
        out_specs=(in_vmem(),) * 5,
        scratch_shapes=[pltpu.SemaphoreType.DMA((len(plan),))],
        compiler_params=params(),
        cost_estimate=cost(4 * rows * width * width, width * columns * 4),
        name="enter_first",
    )(index, hidden_t, gain, cos, sin, *sources)


def enter_kernel(h_ref, gain_ref, cos_ref, sin_ref, w_ref, normed_ref, q_ref, kv_ref):
    enter_body(
        h_ref[...], gain_ref, cos_ref, sin_ref, lambda: None, normed_ref, q_ref, kv_ref, w_ref
    )


def enter(hidden, gain, cos, sin, weights_a):
    rows, width = hidden.shape
    key_width = KEY_VALUE_HEADS * HEAD_SIZE
    wide = width + 2 * key_width + HEAD_SIZE
    return pl.pallas_call(
        enter_kernel,
        out_shape=(
            shape((rows, width), bf16),
            shape((width, rows), bf16),
            shape((2 * key_width, rows), bf16),
        ),
        in_specs=[in_vmem()] * 5,
        out_specs=(in_vmem(),) * 3,
        compiler_params=params(),
        cost_estimate=cost(2 * rows * width * wide, width * wide * 2 + rows * width * 10),
        name="enter",
    )(hidden, gain, cos, sin, kept(weights_a))


def out_weight(a_ref):
    return a_ref[:, a_ref.shape[1] - a_ref.shape[0] - HEAD_SIZE :]


def stacked_heads(ref, group):
    parts = []
    for j in range(SHARING):
        low = (group * SHARING + j) * HEAD_SIZE
        parts.append(ref[low : low + HEAD_SIZE, :])
    return jnp.concatenate(parts, axis=1)


def key_block(ref, group):
    return ref[group * HEAD_SIZE : (group + 1) * HEAD_SIZE, :]


def value_block(ref, group):
    key_width = KEY_VALUE_HEADS * HEAD_SIZE
    return ref[key_width + group * HEAD_SIZE : key_width + (group + 1) * HEAD_SIZE, :]


def causal(rows):
    keys = lax.broadcasted_iota(jnp.int32, (rows, SHARING * rows), 0)
    queries = lax.broadcasted_iota(jnp.int32, (rows, SHARING * rows), 1) % rows
    return keys <= queries


def whole_copies(source_ref, target_ref, sems):
    parts = 4
    height = source_ref.shape[0] // parts
    return [
        pltpu.make_async_copy(
            source_ref.at[pl.ds(i * height, height), :],
            target_ref.at[pl.ds(i * height, height), :],
            sems.at[i],
        )
        for i in range(parts)
    ]


def forward_kernel(plans, counts, *refs):
    (visible_ref, bits_ref, h_ref, q_ref, kv0_ref, kv1_ref, kv2_ref, kv3_ref, gain_ref, a_ref) = refs[:10]
    gu_sources = refs[10 : 10 + counts[0]]
    dn_sources = refs[10 + counts[0] : 10 + counts[0] + counts[1]]
    refs = refs[10 + counts[0] + counts[1] :]
    (out_ref, att_ref, att_t_ref, lse_ref, middle_ref, nf_ref, gating_ref, upward_ref, inner_ref) = refs[:9]
    refs = refs[9:]
    gu_ref, gu_sems, dn_sems = refs[-3:]
    if plans is not None:
        gu_hbm, dn_ref = refs[:2]
        refs = refs[2:]
        gu_loads = piece_copies(plans[0], bits_ref, gu_sources, gu_ref, gu_sems)
        dn_loads = piece_copies(plans[1], bits_ref, dn_sources, dn_ref, dn_sems)
    else:
        (dn_ref,) = dn_sources
        gu_loads, dn_loads = whole_copies(gu_sources[0], gu_ref, gu_sems), []
    acc_ref, m_ref, l_ref = refs[:3]
    rows, width = h_ref.shape
    ffn = inner_ref.shape[1]
    for load in gu_loads + dn_loads:
        load.start()

    allowed = causal(rows)
    for group in range(KEY_VALUE_HEADS):
        scores = nn(key_block(kv0_ref, group).T, stacked_heads(q_ref, group))
        scores = jnp.where(allowed, scores, masked)
        peak = jnp.max(scores, axis=0, keepdims=True)
        raised = jnp.exp(scores - peak)
        m_ref[group : group + 1, :] = peak
        l_ref[group : group + 1, :] = jnp.sum(raised, axis=0, keepdims=True)
        acc_ref[group] = nn(value_block(kv0_ref, group), raised.astype(bf16))
    for member, kv_ref in ((1, kv1_ref), (2, kv2_ref), (3, kv3_ref)):

        @pl.when(visible_ref[member] == 1)
        def _(kv_ref=kv_ref):
            for group in range(KEY_VALUE_HEADS):
                scores = nn(key_block(kv_ref, group).T, stacked_heads(q_ref, group))
                old = m_ref[group : group + 1, :]
                peak = jnp.maximum(old, jnp.max(scores, axis=0, keepdims=True))
                raised = jnp.exp(scores - peak)
                fade = jnp.exp(old - peak)
                m_ref[group : group + 1, :] = peak
                l_ref[group : group + 1, :] = l_ref[group : group + 1, :] * fade + jnp.sum(
                    raised, axis=0, keepdims=True
                )
                acc_ref[group] = acc_ref[group] * fade + nn(
                    value_block(kv_ref, group), raised.astype(bf16)
                )

    total = l_ref[...]
    lse_ref[...] = m_ref[...] + jnp.log(total)
    for group in range(KEY_VALUE_HEADS):
        mean = acc_ref[group] / total[group : group + 1, :]
        for j in range(SHARING):
            low = (group * SHARING + j) * HEAD_SIZE
            att_t_ref[low : low + HEAD_SIZE, :] = mean[:, j * rows : (j + 1) * rows].astype(bf16)
    attended = att_t_ref[...].T
    att_ref[...] = attended
    middle = h_ref[...] + nn(attended, out_weight(a_ref))[:, HEAD_SIZE:]
    middle_ref[...] = middle
    normed = (middle * inverse_rms(middle) * gain_ref[...]).astype(bf16)
    nf_ref[...] = normed
    for load in gu_loads:
        load.wait()
    gu_stores = whole_copies(gu_ref, gu_hbm, gu_sems) if plans is not None else []
    for store in gu_stores:
        store.start()
    step = 512
    for low in range(0, ffn, step):
        gating = nn(normed, gu_ref[:, low : low + step])
        upward = nn(normed, gu_ref[:, ffn + low : ffn + low + step])
        gating_ref[:, low : low + step] = gating.astype(bf16)
        upward_ref[:, low : low + step] = upward.astype(bf16)
        inner_ref[:, low : low + step] = (gating * jax.nn.sigmoid(gating) * upward).astype(bf16)
    for load in dn_loads:
        load.wait()
    finished = middle + nt(inner_ref[...], dn_ref[...])
    out_ref[...] = finished if plans is not None else finished.T.astype(bf16)
    for store in gu_stores:
        store.wait()


def forward_block(visible, index, hidden, q, kvs, gain, weights_a, gu, dn, plans=None):
    rows, width = hidden.shape
    ffn = gu[0].shape[1] if plans is not None else gu[0].shape[1] // 2
    lanes = SHARING * rows
    counts = (len(gu), len(dn))
    first = plans is not None
    whole = (pltpu.HBM((width, 2 * ffn), bf16), pltpu.VMEM((width, ffn), bf16))
    return pl.pallas_call(
        functools.partial(forward_kernel, plans, counts),
        out_shape=(
            shape((rows, width), f32) if first else shape((width, rows), bf16),
            shape((rows, width), bf16),
            shape((width, rows), bf16),
            shape((KEY_VALUE_HEADS, lanes), f32),
            shape((rows, width), f32),
            shape((rows, width), bf16),
            shape((rows, ffn), bf16),
            shape((rows, ffn), bf16),
            shape((rows, ffn), bf16),
        )
        + (whole if first else ()),
        in_specs=[in_smem()] * 2
        + [in_vmem()] * 8
        + [anywhere()] * counts[0]
        + [anywhere() if first else in_vmem()] * counts[1],
        out_specs=(in_vmem(),) * 9 + ((anywhere(), in_vmem()) if first else ()),
        scratch_shapes=[
            pltpu.VMEM((KEY_VALUE_HEADS, HEAD_SIZE, lanes), f32),
            pltpu.VMEM((KEY_VALUE_HEADS, lanes), f32),
            pltpu.VMEM((KEY_VALUE_HEADS, lanes), f32),
            pltpu.VMEM((width, 2 * ffn), bf16),
            pltpu.SemaphoreType.DMA((len(plans[0]) if first else 4,)),
            pltpu.SemaphoreType.DMA((len(plans[1]) if first else 1,)),
        ],
        compiler_params=params(FFN_MEBIBYTES),
        cost_estimate=cost(2 * rows * width * (4 * ffn), 3 * width * ffn * 2 + rows * ffn * 8),
        name="forward_first" if first else "forward_last",
    )(
        visible, index, hidden, q, *kvs, gain, kept(weights_a),
        *([*gu, *dn] if first else [in_hbm(gu[0]), kept(dn[0])]),
    )


def feed_back_kernel(
    g_ref,
    middle_ref,
    gating_ref,
    upward_ref,
    gain_ref,
    a_ref,
    gu_hbm,
    dn_ref,
    gb_ref,
    dgu_ref,
    dmid_ref,
    gm_ref,
    do_ref,
    dgain_ref,
    sum_ref,
    gu_ref,
    gu_sems,
):
    rows, width = middle_ref.shape
    ffn = gating_ref.shape[1]
    loads = whole_copies(gu_hbm, gu_ref, gu_sems)
    for load in loads:
        load.start()
    grad = g_ref[...] if g_ref.shape[0] == rows else g_ref[...].astype(f32).T
    short = grad.astype(bf16)
    gb_ref[...] = short
    step = 512
    for low in range(0, ffn, step):
        part = slice(low, low + step)
        behind = slice(ffn + low, ffn + low + step)
        d_inner = nn(short, dn_ref[:, part])
        gating = gating_ref[:, part].astype(f32)
        upward = upward_ref[:, part].astype(f32)
        gate = jax.nn.sigmoid(gating)
        d_gating = (d_inner * upward * (gate * (1.0 + gating * (1.0 - gate)))).astype(bf16)
        d_upward = (d_inner * (gating * gate)).astype(bf16)
        dgu_ref[:, part] = d_gating
        dgu_ref[:, behind] = d_upward
    for load in loads:
        load.wait()
    sum_ref[...] = nt(dgu_ref[...], gu_ref[...])
    d_normed = sum_ref[...]
    middle = middle_ref[...]
    factor = inverse_rms(middle)
    unit = middle * factor
    dgain_ref[...] = jnp.sum(d_normed * unit, axis=0, keepdims=True)
    scaled = d_normed * gain_ref[...]
    d_middle = grad + factor * (scaled - unit * jnp.mean(scaled * unit, axis=-1, keepdims=True))
    dmid_ref[...] = d_middle
    padded = jnp.concatenate(
        [jnp.zeros((rows, HEAD_SIZE), f32), d_middle], axis=1
    ).astype(bf16)
    gm_ref[...] = padded
    do_ref[...] = nt(padded, out_weight(a_ref)).T.astype(bf16)


def feed_back(grad, middle, gating, upward, gain, weights):
    rows, width = middle.shape
    weights_a, weights_gu, weights_dn = weights
    ffn = weights_dn.shape[1]
    wo_wide = width + HEAD_SIZE
    return pl.pallas_call(
        feed_back_kernel,
        out_shape=(
            shape((rows, width), bf16),
            shape((rows, 2 * ffn), bf16),
            shape((rows, width), f32),
            shape((rows, wo_wide), bf16),
            shape((width, rows), bf16),
            shape((1, width), f32),
        ),
        in_specs=[in_vmem()] * 6 + [anywhere(), in_vmem()],
        out_specs=(in_vmem(),) * 6,
        scratch_shapes=[
            pltpu.VMEM((rows, width), f32),
            pltpu.VMEM((width, 2 * ffn), bf16),
            pltpu.SemaphoreType.DMA((4,)),
        ],
        compiler_params=params(FFN_MEBIBYTES),
        cost_estimate=cost(2 * rows * width * (4 * ffn), 3 * width * ffn * 2 + rows * ffn * 8),
        name="feed_back",
    )(grad, middle, gating, upward, gain, kept(weights_a), in_hbm(weights_gu), kept(weights_dn))


def attend_back_kernel(
    visible_ref,
    q_ref,
    do_ref,
    att_ref,
    lse_ref,
    cos_ref,
    sin_ref,
    kv0_ref,
    kv1_ref,
    kv2_ref,
    kv3_ref,
    dq_ref,
    dkv0_ref,
    dkv1_ref,
    dkv2_ref,
    dkv3_ref,
    acc_ref,
    row_ref,
):
    rows = q_ref.shape[1]
    key_width = KEY_VALUE_HEADS * HEAD_SIZE
    allowed = causal(rows)
    for group in range(KEY_VALUE_HEADS):
        row_ref[group : group + 1, :] = jnp.sum(
            stacked_heads(do_ref, group).astype(f32) * stacked_heads(att_ref, group).astype(f32),
            axis=0,
            keepdims=True,
        )

    def one(group, kv_ref, dkv_ref, own):
        queries = stacked_heads(q_ref, group)
        d_out = stacked_heads(do_ref, group)
        keys = key_block(kv_ref, group)
        scores = nn(keys.T, queries)
        if own:
            scores = jnp.where(allowed, scores, masked)
        probs = jnp.exp(scores - lse_ref[group : group + 1, :])
        d_probs = nn(value_block(kv_ref, group).T, d_out)
        d_scores = (probs * (d_probs - row_ref[group : group + 1, :])).astype(bf16)
        dkv_ref[group * HEAD_SIZE : (group + 1) * HEAD_SIZE, :] = nt(queries, d_scores).astype(bf16)
        dkv_ref[key_width + group * HEAD_SIZE : key_width + (group + 1) * HEAD_SIZE, :] = nt(
            d_out, probs.astype(bf16)
        ).astype(bf16)
        moved = nn(keys, d_scores)
        if own:
            acc_ref[group] = moved
        else:
            acc_ref[group] += moved

    for group in range(KEY_VALUE_HEADS):
        one(group, kv0_ref, dkv0_ref, True)
    for member, kv_ref, dkv_ref in (
        (1, kv1_ref, dkv1_ref),
        (2, kv2_ref, dkv2_ref),
        (3, kv3_ref, dkv3_ref),
    ):

        @pl.when(visible_ref[member] == 1)
        def _(kv_ref=kv_ref, dkv_ref=dkv_ref):
            for group in range(KEY_VALUE_HEADS):
                one(group, kv_ref, dkv_ref, False)

        @pl.when(visible_ref[member] == 0)
        def _(dkv_ref=dkv_ref):
            dkv_ref[...] = jnp.zeros_like(dkv_ref)

    cos, sin = cos_ref[...], sin_ref[...]
    for group in range(KEY_VALUE_HEADS):
        for j in range(SHARING):
            low = (group * SHARING + j) * HEAD_SIZE
            lanes = slice(j * rows, (j + 1) * rows)
            first = acc_ref[group, :HALF, lanes] * score_scale
            second = acc_ref[group, HALF:, lanes] * score_scale
            dq_ref[low : low + HALF, :] = (first * cos + second * sin).astype(bf16)
            dq_ref[low + HALF : low + HEAD_SIZE, :] = (second * cos - first * sin).astype(bf16)


def attend_back(visible, q, d_out, att_t, lse, cos, sin, kvs):
    width, rows = q.shape
    key_rows = kvs[0].shape[0]
    lanes = SHARING * rows
    return pl.pallas_call(
        attend_back_kernel,
        out_shape=(shape((width, rows), bf16),) + (shape((key_rows, rows), bf16),) * 4,
        in_specs=[in_smem()] + [in_vmem()] * 10,
        out_specs=(in_vmem(),) * 5,
        scratch_shapes=[
            pltpu.VMEM((KEY_VALUE_HEADS, HEAD_SIZE, lanes), f32),
            pltpu.VMEM((KEY_VALUE_HEADS, lanes), f32),
        ],
        compiler_params=params(),
        cost_estimate=cost(2 * rows * width * 4 * rows * 10, 10 * width * rows * 2),
        name="attend_back",
    )(visible, q, d_out, att_t, lse, cos, sin, *kvs)


def leave_kernel(
    h_ref,
    dmid_ref,
    dq_ref,
    own_ref,
    got_ref,
    gain_ref,
    cos_ref,
    sin_ref,
    w_ref,
    g_ref,
    dqkv_ref,
    dgain_ref,
    turned_ref,
):
    width, rows = dq_ref.shape
    key_width = own_ref.shape[0] // 2
    wide = turned_ref.shape[0]
    cos, sin = cos_ref[...], sin_ref[...]
    turned_ref[:width, :] = dq_ref[...]
    summed = own_ref[...].astype(f32) + got_ref[...].astype(f32)
    for head in range(KEY_VALUE_HEADS):
        low = head * HEAD_SIZE
        first = summed[low : low + HALF]
        second = summed[low + HALF : low + HEAD_SIZE]
        base = width + low
        turned_ref[base : base + HALF, :] = (first * cos + second * sin).astype(bf16)
        turned_ref[base + HALF : base + HEAD_SIZE, :] = (second * cos - first * sin).astype(bf16)
    turned_ref[width + key_width : width + 2 * key_width, :] = summed[key_width:].astype(bf16)
    turned_ref[width + 2 * key_width :, :] = jnp.zeros((wide - width - 2 * key_width, rows), bf16)
    d_mixed = turned_ref[...].T
    dqkv_ref[...] = d_mixed
    d_normed = nt(d_mixed, w_ref[:, :wide])
    hidden = h_ref[...]
    factor = inverse_rms(hidden)
    unit = hidden * factor
    dgain_ref[...] = jnp.sum(d_normed * unit, axis=0, keepdims=True)
    scaled = d_normed * gain_ref[...]
    grad = dmid_ref[...] + factor * (
        scaled - unit * jnp.mean(scaled * unit, axis=-1, keepdims=True)
    )
    g_ref[...] = grad if g_ref.dtype == f32 else grad.T.astype(bf16)


def leave(hidden, d_middle, dq, own, got, gain, cos, sin, weights_a):
    rows, width = hidden.shape
    key_width = KEY_VALUE_HEADS * HEAD_SIZE
    wide = width + 2 * key_width + HEAD_SIZE
    return pl.pallas_call(
        leave_kernel,
        out_shape=(
            shape((rows, width), f32),
            shape((rows, wide), bf16),
            shape((1, width), f32),
        ),
        in_specs=[in_vmem()] * 9,
        out_specs=(in_vmem(),) * 3,
        scratch_shapes=[pltpu.VMEM((wide, rows), bf16)],
        compiler_params=params(),
        cost_estimate=cost(2 * rows * width * wide, width * wide * 2 + rows * width * 14),
        name="leave",
    )(hidden, d_middle, dq, own, got, gain, cos, sin, kept(weights_a))


def grad_parts(place_ref, right, keep_ref, send_ref, xt_ref):
    block, step = keep_ref.shape[2:]
    core, chip, quarter = place_ref[0], place_ref[1], place_ref[2]
    for part in range(4):
        columns = right(part * step, (part + 1) * step)
        for away in range(2):
            for out_ref, which in ((keep_ref, core), (send_ref, 1 - core)):
                start = pl.multiple_of((2 * (chip ^ away) + which) * block, 16)
                out_ref[away, part ^ quarter] = nn(
                    xt_ref[pl.ds(start, block), :], columns
                ).astype(bf16)


def feed_back_gate_kernel(*refs):
    (place_ref, g_ref, middle_ref, gating_ref, upward_ref, gain_ref, nf2_ref, nf_ref, dgu2_ref,
     a_ref, gu_hbm, dn_ref, dmid_ref, gm_ref, do_ref, dgain_ref, keep_ref, send_ref, keep2_ref,
     send2_ref, gb_ref, dgu_ref, sum_ref, xt_ref, gu_ref, gu_sems) = refs
    feed_back_kernel(
        g_ref, middle_ref, gating_ref, upward_ref, gain_ref, a_ref, gu_hbm, dn_ref, gb_ref, dgu_ref,
        dmid_ref, gm_ref, do_ref, dgain_ref, sum_ref, gu_ref, gu_sems,
    )

    rows = nf_ref.shape[0]
    ffn = gating_ref.shape[1]
    xt_ref[:, :rows] = nf2_ref[...].T
    xt_ref[:, rows:] = nf_ref[...].T
    for base, out_refs in ((0, (keep_ref, send_ref)), (ffn, (keep2_ref, send2_ref))):

        def right(low, high, base=base):
            return jnp.concatenate(
                [dgu2_ref[:, base + low : base + high], dgu_ref[:, base + low : base + high]], axis=0
            )

        grad_parts(place_ref, right, *out_refs, xt_ref)


def feed_back_gate(place, grad, middle, gating, upward, gain, nf2, nf, dgu2, weights):
    rows, width = grad.shape
    weights_a, weights_gu, weights_dn = weights
    ffn = weights_dn.shape[1]
    wo_wide = width + HEAD_SIZE
    return pl.pallas_call(
        feed_back_gate_kernel,
        out_shape=(
            shape((rows, width), f32),
            shape((rows, wo_wide), bf16),
            shape((width, rows), bf16),
            shape((1, width), f32),
        )
        + (shape((2, 4, width // 4, ffn // 4), bf16),) * 4,
        in_specs=[in_smem()] + [in_vmem()] * 9 + [anywhere(), in_vmem()],
        out_specs=(in_vmem(),) * 8,
        scratch_shapes=[
            pltpu.VMEM((rows, width), bf16),
            pltpu.VMEM((rows, 2 * ffn), bf16),
            pltpu.VMEM((rows, width), f32),
            pltpu.VMEM((width, 2 * rows), bf16),
            pltpu.VMEM((width, 2 * ffn), bf16),
            pltpu.SemaphoreType.DMA((4,)),
        ],
        compiler_params=params(FFN_MEBIBYTES),
        cost_estimate=cost(2 * rows * width * (8 * ffn), 3 * width * ffn * 2 + rows * ffn * 8),
        name="feed_back_gate",
    )(place, grad, middle, gating, upward, gain, nf2, nf, dgu2, kept(weights_a), in_hbm(weights_gu),
      kept(weights_dn))


def leave_mixed_kernel(*refs):
    (place_ref, h_ref, dmid_ref, dq_ref, own_ref, got_ref, gain_ref, cos_ref, sin_ref, n1_ref, n2_ref,
     d1_ref, a1_ref, a2_ref, m1_ref, m2_ref, attention_gain_ref, ffn_gain_ref, ffn_gain2_ref, w_ref,
     g_ref, keep_ref, send_ref, d2_ref, dgain_ref, turned_ref, nt_ref, at_ref, gains_ref) = refs
    leave_kernel(
        h_ref, dmid_ref, dq_ref, own_ref, got_ref, gain_ref, cos_ref, sin_ref, w_ref, g_ref, d2_ref,
        dgain_ref, turned_ref,
    )
    gains = (attention_gain_ref[...] + dgain_ref[...], ffn_gain_ref[...] + ffn_gain2_ref[...])
    attention_grad_kernel(
        place_ref, n1_ref, n2_ref, d1_ref, d2_ref, a1_ref, a2_ref, m1_ref, m2_ref, gains, keep_ref,
        send_ref, nt_ref, at_ref, gains_ref,
    )


def leave_mixed(
    place, hidden, d_middle, dq, own, got, gain, cos, sin, normed, dqkv2, att, gm, gain_grads, weights_a
):
    rows, width = hidden.shape
    key_width = KEY_VALUE_HEADS * HEAD_SIZE
    wide = width + 2 * key_width + HEAD_SIZE
    block = width // 4 + GAIN_ROWS
    columns = 2 * width + 2 * key_width
    return pl.pallas_call(
        leave_mixed_kernel,
        out_shape=(shape((width, rows), bf16),)
        + (shape((2, 4, block, columns // 4), bf16),) * 2,
        in_specs=[in_smem()] + [in_vmem()] * 19,
        out_specs=(in_vmem(),) * 3,
        scratch_shapes=[
            pltpu.VMEM((rows, wide), bf16),
            pltpu.VMEM((1, width), f32),
            pltpu.VMEM((wide, rows), bf16),
            pltpu.VMEM((width, 2 * rows), bf16),
            pltpu.VMEM((width, 2 * rows), bf16),
            pltpu.VMEM((GAIN_ROWS, columns), f32),
        ],
        compiler_params=params(),
        cost_estimate=cost(6 * rows * width * wide, width * wide * 2 + rows * width * 14),
        name="leave_mixed",
    )(place, hidden, d_middle, dq, own, got, gain, cos, sin, *normed, dqkv2, *att, *gm, *gain_grads,
      kept(weights_a))


def down_grad_kernel(place_ref, g2_ref, g_ref, inner2_ref, inner_ref, keep_ref, send_ref, gt_ref):
    rows = g2_ref.shape[0]
    height, step = keep_ref.shape[2:]
    gt_ref[:, :rows] = g2_ref[...].T
    gt_ref[:, rows:] = g_ref[...].astype(bf16).T
    core, chip, quarter = place_ref[0], place_ref[1], place_ref[2]
    for away in range(2):
        for out_ref, which in ((keep_ref, core), (send_ref, 1 - core)):
            columns = pl.ds(pl.multiple_of((2 * (chip ^ away) + which) * step, 128), step)
            right = jnp.concatenate([inner2_ref[:, columns], inner_ref[:, columns]], axis=0)
            for part in range(4):
                out_ref[away, part ^ quarter] = nn(
                    gt_ref[part * height : (part + 1) * height, :], right
                ).astype(bf16)


def down_grad_parts(place, g2, g, inner2, inner):
    rows, width = g.shape
    ffn = inner.shape[1]
    return pl.pallas_call(
        down_grad_kernel,
        out_shape=(shape((2, 4, width // 4, ffn // 4), bf16),) * 2,
        in_specs=[in_smem()] + [in_vmem()] * 4,
        out_specs=(in_vmem(),) * 2,
        scratch_shapes=[pltpu.VMEM((width, 2 * rows), bf16)],
        compiler_params=params(),
        cost_estimate=cost(4 * rows * width * ffn, width * ffn * 2),
        name="down_grad",
    )(place, g2, g, inner2, inner)


def attention_grad_kernel(
    place_ref, n1_ref, n2_ref, d1_ref, d2_ref, a1_ref, a2_ref, m1_ref, m2_ref, gains,
    keep_ref, send_ref, nt_ref, at_ref, gains_ref,
):
    rows = n1_ref.shape[0]
    block = n1_ref.shape[1] // 4
    wide = d1_ref.shape[1]
    edge = wide - 128
    step = keep_ref.shape[3]
    nt_ref[:, :rows] = n1_ref[...].T
    nt_ref[:, rows:] = n2_ref[...].T
    at_ref[:, :rows] = a1_ref[...].T
    at_ref[:, rows:] = a2_ref[...].T
    half = GAIN_ROWS // 2
    gains_ref[...] = jnp.zeros_like(gains_ref)
    for i, gain in enumerate(gains):
        gains_ref[i * half : (i + 1) * half, : gain.shape[1]] = jnp.broadcast_to(
            gain, (half, gain.shape[1])
        )
    core, chip, quarter = place_ref[0], place_ref[1], place_ref[2]
    d_mixed = jnp.concatenate([d1_ref[...], d2_ref[...]], axis=0)
    d_out = jnp.concatenate([m1_ref[...], m2_ref[...]], axis=0)
    for away in range(2):
        for out_ref, which in ((keep_ref, core), (send_ref, 1 - core)):
            member = 2 * (chip ^ away) + which
            start = pl.multiple_of(member * block, 16)
            normed = nt_ref[pl.ds(start, block), :]
            attended = at_ref[pl.ds(start, block), :]
            for part in range(4):
                low, high = part * step, (part + 1) * step
                pieces = []
                if low < edge:
                    pieces.append(nn(normed, d_mixed[:, low : min(high, edge)]))
                if low <= edge < high:
                    pieces.append(nn(normed, d_mixed[:, edge:]) + nn(attended, d_out[:, :128]))
                if high > wide:
                    base = wide - 128
                    pieces.append(nn(attended, d_out[:, max(low, wide) - base : high - base]))
                piece = pieces[0] if len(pieces) == 1 else jnp.concatenate(pieces, axis=1)
                out_ref[away, part ^ quarter, :block, :] = piece.astype(bf16)
                out_ref[away, part ^ quarter, block:, :] = gains_ref[:, low:high].astype(bf16)


def finish_kernel(place_ref, p0_ref, p1_ref, p2_ref, p3_ref, out_ref):
    part = pl.program_id(0)
    for i, ref in enumerate((p0_ref, p1_ref, p2_ref, p3_ref)):

        @pl.when(part == i)
        def _(ref=ref):
            out_ref[...] = ref[...].astype(f32)


def finish(place, pieces, by_rows):
    height, step = pieces[0].shape
    whole = pl.BlockSpec((height, step), lambda i, place: (0, 0))
    if by_rows:
        dims, index = (4 * height, step), lambda i, place: (i ^ place[2], 0)
    else:
        dims, index = (height, 4 * step), lambda i, place: (0, i ^ place[2])
    return pl.pallas_call(
        finish_kernel,
        grid_spec=pltpu.PrefetchScalarGridSpec(
            num_scalar_prefetch=1,
            grid=(4,),
            in_specs=[whole] * 4,
            out_specs=pl.BlockSpec((height, step), index),
        ),
        out_shape=shape(dims, f32),
        compiler_params=params(),
        cost_estimate=cost(0, 24 * height * step),
        name="finish",
    )(place, *pieces)


def finish_mixed_kernel(
    place_ref, p0_ref, p1_ref, p2_ref, p3_ref, query_ref, key_ref, value_ref, out_ref, gain_ref,
    mixed_ref,
):
    quarter = place_ref[2]
    block, width = query_ref.shape
    key_width = key_ref.shape[0]
    step = p0_ref.shape[1]
    for i, ref in enumerate((p0_ref, p1_ref, p2_ref, p3_ref)):
        start = pl.multiple_of((quarter ^ i) * step, 128)
        mixed_ref[:, pl.ds(start, step)] = ref[...].astype(f32)
    first_end = width + key_width
    second_end = first_end + key_width
    query_ref[...] = mixed_ref[:block, :width]
    key_ref[...] = mixed_ref[:block, width:first_end].T
    value_ref[...] = mixed_ref[:block, first_end:second_end].T
    out_ref[...] = mixed_ref[:block, second_end:]
    gain_ref[...] = mixed_ref[block:, : gain_ref.shape[1]]


def finish_mixed(place, pieces, width, key_width):
    height, step = pieces[0].shape
    block = height - GAIN_ROWS
    return pl.pallas_call(
        finish_mixed_kernel,
        out_shape=(
            shape((block, width), f32),
            shape((key_width, block), f32),
            shape((key_width, block), f32),
            shape((block, width), f32),
            shape((GAIN_ROWS, width + HEAD_SIZE), f32),
        ),
        in_specs=[in_smem()] + [in_vmem()] * 4,
        out_specs=(in_vmem(),) * 5,
        scratch_shapes=[pltpu.VMEM((height, 4 * step), f32)],
        compiler_params=params(),
        cost_estimate=cost(0, 24 * height * step),
        name="finish_mixed",
    )(place, *pieces)


def flip(value, axis_name, distance):
    size = lax.axis_size(axis_name)
    return lax.ppermute(value, axis_name, [(i, i ^ distance) for i in range(size)])


def pick(condition, when_true, when_false):
    return jnp.where(condition, when_true, when_false)


def order_by(bit, own, other):
    return (pick(bit == 1, other, own), pick(bit == 1, own, other))


def exchange_kv(block):
    beside = flip(block, "fsdp", 1)
    across = flip(block, "fsdp", 2)
    diagonal = flip(across, "fsdp", 1)
    return (block, beside, across, diagonal)


def fold_kv(pieces):
    rows = pieces[0].shape[0]
    got = flip(jnp.concatenate([pieces[1], pieces[3]], axis=0), "fsdp", 1)
    return total(pieces[0], got[:rows]), total(pieces[2], got[rows:])


def return_kv(pieces):
    own, across = fold_kv(pieces)
    return own, flip(across, "fsdp", 2)


def total(*terms):
    result = terms[0].astype(f32)
    for term in terms[1:]:
        result = result + term.astype(f32)
    return result.astype(bf16)


class Order:
    def __init__(self, *token):
        self.token = token

    def tie(self, *values):
        tied = lax.optimization_barrier(self.token + values)[len(self.token) :]
        return tied[0] if len(tied) == 1 else tied

    def done(self, value):
        self.token = (value,)
        return value

    def done_all(self, *values):
        self.token = values
        return values


class Reduction:
    def __init__(self, order, keep, send):
        self.order = order
        self.keep = keep
        self.core = flip(order.tie(send), "fsdp", 1)

    def chip(self):
        self.core = self.order.tie(self.core)
        high = total(self.keep[1, 2:], self.core[1, 2:])
        low = total(self.keep[1, :2], self.core[1, :2])
        high, low = self.order.done_all(high, low)
        self.high = flip(high, "fsdp", 2)
        self.low = flip(low, "fsdp", 2)

    def first(self, both=False):
        if both:
            self.high, self.low = self.order.tie(self.high, self.low)
        else:
            self.high = self.order.tie(self.high)
        out = total(self.keep[0, 2:], self.core[0, 2:], self.high)
        self.got = flip(self.order.done(out), "dp", 1)

    def rest(self):
        self.low = self.order.done(self.order.tie(self.low))

    def second(self):
        self.got, self.low = self.order.tie(self.got, self.low)
        self.terms = (self.keep[0, :2], self.core[0, :2], self.low, self.got)
        self.got = flip(self.order.done(total(*[term[1] for term in self.terms])), "dp", 2)

    def third(self):
        size = lax.axis_size("dp")
        own = total(*[term[0] for term in self.terms], self.order.tie(self.got))
        distance = 4
        while 2 * distance < size:
            own = total(own, flip(own, "dp", distance))
            distance *= 2
        self.own = self.order.done(own)
        self.got = flip(own, "dp", distance) if distance < size else jnp.zeros_like(own)

    def back(self):
        self.own = self.order.done(total(self.own, self.order.tie(self.got)))
        self.beside = flip(self.own, "dp", 2)
        self.pieces = [self.own, self.beside, flip(self.own, "dp", 1)]

    def back_again(self):
        self.beside = self.order.done(self.order.tie(self.beside))
        self.pieces.append(flip(self.beside, "dp", 1))

    def end(self):
        return self.order.tie(*self.pieces)


def rotation(token_positions):
    frequency = rope_base ** (-jnp.arange(HALF, dtype=f32) / HALF)
    angles = frequency[:, None] * token_positions.astype(f32)[None, :]
    return jnp.cos(angles), jnp.sin(angles)


def body(
    tokens,
    cotangent,
    sequence_ids,
    span_position,
    attention_norm,
    query_weight,
    key_matrix,
    value_matrix,
    output_weight,
    feedforward_norm,
    gate_weight,
    up_weight,
    down_weight,
):
    rows, width = tokens.shape
    key_width = key_matrix.shape[1]
    ffn = gate_weight.shape[1]
    itself = lax.axis_index("fsdp")
    outer = lax.axis_index("dp")
    quarter = 2 * (outer % 2) + (outer // 2) % 2
    place = jnp.stack([itself % 2, itself // 2, quarter]).astype(jnp.int32)

    outer = lax.axis_index("dp")
    bits = jnp.stack([outer % 2, (outer // 2) % 2, itself]).astype(jnp.int32)
    packed, *mine = pack(
        bits, query_weight, key_matrix.T, value_matrix.T, output_weight, gate_weight, up_weight
    )
    down_t = down_weight.T
    half = width // 2
    mine.append(pick(outer % 2 == 1, down_t[half:], down_t[:half]))
    gains = jnp.stack([attention_norm, feedforward_norm], axis=0)
    gains = [flip(gains, "fsdp", distance) if distance else gains for distance in range(4)]
    mine = Order(*gains).tie(*mine)
    far = [flip(piece, "fsdp", 2) for piece in mine]
    shards = (packed, gate_weight, up_weight, down_t)
    near = [flip(shard, "fsdp", 1) for shard in shards]
    sequence_ids, span_position = Order(*mine).tie(sequence_ids, span_position)
    places = jnp.arange(rows, dtype=jnp.int32) + span_position[itself] * rows
    cos, sin = rotation(places)
    others = itself ^ jnp.arange(4)
    visible = (
        (sequence_ids[others] == sequence_ids[itself])
        & (span_position[others] <= span_position[itself])
    ).astype(jnp.int32)

    beside = order_by(itself % 2, gains[0], gains[1])
    away = order_by(itself % 2, gains[2], gains[3])
    chip = itself // 2 == 1
    gains = jnp.concatenate(
        [pick(chip, a, n) for a, n in zip(away, beside)]
        + [pick(chip, n, a) for a, n in zip(away, beside)],
        axis=1,
    ).astype(f32)
    attention_gain, ffn_gain = gains[:1], gains[1:]
    order = Order(cos, sin, visible, attention_gain, ffn_gain)
    share = ((1, 0), (1, 0), (2, 1), (1, 0))

    def shared(i):
        got = order.done(order.tie(far[i]))
        return got, flip(got, "dp", share[i][0])

    def gathered(i, got, other):
        return [shards[i], near[i], got, other, flip(got, "fsdp", 1), flip(other, "fsdp", 1)]

    shared_a = shared(0)
    order.done_all(*order.tie(*shared_a))
    shared_gate = shared(1)
    sources_a = gathered(0, *shared_a)
    order.done_all(*order.tie(*near), *sources_a)
    tokens_t = order.tie(tokens.T)
    hidden, normed, q, kv, weights_a = enter_first(
        bits, tokens_t, attention_gain, cos, sin, shared_plan(0, 0, 0), tuple(sources_a)
    )
    order.done(kv)
    shared_up = shared(2)
    shared_gate = order.done_all(*order.tie(*shared_gate))
    kvs = exchange_kv(kv)
    shared_down = shared(3)
    order.done_all(*order.tie(*shared_up))
    sources_gu = gathered(1, *shared_gate) + gathered(2, *shared_up)
    sources_dn = gathered(3, *order.tie(*shared_down))
    plan_gu = shared_plan(0, 0, 0) + shared_plan(6, ffn, 1)
    plan_dn = shared_plan(0, None, 0)
    finished, att, att_t, lse, middle, nf, gating, upward, inner, weights_gu, weights_dn = forward_block(
        visible, bits, hidden, q, kvs, ffn_gain, weights_a, tuple(sources_gu), tuple(sources_dn),
        (plan_gu, plan_dn),
    )
    weights = (weights_a, weights_gu, weights_dn)
    saved = [(hidden, normed, q, kvs, att, att_t, lse, middle, nf, gating, upward, inner)]
    hidden = finished
    normed, q, kv = enter(hidden, attention_gain, cos, sin, weights_a)
    kvs = exchange_kv(kv)
    activations, att, att_t, lse, middle, nf, gating, upward, inner = forward_block(
        visible, bits, hidden, q, kvs, ffn_gain, weights_a, (weights_gu,), (weights_dn,)
    )
    saved.append((hidden, normed, q, kvs, att, att_t, lse, middle, nf, gating, upward, inner))

    hidden, normed2, q, kvs, att2, att_t, lse, middle, nf2, gating, upward, inner2 = saved[1]
    gb2, dgu2, d_middle, gm2, d_out, ffn_gain_grad2 = feed_back(
        cotangent.T, middle, gating, upward, ffn_gain, weights
    )
    dq, *dkvs = attend_back(visible, q, d_out, att_t, lse, cos, sin, kvs)
    own, got = return_kv(dkvs)
    grad, dqkv2, attention_gain_grad2 = leave(
        hidden, d_middle, dq, own, got, attention_gain, cos, sin, weights_a
    )

    hidden, normed, q, kvs, att, att_t, lse, middle, nf, gating, upward, inner = saved[0]
    order = Order(grad)
    down = Reduction(order, *down_grad_parts(place, gb2, grad, inner2, inner))
    down.chip()
    d_middle, gm, d_out, ffn_gain_grad, *rest = feed_back_gate(
        place, order.tie(grad), middle, gating, upward, ffn_gain, nf2, nf, dgu2, weights
    )
    order.done(d_middle)
    down.first(both=True)
    gate = Reduction(order, *rest[:2])
    gate.chip()
    up = Reduction(order, *rest[2:])
    dq, *dkvs = attend_back(visible, order.tie(q), d_out, att_t, lse, cos, sin, kvs)
    order.done(dq)
    gate.first()
    down.second()
    own, across = fold_kv(order.tie(*dkvs))
    order.done(across)
    gate.rest()
    down.third()
    across = order.tie(across)
    got = order.done(order.tie(flip(across, "fsdp", 2)))
    gate.second()
    up.chip()
    d_middle = order.tie(d_middle)
    grad, *mixed = leave_mixed(
        place,
        hidden,
        d_middle,
        dq,
        own,
        got,
        attention_gain,
        cos,
        sin,
        (normed2, normed),
        dqkv2,
        (att2, att),
        (gm2, gm),
        (attention_gain_grad2, ffn_gain_grad2, ffn_gain_grad),
        weights_a,
    )
    order.done(grad)
    up.first()
    down.back()
    gate.third()
    mixed = Reduction(order, *mixed)
    mixed.chip()
    up.second()
    gate.back()
    mixed.first()
    up.third()
    down.back_again()
    mixed.rest()
    mixed.second()
    gate.back_again()
    up.back()
    down_grad = order.done(finish(place, down.end(), True))
    mixed.third()
    up.back_again()
    gate_grad = order.done(finish(place, gate.end(), False))
    mixed.back()
    up_grad = order.done(finish(place, up.end(), False))
    mixed.back_again()
    query_grad, key_grad, value_grad, output_grad, gain_grads = finish_mixed(
        place, mixed.end(), width, key_width
    )
    shard_rows = attention_norm.shape[0]
    gain_grads = lax.dynamic_slice_in_dim(gain_grads, itself * shard_rows, shard_rows, axis=1)
    return (
        activations.T,
        grad.T,
        gain_grads[0],
        query_grad,
        key_grad.T,
        value_grad.T,
        output_grad,
        gain_grads[GAIN_ROWS // 2],
        gate_grad,
        up_grad,
        down_grad.T,
    )


def solution(mesh):
    return jax.shard_map(
        body,
        mesh=mesh,
        in_specs=(
            P(("dp", "fsdp"), None),
            P(("dp", "fsdp"), None),
            P("dp"),
            P("dp"),
            P("fsdp"),
            P("fsdp", None),
            P("fsdp", None),
            P("fsdp", None),
            P("fsdp", None),
            P("fsdp"),
            P("fsdp", None),
            P("fsdp", None),
            P("fsdp", None),
        ),
        out_specs=(
            P(("dp", "fsdp"), None),
            P(("dp", "fsdp"), None),
            P("fsdp"),
            P("fsdp", None),
            P("fsdp", None),
            P("fsdp", None),
            P("fsdp", None),
            P("fsdp"),
            P("fsdp", None),
            P("fsdp", None),
            P("fsdp", None),
        ),
        check_vma=False,
    )
```

```python
import functools

import jax
import jax.numpy as jnp
from jax import lax
from jax.experimental import pallas as pl
from jax.experimental.pallas import tpu as pltpu
from jax.sharding import PartitionSpec as P

QUERY_HEADS = 15
KEY_VALUE_HEADS = 5
HEAD_SIZE = 64
SHARING = QUERY_HEADS // KEY_VALUE_HEADS
HALF = HEAD_SIZE // 2

epsilon = 1e-05
rope_base = 10000.0
masked = -1e30
score_scale = HEAD_SIZE ** (-0.5)

bf16 = jnp.bfloat16
f32 = jnp.float32
GAIN_ROWS = 16
FFN_MEBIBYTES = 26


def nn(left, right):
    return jnp.dot(left, right, preferred_element_type=f32)


def nt(left, right):
    return lax.dot_general(left, right, (((1,), (1,)), ((), ())), preferred_element_type=f32)


def in_vmem():
    return pl.BlockSpec(memory_space=pltpu.VMEM)


def in_smem():
    return pl.BlockSpec(memory_space=pltpu.SMEM)


def anywhere():
    return pl.BlockSpec(memory_space=pl.ANY)


def params(mebibytes=14):
    return pltpu.CompilerParams(vmem_limit_bytes=mebibytes * 1024 * 1024)


def shape(dims, dtype):
    return jax.ShapeDtypeStruct(dims, dtype)


def kept(array):
    return pltpu.with_memory_space_constraint(array, pltpu.VMEM)


def in_hbm(array):
    return pltpu.with_memory_space_constraint(array, pltpu.HBM)


def cost(flops, bytes_accessed):
    return pl.CostEstimate(flops=int(flops), bytes_accessed=int(bytes_accessed), transcendentals=0)


def inverse_rms(hidden):
    return lax.rsqrt(jnp.mean(hidden * hidden, axis=-1, keepdims=True) + epsilon)


def pack_kernel(
    bits_ref, query_hbm, key_hbm, value_hbm, out_hbm, gate_hbm, up_hbm, packed_hbm, mine_hbm,
    mine_gate_hbm, mine_up_hbm, query_ref, key_ref, value_ref, out_ref, gate_ref, up_ref, packed_ref,
    mine_ref, sems,
):
    half = gate_ref.shape[1]
    loads = [
        pltpu.make_async_copy(source, target, sems.at[i])
        for i, (source, target) in enumerate(
            (
                (query_hbm, query_ref),
                (key_hbm, key_ref),
                (value_hbm, value_ref),
                (out_hbm, out_ref),
                (gate_hbm.at[:, pl.ds(pl.multiple_of(bits_ref[0] * half, 128), half)], gate_ref),
                (up_hbm.at[:, pl.ds(pl.multiple_of(bits_ref[1] * half, 128), half)], up_ref),
            )
        )
    ]
    for load in loads:
        load.start()
    for load in loads[:4]:
        load.wait()
    packed_ref[...] = jnp.concatenate(
        [
            query_ref[...].astype(f32),
            key_ref[...].astype(f32).T,
            value_ref[...].astype(f32).T,
            out_ref[...].astype(f32),
        ],
        axis=1,
    ).astype(bf16)
    wide = mine_ref.shape[1]
    mine_ref[...] = packed_ref[:, pl.ds(pl.multiple_of(bits_ref[0] * wide, 128), wide)]
    for load in loads[4:]:
        load.wait()
    stores = [
        pltpu.make_async_copy(source, target, sems.at[i])
        for i, (source, target) in enumerate(
            (
                (mine_ref, mine_hbm),
                (gate_ref, mine_gate_hbm),
                (up_ref, mine_up_hbm),
                (packed_ref, packed_hbm),
            )
        )
    ]
    for store in stores:
        store.start()
    for store in stores:
        store.wait()


def pack(bits, query, key_t, value_t, out, gate, up):
    rows, width = query.shape
    columns = 2 * width + 2 * key_t.shape[0]
    ffn = gate.shape[1]
    return pl.pallas_call(
        pack_kernel,
        out_shape=(
            pltpu.HBM((rows, columns), bf16),
            pltpu.HBM((rows, columns // 2), bf16),
            pltpu.HBM((rows, ffn // 2), bf16),
            pltpu.HBM((rows, ffn // 2), bf16),
        ),
        in_specs=[in_smem()] + [anywhere()] * 6,
        out_specs=(anywhere(),) * 4,
        scratch_shapes=[
            pltpu.VMEM((rows, width), bf16),
            pltpu.VMEM(key_t.shape, bf16),
            pltpu.VMEM(value_t.shape, bf16),
            pltpu.VMEM((rows, width), bf16),
            pltpu.VMEM((rows, ffn // 2), bf16),
            pltpu.VMEM((rows, ffn // 2), bf16),
            pltpu.VMEM((rows, columns), bf16),
            pltpu.VMEM((rows, columns // 2), bf16),
            pltpu.SemaphoreType.DMA((6,)),
        ],
        compiler_params=params(),
        cost_estimate=cost(0, 8 * rows * columns),
        name="pack",
    )(bits, *[in_hbm(part) for part in (query, key_t, value_t, out, gate, up)])


def piece_copies(plan, bits_ref, sources, target_ref, sems):
    me = bits_ref[2]
    copies = []
    for i, (which, member, column, part, bit) in enumerate(plan):
        source = sources[which]
        height, width = source.shape
        if column is None:
            turned = pl.ds(pl.multiple_of((me ^ member) * width, 128), width)
            if part is None:
                rows = pl.ds(0, height)
            else:
                rows = pl.ds(pl.multiple_of((bits_ref[bit] ^ part) * height, 16), height)
            target = target_ref.at[rows, turned]
        else:
            rows = pl.ds(pl.multiple_of((me ^ member) * height, 16), height)
            if part is None:
                columns = pl.ds(column, width)
            else:
                columns = pl.ds(
                    pl.multiple_of(column + (bits_ref[bit] ^ part) * width, 128), width
                )
            target = target_ref.at[rows, columns]
        copies.append(pltpu.make_async_copy(source, target, sems.at[i]))
    return copies


def shared_plan(first, column, bit):
    return (
        (first, 0, column, None, bit),
        (first + 1, 1, column, None, bit),
        (first + 2, 2, column, 0, bit),
        (first + 3, 2, column, 1, bit),
        (first + 4, 3, column, 0, bit),
        (first + 5, 3, column, 1, bit),
    )


def enter_body(hidden, gain_ref, cos_ref, sin_ref, ready, normed_ref, q_ref, kv_ref, w_ref):
    width = hidden.shape[1]
    key_width = kv_ref.shape[0] // 2
    mixed_width = width + key_width
    wide = width + 2 * key_width + HEAD_SIZE
    normed = (hidden * inverse_rms(hidden) * gain_ref[...]).astype(bf16)
    normed_ref[...] = normed
    cos, sin = cos_ref[...], sin_ref[...]
    ready()
    mixed = nn(normed, w_ref[:, :mixed_width]).T
    for head in range(QUERY_HEADS + KEY_VALUE_HEADS):
        low = head * HEAD_SIZE
        first = mixed[low : low + HALF]
        second = mixed[low + HALF : low + HEAD_SIZE]
        top = first * cos - second * sin
        bottom = second * cos + first * sin
        if head < QUERY_HEADS:
            q_ref[low : low + HALF, :] = (top * score_scale).astype(bf16)
            q_ref[low + HALF : low + HEAD_SIZE, :] = (bottom * score_scale).astype(bf16)
        else:
            low = low - width
            kv_ref[low : low + HALF, :] = top.astype(bf16)
            kv_ref[low + HALF : low + HEAD_SIZE, :] = bottom.astype(bf16)
    values = nn(normed, w_ref[:, mixed_width:wide]).T
    kv_ref[key_width:, :] = values[:key_width].astype(bf16)


def enter_first_kernel(plan, count, index_ref, h_ref, gain_ref, cos_ref, sin_ref, *refs):
    sources = refs[:count]
    hidden_ref, normed_ref, q_ref, kv_ref, w_ref, sems = refs[count:]
    copies = piece_copies(plan, index_ref, sources, w_ref, sems)
    for copy in copies:
        copy.start()
    hidden = h_ref[...].astype(f32).T
    hidden_ref[...] = hidden

    def ready():
        for copy in copies:
            copy.wait()

    enter_body(hidden, gain_ref, cos_ref, sin_ref, ready, normed_ref, q_ref, kv_ref, w_ref)


def enter_first(index, hidden_t, gain, cos, sin, plan, sources):
    width, rows = hidden_t.shape
    key_width = KEY_VALUE_HEADS * HEAD_SIZE
    columns = 2 * (width + key_width)
    return pl.pallas_call(
        functools.partial(enter_first_kernel, plan, len(sources)),
        out_shape=(
            shape((rows, width), f32),
            shape((rows, width), bf16),
            shape((width, rows), bf16),
            shape((2 * key_width, rows), bf16),
            pltpu.VMEM((width, columns), bf16),
        ),
        in_specs=[in_smem()] + [in_vmem()] * 4 + [anywhere()] * len(sources),
        out_specs=(in_vmem(),) * 5,
        scratch_shapes=[pltpu.SemaphoreType.DMA((len(plan),))],
        compiler_params=params(),
        cost_estimate=cost(4 * rows * width * width, width * columns * 4),
        name="enter_first",
    )(index, hidden_t, gain, cos, sin, *sources)


def enter_kernel(h_ref, gain_ref, cos_ref, sin_ref, w_ref, normed_ref, q_ref, kv_ref):
    enter_body(
        h_ref[...], gain_ref, cos_ref, sin_ref, lambda: None, normed_ref, q_ref, kv_ref, w_ref
    )


def enter(hidden, gain, cos, sin, weights_a):
    rows, width = hidden.shape
    key_width = KEY_VALUE_HEADS * HEAD_SIZE
    wide = width + 2 * key_width + HEAD_SIZE
    return pl.pallas_call(
        enter_kernel,
        out_shape=(
            shape((rows, width), bf16),
            shape((width, rows), bf16),
            shape((2 * key_width, rows), bf16),
        ),
        in_specs=[in_vmem()] * 5,
        out_specs=(in_vmem(),) * 3,
        compiler_params=params(),
        cost_estimate=cost(2 * rows * width * wide, width * wide * 2 + rows * width * 10),
        name="enter",
    )(hidden, gain, cos, sin, kept(weights_a))


def out_weight(a_ref):
    return a_ref[:, a_ref.shape[1] - a_ref.shape[0] - HEAD_SIZE :]


def stacked_heads(ref, group):
    parts = []
    for j in range(SHARING):
        low = (group * SHARING + j) * HEAD_SIZE
        parts.append(ref[low : low + HEAD_SIZE, :])
    return jnp.concatenate(parts, axis=1)


def key_block(ref, group):
    return ref[group * HEAD_SIZE : (group + 1) * HEAD_SIZE, :]


def value_block(ref, group):
    key_width = KEY_VALUE_HEADS * HEAD_SIZE
    return ref[key_width + group * HEAD_SIZE : key_width + (group + 1) * HEAD_SIZE, :]


def causal(rows):
    keys = lax.broadcasted_iota(jnp.int32, (rows, SHARING * rows), 0)
    queries = lax.broadcasted_iota(jnp.int32, (rows, SHARING * rows), 1) % rows
    return keys <= queries


def whole_copies(source_ref, target_ref, sems):
    parts = 4
    height = source_ref.shape[0] // parts
    return [
        pltpu.make_async_copy(
            source_ref.at[pl.ds(i * height, height), :],
            target_ref.at[pl.ds(i * height, height), :],
            sems.at[i],
        )
        for i in range(parts)
    ]


def forward_kernel(plans, counts, *refs):
    (visible_ref, bits_ref, h_ref, q_ref, kv0_ref, kv1_ref, kv2_ref, kv3_ref, gain_ref, a_ref) = refs[:10]
    gu_sources = refs[10 : 10 + counts[0]]
    dn_sources = refs[10 + counts[0] : 10 + counts[0] + counts[1]]
    refs = refs[10 + counts[0] + counts[1] :]
    (out_ref, att_ref, att_t_ref, lse_ref, middle_ref, nf_ref, gating_ref, upward_ref, inner_ref) = refs[:9]
    refs = refs[9:]
    gu_ref, gu_sems, dn_sems = refs[-3:]
    if plans is not None:
        gu_hbm, dn_ref = refs[:2]
        refs = refs[2:]
        gu_loads = piece_copies(plans[0], bits_ref, gu_sources, gu_ref, gu_sems)
        dn_loads = piece_copies(plans[1], bits_ref, dn_sources, dn_ref, dn_sems)
    else:
        (dn_ref,) = dn_sources
        gu_loads, dn_loads = whole_copies(gu_sources[0], gu_ref, gu_sems), []
    acc_ref, m_ref, l_ref, kvs_ref = refs[:4]
    rows, width = h_ref.shape
    ffn = inner_ref.shape[1]
    for load in gu_loads + dn_loads:
        load.start()

    allowed = causal(rows)
    for group in range(KEY_VALUE_HEADS):
        scores = nn(key_block(kv0_ref, group).T, stacked_heads(q_ref, group))
        scores = jnp.where(allowed, scores, masked)
        peak = jnp.max(scores, axis=0, keepdims=True)
        raised = jnp.exp(scores - peak)
        m_ref[group : group + 1, :] = peak
        l_ref[group : group + 1, :] = jnp.sum(raised, axis=0, keepdims=True)
        acc_ref[group] = nn(value_block(kv0_ref, group), raised.astype(bf16))
    for i, kv_ref in enumerate((kv1_ref, kv2_ref, kv3_ref)):
        kvs_ref[i] = kv_ref[...]

    @pl.loop(0, 3)
    def _(member):
        kv_ref = kvs_ref.at[member]

        @pl.when(visible_ref[member + 1] == 1)
        def _():
            for group in range(KEY_VALUE_HEADS):
                scores = nn(key_block(kv_ref, group).T, stacked_heads(q_ref, group))
                old = m_ref[group : group + 1, :]
                peak = jnp.maximum(old, jnp.max(scores, axis=0, keepdims=True))
                raised = jnp.exp(scores - peak)
                fade = jnp.exp(old - peak)
                m_ref[group : group + 1, :] = peak
                l_ref[group : group + 1, :] = l_ref[group : group + 1, :] * fade + jnp.sum(
                    raised, axis=0, keepdims=True
                )
                acc_ref[group] = acc_ref[group] * fade + nn(
                    value_block(kv_ref, group), raised.astype(bf16)
                )

    total = l_ref[...]
    lse_ref[...] = m_ref[...] + jnp.log(total)
    for group in range(KEY_VALUE_HEADS):
        mean = acc_ref[group] / total[group : group + 1, :]
        for j in range(SHARING):
            low = (group * SHARING + j) * HEAD_SIZE
            att_t_ref[low : low + HEAD_SIZE, :] = mean[:, j * rows : (j + 1) * rows].astype(bf16)
    attended = att_t_ref[...].T
    att_ref[...] = attended
    middle = h_ref[...] + nn(attended, out_weight(a_ref))[:, HEAD_SIZE:]
    middle_ref[...] = middle
    normed = (middle * inverse_rms(middle) * gain_ref[...]).astype(bf16)
    nf_ref[...] = normed
    for load in gu_loads:
        load.wait()
    gu_stores = whole_copies(gu_ref, gu_hbm, gu_sems) if plans is not None else []
    for store in gu_stores:
        store.start()
    step = 512
    for low in range(0, ffn, step):
        gating = nn(normed, gu_ref[:, low : low + step])
        upward = nn(normed, gu_ref[:, ffn + low : ffn + low + step])
        gating_ref[:, low : low + step] = gating.astype(bf16)
        upward_ref[:, low : low + step] = upward.astype(bf16)
        inner_ref[:, low : low + step] = (gating * jax.nn.sigmoid(gating) * upward).astype(bf16)
    for load in dn_loads:
        load.wait()
    finished = middle + nt(inner_ref[...], dn_ref[...])
    out_ref[...] = finished if plans is not None else finished.T.astype(bf16)
    for store in gu_stores:
        store.wait()


def forward_block(visible, index, hidden, q, kvs, gain, weights_a, gu, dn, plans=None):
    rows, width = hidden.shape
    ffn = gu[0].shape[1] if plans is not None else gu[0].shape[1] // 2
    lanes = SHARING * rows
    counts = (len(gu), len(dn))
    first = plans is not None
    whole = (pltpu.HBM((width, 2 * ffn), bf16), pltpu.VMEM((width, ffn), bf16))
    return pl.pallas_call(
        functools.partial(forward_kernel, plans, counts),
        out_shape=(
            shape((rows, width), f32) if first else shape((width, rows), bf16),
            shape((rows, width), bf16),
            shape((width, rows), bf16),
            shape((KEY_VALUE_HEADS, lanes), f32),
            shape((rows, width), f32),
            shape((rows, width), bf16),
            shape((rows, ffn), bf16),
            shape((rows, ffn), bf16),
            shape((rows, ffn), bf16),
        )
        + (whole if first else ()),
        in_specs=[in_smem()] * 2
        + [in_vmem()] * 8
        + [anywhere()] * counts[0]
        + [anywhere() if first else in_vmem()] * counts[1],
        out_specs=(in_vmem(),) * 9 + ((anywhere(), in_vmem()) if first else ()),
        scratch_shapes=[
            pltpu.VMEM((KEY_VALUE_HEADS, HEAD_SIZE, lanes), f32),
            pltpu.VMEM((KEY_VALUE_HEADS, lanes), f32),
            pltpu.VMEM((KEY_VALUE_HEADS, lanes), f32),
            pltpu.VMEM((3, *kvs[0].shape), bf16),
            pltpu.VMEM((width, 2 * ffn), bf16),
            pltpu.SemaphoreType.DMA((len(plans[0]) if first else 4,)),
            pltpu.SemaphoreType.DMA((len(plans[1]) if first else 1,)),
        ],
        compiler_params=params(FFN_MEBIBYTES),
        cost_estimate=cost(2 * rows * width * (4 * ffn), 3 * width * ffn * 2 + rows * ffn * 8),
        name="forward_first" if first else "forward_last",
    )(
        visible, index, hidden, q, *kvs, gain, kept(weights_a),
        *([*gu, *dn] if first else [in_hbm(gu[0]), kept(dn[0])]),
    )


def feed_back_kernel(
    g_ref,
    middle_ref,
    gating_ref,
    upward_ref,
    gain_ref,
    a_ref,
    gu_hbm,
    dn_ref,
    gb_ref,
    dgu_ref,
    dmid_ref,
    gm_ref,
    do_ref,
    dgain_ref,
    sum_ref,
    gu_ref,
    gu_sems,
):
    rows, width = middle_ref.shape
    ffn = gating_ref.shape[1]
    loads = whole_copies(gu_hbm, gu_ref, gu_sems)
    for load in loads:
        load.start()
    grad = g_ref[...] if g_ref.shape[0] == rows else g_ref[...].astype(f32).T
    short = grad.astype(bf16)
    gb_ref[...] = short
    step = 512
    for low in range(0, ffn, step):
        part = slice(low, low + step)
        behind = slice(ffn + low, ffn + low + step)
        d_inner = nn(short, dn_ref[:, part])
        gating = gating_ref[:, part].astype(f32)
        upward = upward_ref[:, part].astype(f32)
        gate = jax.nn.sigmoid(gating)
        d_gating = (d_inner * upward * (gate * (1.0 + gating * (1.0 - gate)))).astype(bf16)
        d_upward = (d_inner * (gating * gate)).astype(bf16)
        dgu_ref[:, part] = d_gating
        dgu_ref[:, behind] = d_upward
    for load in loads:
        load.wait()
    sum_ref[...] = nt(dgu_ref[...], gu_ref[...])
    d_normed = sum_ref[...]
    middle = middle_ref[...]
    factor = inverse_rms(middle)
    unit = middle * factor
    dgain_ref[...] = jnp.sum(d_normed * unit, axis=0, keepdims=True)
    scaled = d_normed * gain_ref[...]
    d_middle = grad + factor * (scaled - unit * jnp.mean(scaled * unit, axis=-1, keepdims=True))
    dmid_ref[...] = d_middle
    padded = jnp.concatenate(
        [jnp.zeros((rows, HEAD_SIZE), f32), d_middle], axis=1
    ).astype(bf16)
    gm_ref[...] = padded
    do_ref[...] = nt(padded, out_weight(a_ref)).T.astype(bf16)


def feed_back(grad, middle, gating, upward, gain, weights):
    rows, width = middle.shape
    weights_a, weights_gu, weights_dn = weights
    ffn = weights_dn.shape[1]
    wo_wide = width + HEAD_SIZE
    return pl.pallas_call(
        feed_back_kernel,
        out_shape=(
            shape((rows, width), bf16),
            shape((rows, 2 * ffn), bf16),
            shape((rows, width), f32),
            shape((rows, wo_wide), bf16),
            shape((width, rows), bf16),
            shape((1, width), f32),
        ),
        in_specs=[in_vmem()] * 6 + [anywhere(), in_vmem()],
        out_specs=(in_vmem(),) * 6,
        scratch_shapes=[
            pltpu.VMEM((rows, width), f32),
            pltpu.VMEM((width, 2 * ffn), bf16),
            pltpu.SemaphoreType.DMA((4,)),
        ],
        compiler_params=params(FFN_MEBIBYTES),
        cost_estimate=cost(2 * rows * width * (4 * ffn), 3 * width * ffn * 2 + rows * ffn * 8),
        name="feed_back",
    )(grad, middle, gating, upward, gain, kept(weights_a), in_hbm(weights_gu), kept(weights_dn))


def attend_back_kernel(
    visible_ref,
    q_ref,
    do_ref,
    att_ref,
    lse_ref,
    cos_ref,
    sin_ref,
    kv0_ref,
    kv1_ref,
    kv2_ref,
    kv3_ref,
    dq_ref,
    keep_ref,
    send_ref,
    acc_ref,
    row_ref,
    kvs_ref,
    dkvs_ref,
):
    rows = q_ref.shape[1]
    key_width = KEY_VALUE_HEADS * HEAD_SIZE
    allowed = causal(rows)
    for group in range(KEY_VALUE_HEADS):
        row_ref[group : group + 1, :] = jnp.sum(
            stacked_heads(do_ref, group).astype(f32) * stacked_heads(att_ref, group).astype(f32),
            axis=0,
            keepdims=True,
        )

    def one(group, kv_ref, dkv_ref, own):
        queries = stacked_heads(q_ref, group)
        d_out = stacked_heads(do_ref, group)
        keys = key_block(kv_ref, group)
        scores = nn(keys.T, queries)
        if own:
            scores = jnp.where(allowed, scores, masked)
        probs = jnp.exp(scores - lse_ref[group : group + 1, :])
        d_probs = nn(value_block(kv_ref, group).T, d_out)
        d_scores = (probs * (d_probs - row_ref[group : group + 1, :])).astype(bf16)
        dkv_ref[group * HEAD_SIZE : (group + 1) * HEAD_SIZE, :] = nt(queries, d_scores).astype(bf16)
        dkv_ref[key_width + group * HEAD_SIZE : key_width + (group + 1) * HEAD_SIZE, :] = nt(
            d_out, probs.astype(bf16)
        ).astype(bf16)
        moved = nn(keys, d_scores)
        if own:
            acc_ref[group] = moved
        else:
            acc_ref[group] += moved

    for group in range(KEY_VALUE_HEADS):
        one(group, kv0_ref, keep_ref.at[0], True)
    for i, kv_ref in enumerate((kv1_ref, kv2_ref, kv3_ref)):
        kvs_ref[i] = kv_ref[...]

    @pl.loop(0, 3)
    def _(member):
        kv_ref, dkv_ref = kvs_ref.at[member], dkvs_ref.at[member]

        @pl.when(visible_ref[member + 1] == 1)
        def _():
            for group in range(KEY_VALUE_HEADS):
                one(group, kv_ref, dkv_ref, False)

        @pl.when(visible_ref[member + 1] == 0)
        def _():
            dkv_ref[...] = jnp.zeros(dkv_ref.shape, bf16)

    send_ref[0] = dkvs_ref[0]
    keep_ref[1] = dkvs_ref[1]
    send_ref[1] = dkvs_ref[2]
    cos, sin = cos_ref[...], sin_ref[...]
    for group in range(KEY_VALUE_HEADS):
        for j in range(SHARING):
            low = (group * SHARING + j) * HEAD_SIZE
            lanes = slice(j * rows, (j + 1) * rows)
            first = acc_ref[group, :HALF, lanes] * score_scale
            second = acc_ref[group, HALF:, lanes] * score_scale
            dq_ref[low : low + HALF, :] = (first * cos + second * sin).astype(bf16)
            dq_ref[low + HALF : low + HEAD_SIZE, :] = (second * cos - first * sin).astype(bf16)


def attend_back(visible, q, d_out, att_t, lse, cos, sin, kvs):
    width, rows = q.shape
    key_rows = kvs[0].shape[0]
    lanes = SHARING * rows
    return pl.pallas_call(
        attend_back_kernel,
        out_shape=(shape((width, rows), bf16),) + (shape((2, key_rows, rows), bf16),) * 2,
        in_specs=[in_smem()] + [in_vmem()] * 10,
        out_specs=(in_vmem(),) * 3,
        scratch_shapes=[
            pltpu.VMEM((KEY_VALUE_HEADS, HEAD_SIZE, lanes), f32),
            pltpu.VMEM((KEY_VALUE_HEADS, lanes), f32),
            pltpu.VMEM((3, key_rows, rows), bf16),
            pltpu.VMEM((3, key_rows, rows), bf16),
        ],
        compiler_params=params(),
        cost_estimate=cost(2 * rows * width * 4 * rows * 10, 10 * width * rows * 2),
        name="attend_back",
    )(visible, q, d_out, att_t, lse, cos, sin, *kvs)


def leave_kernel(
    h_ref,
    dmid_ref,
    dq_ref,
    own_ref,
    got_ref,
    gain_ref,
    cos_ref,
    sin_ref,
    w_ref,
    g_ref,
    dqkv_ref,
    dgain_ref,
    turned_ref,
):
    width, rows = dq_ref.shape
    key_width = own_ref.shape[0] // 2
    wide = turned_ref.shape[0]
    cos, sin = cos_ref[...], sin_ref[...]
    turned_ref[:width, :] = dq_ref[...]
    summed = own_ref[...].astype(f32) + got_ref[...].astype(f32)
    for head in range(KEY_VALUE_HEADS):
        low = head * HEAD_SIZE
        first = summed[low : low + HALF]
        second = summed[low + HALF : low + HEAD_SIZE]
        base = width + low
        turned_ref[base : base + HALF, :] = (first * cos + second * sin).astype(bf16)
        turned_ref[base + HALF : base + HEAD_SIZE, :] = (second * cos - first * sin).astype(bf16)
    turned_ref[width + key_width : width + 2 * key_width, :] = summed[key_width:].astype(bf16)
    turned_ref[width + 2 * key_width :, :] = jnp.zeros((wide - width - 2 * key_width, rows), bf16)
    d_mixed = turned_ref[...].T
    dqkv_ref[...] = d_mixed
    d_normed = nt(d_mixed, w_ref[:, :wide])
    hidden = h_ref[...]
    factor = inverse_rms(hidden)
    unit = hidden * factor
    dgain_ref[...] = jnp.sum(d_normed * unit, axis=0, keepdims=True)
    scaled = d_normed * gain_ref[...]
    grad = dmid_ref[...] + factor * (
        scaled - unit * jnp.mean(scaled * unit, axis=-1, keepdims=True)
    )
    g_ref[...] = grad if g_ref.dtype == f32 else grad.T.astype(bf16)


def leave(hidden, d_middle, dq, own, got, gain, cos, sin, weights_a):
    rows, width = hidden.shape
    key_width = KEY_VALUE_HEADS * HEAD_SIZE
    wide = width + 2 * key_width + HEAD_SIZE
    return pl.pallas_call(
        leave_kernel,
        out_shape=(
            shape((rows, width), f32),
            shape((rows, wide), bf16),
            shape((1, width), f32),
        ),
        in_specs=[in_vmem()] * 9,
        out_specs=(in_vmem(),) * 3,
        scratch_shapes=[pltpu.VMEM((wide, rows), bf16)],
        compiler_params=params(),
        cost_estimate=cost(2 * rows * width * wide, width * wide * 2 + rows * width * 14),
        name="leave",
    )(hidden, d_middle, dq, own, got, gain, cos, sin, kept(weights_a))


def grad_parts(place_ref, right, keep_ref, send_ref, xt_ref):
    block, step = keep_ref.shape[2:]
    core, chip, quarter = place_ref[0], place_ref[1], place_ref[2]
    for part in range(4):
        columns = right(part * step, (part + 1) * step)
        for away in range(2):
            for out_ref, which in ((keep_ref, core), (send_ref, 1 - core)):
                start = pl.multiple_of((2 * (chip ^ away) + which) * block, 16)
                out_ref[away, part ^ quarter] = nn(
                    xt_ref[pl.ds(start, block), :], columns
                ).astype(bf16)


def feed_back_gate_kernel(*refs):
    (place_ref, g_ref, middle_ref, gating_ref, upward_ref, gain_ref, nf2_ref, nf_ref, dgu2_ref,
     a_ref, gu_hbm, dn_ref, dmid_ref, gm_ref, do_ref, dgain_ref, keep_ref, send_ref, keep2_ref,
     send2_ref, gb_ref, dgu_ref, sum_ref, xt_ref, gu_ref, gu_sems) = refs
    feed_back_kernel(
        g_ref, middle_ref, gating_ref, upward_ref, gain_ref, a_ref, gu_hbm, dn_ref, gb_ref, dgu_ref,
        dmid_ref, gm_ref, do_ref, dgain_ref, sum_ref, gu_ref, gu_sems,
    )

    rows = nf_ref.shape[0]
    ffn = gating_ref.shape[1]
    xt_ref[:, :rows] = nf2_ref[...].T
    xt_ref[:, rows:] = nf_ref[...].T
    for base, out_refs in ((0, (keep_ref, send_ref)), (ffn, (keep2_ref, send2_ref))):

        def right(low, high, base=base):
            return jnp.concatenate(
                [dgu2_ref[:, base + low : base + high], dgu_ref[:, base + low : base + high]], axis=0
            )

        grad_parts(place_ref, right, *out_refs, xt_ref)


def feed_back_gate(place, grad, middle, gating, upward, gain, nf2, nf, dgu2, weights):
    rows, width = grad.shape
    weights_a, weights_gu, weights_dn = weights
    ffn = weights_dn.shape[1]
    wo_wide = width + HEAD_SIZE
    return pl.pallas_call(
        feed_back_gate_kernel,
        out_shape=(
            shape((rows, width), f32),
            shape((rows, wo_wide), bf16),
            shape((width, rows), bf16),
            shape((1, width), f32),
        )
        + (shape((2, 4, width // 4, ffn // 4), bf16),) * 4,
        in_specs=[in_smem()] + [in_vmem()] * 9 + [anywhere(), in_vmem()],
        out_specs=(in_vmem(),) * 8,
        scratch_shapes=[
            pltpu.VMEM((rows, width), bf16),
            pltpu.VMEM((rows, 2 * ffn), bf16),
            pltpu.VMEM((rows, width), f32),
            pltpu.VMEM((width, 2 * rows), bf16),
            pltpu.VMEM((width, 2 * ffn), bf16),
            pltpu.SemaphoreType.DMA((4,)),
        ],
        compiler_params=params(FFN_MEBIBYTES),
        cost_estimate=cost(2 * rows * width * (8 * ffn), 3 * width * ffn * 2 + rows * ffn * 8),
        name="feed_back_gate",
    )(place, grad, middle, gating, upward, gain, nf2, nf, dgu2, kept(weights_a), in_hbm(weights_gu),
      kept(weights_dn))


def leave_mixed_kernel(*refs):
    (place_ref, h_ref, dmid_ref, dq_ref, own_ref, got_ref, gain_ref, cos_ref, sin_ref, n1_ref, n2_ref,
     d1_ref, a1_ref, a2_ref, m1_ref, m2_ref, attention_gain_ref, ffn_gain_ref, ffn_gain2_ref, w_ref,
     g_ref, keep_ref, send_ref, d2_ref, dgain_ref, turned_ref, nt_ref, at_ref, gains_ref) = refs
    leave_kernel(
        h_ref, dmid_ref, dq_ref, own_ref, got_ref, gain_ref, cos_ref, sin_ref, w_ref, g_ref, d2_ref,
        dgain_ref, turned_ref,
    )
    gains = (attention_gain_ref[...] + dgain_ref[...], ffn_gain_ref[...] + ffn_gain2_ref[...])
    attention_grad_kernel(
        place_ref, n1_ref, n2_ref, d1_ref, d2_ref, a1_ref, a2_ref, m1_ref, m2_ref, gains, keep_ref,
        send_ref, nt_ref, at_ref, gains_ref,
    )


def leave_mixed(
    place, hidden, d_middle, dq, own, got, gain, cos, sin, normed, dqkv2, att, gm, gain_grads, weights_a
):
    rows, width = hidden.shape
    key_width = KEY_VALUE_HEADS * HEAD_SIZE
    wide = width + 2 * key_width + HEAD_SIZE
    block = width // 4 + GAIN_ROWS
    columns = 2 * width + 2 * key_width
    return pl.pallas_call(
        leave_mixed_kernel,
        out_shape=(shape((width, rows), bf16),)
        + (shape((2, 4, block, columns // 4), bf16),) * 2,
        in_specs=[in_smem()] + [in_vmem()] * 19,
        out_specs=(in_vmem(),) * 3,
        scratch_shapes=[
            pltpu.VMEM((rows, wide), bf16),
            pltpu.VMEM((1, width), f32),
            pltpu.VMEM((wide, rows), bf16),
            pltpu.VMEM((width, 2 * rows), bf16),
            pltpu.VMEM((width, 2 * rows), bf16),
            pltpu.VMEM((GAIN_ROWS, columns), f32),
        ],
        compiler_params=params(),
        cost_estimate=cost(6 * rows * width * wide, width * wide * 2 + rows * width * 14),
        name="leave_mixed",
    )(place, hidden, d_middle, dq, own, got, gain, cos, sin, *normed, dqkv2, *att, *gm, *gain_grads,
      kept(weights_a))


def down_grad_kernel(place_ref, g2_ref, g_ref, inner2_ref, inner_ref, keep_ref, send_ref, gt_ref):
    rows = g2_ref.shape[0]
    height, step = keep_ref.shape[2:]
    gt_ref[:, :rows] = g2_ref[...].T
    gt_ref[:, rows:] = g_ref[...].astype(bf16).T
    core, chip, quarter = place_ref[0], place_ref[1], place_ref[2]
    for away in range(2):
        for out_ref, which in ((keep_ref, core), (send_ref, 1 - core)):
            columns = pl.ds(pl.multiple_of((2 * (chip ^ away) + which) * step, 128), step)
            right = jnp.concatenate([inner2_ref[:, columns], inner_ref[:, columns]], axis=0)
            for part in range(4):
                out_ref[away, part ^ quarter] = nn(
                    gt_ref[part * height : (part + 1) * height, :], right
                ).astype(bf16)


def down_grad_parts(place, g2, g, inner2, inner):
    rows, width = g.shape
    ffn = inner.shape[1]
    return pl.pallas_call(
        down_grad_kernel,
        out_shape=(shape((2, 4, width // 4, ffn // 4), bf16),) * 2,
        in_specs=[in_smem()] + [in_vmem()] * 4,
        out_specs=(in_vmem(),) * 2,
        scratch_shapes=[pltpu.VMEM((width, 2 * rows), bf16)],
        compiler_params=params(),
        cost_estimate=cost(4 * rows * width * ffn, width * ffn * 2),
        name="down_grad",
    )(place, g2, g, inner2, inner)


def attention_grad_kernel(
    place_ref, n1_ref, n2_ref, d1_ref, d2_ref, a1_ref, a2_ref, m1_ref, m2_ref, gains,
    keep_ref, send_ref, nt_ref, at_ref, gains_ref,
):
    rows = n1_ref.shape[0]
    block = n1_ref.shape[1] // 4
    wide = d1_ref.shape[1]
    edge = wide - 128
    step = keep_ref.shape[3]
    nt_ref[:, :rows] = n1_ref[...].T
    nt_ref[:, rows:] = n2_ref[...].T
    at_ref[:, :rows] = a1_ref[...].T
    at_ref[:, rows:] = a2_ref[...].T
    half = GAIN_ROWS // 2
    gains_ref[...] = jnp.zeros_like(gains_ref)
    for i, gain in enumerate(gains):
        gains_ref[i * half : (i + 1) * half, : gain.shape[1]] = jnp.broadcast_to(
            gain, (half, gain.shape[1])
        )
    core, chip, quarter = place_ref[0], place_ref[1], place_ref[2]
    d_mixed = jnp.concatenate([d1_ref[...], d2_ref[...]], axis=0)
    d_out = jnp.concatenate([m1_ref[...], m2_ref[...]], axis=0)
    for away in range(2):
        for out_ref, which in ((keep_ref, core), (send_ref, 1 - core)):
            member = 2 * (chip ^ away) + which
            start = pl.multiple_of(member * block, 16)
            normed = nt_ref[pl.ds(start, block), :]
            attended = at_ref[pl.ds(start, block), :]
            for part in range(4):
                low, high = part * step, (part + 1) * step
                pieces = []
                if low < edge:
                    pieces.append(nn(normed, d_mixed[:, low : min(high, edge)]))
                if low <= edge < high:
                    pieces.append(nn(normed, d_mixed[:, edge:]) + nn(attended, d_out[:, :128]))
                if high > wide:
                    base = wide - 128
                    pieces.append(nn(attended, d_out[:, max(low, wide) - base : high - base]))
                piece = pieces[0] if len(pieces) == 1 else jnp.concatenate(pieces, axis=1)
                out_ref[away, part ^ quarter, :block, :] = piece.astype(bf16)
                out_ref[away, part ^ quarter, block:, :] = gains_ref[:, low:high].astype(bf16)


def finish_kernel(place_ref, p0_ref, p1_ref, p2_ref, p3_ref, out_ref):
    part = pl.program_id(0)
    for i, ref in enumerate((p0_ref, p1_ref, p2_ref, p3_ref)):

        @pl.when(part == i)
        def _(ref=ref):
            out_ref[...] = ref[...].astype(f32)


def finish(place, pieces, by_rows):
    height, step = pieces[0].shape
    whole = pl.BlockSpec((height, step), lambda i, place: (0, 0))
    if by_rows:
        dims, index = (4 * height, step), lambda i, place: (i ^ place[2], 0)
    else:
        dims, index = (height, 4 * step), lambda i, place: (0, i ^ place[2])
    return pl.pallas_call(
        finish_kernel,
        grid_spec=pltpu.PrefetchScalarGridSpec(
            num_scalar_prefetch=1,
            grid=(4,),
            in_specs=[whole] * 4,
            out_specs=pl.BlockSpec((height, step), index),
        ),
        out_shape=shape(dims, f32),
        compiler_params=params(),
        cost_estimate=cost(0, 24 * height * step),
        name="finish",
    )(place, *pieces)


def finish_mixed_kernel(
    place_ref, p0_ref, p1_ref, p2_ref, p3_ref, query_ref, key_ref, value_ref, out_ref, gain_ref,
    mixed_ref,
):
    quarter = place_ref[2]
    block, width = query_ref.shape
    key_width = key_ref.shape[0]
    step = p0_ref.shape[1]
    for i, ref in enumerate((p0_ref, p1_ref, p2_ref, p3_ref)):
        start = pl.multiple_of((quarter ^ i) * step, 128)
        mixed_ref[:, pl.ds(start, step)] = ref[...].astype(f32)
    first_end = width + key_width
    second_end = first_end + key_width
    query_ref[...] = mixed_ref[:block, :width]
    key_ref[...] = mixed_ref[:block, width:first_end].T
    value_ref[...] = mixed_ref[:block, first_end:second_end].T
    out_ref[...] = mixed_ref[:block, second_end:]
    gain_ref[...] = mixed_ref[block:, : gain_ref.shape[1]]


def finish_mixed(place, pieces, width, key_width):
    height, step = pieces[0].shape
    block = height - GAIN_ROWS
    return pl.pallas_call(
        finish_mixed_kernel,
        out_shape=(
            shape((block, width), f32),
            shape((key_width, block), f32),
            shape((key_width, block), f32),
            shape((block, width), f32),
            shape((GAIN_ROWS, width + HEAD_SIZE), f32),
        ),
        in_specs=[in_smem()] + [in_vmem()] * 4,
        out_specs=(in_vmem(),) * 5,
        scratch_shapes=[pltpu.VMEM((height, 4 * step), f32)],
        compiler_params=params(),
        cost_estimate=cost(0, 24 * height * step),
        name="finish_mixed",
    )(place, *pieces)


def flip(value, axis_name, distance):
    size = lax.axis_size(axis_name)
    return lax.ppermute(value, axis_name, [(i, i ^ distance) for i in range(size)])


def pick(condition, when_true, when_false):
    return jnp.where(condition, when_true, when_false)


def order_by(bit, own, other):
    return (pick(bit == 1, other, own), pick(bit == 1, own, other))


def exchange_kv(block):
    beside = flip(block, "fsdp", 1)
    across = flip(block, "fsdp", 2)
    diagonal = flip(across, "fsdp", 1)
    return (block, beside, across, diagonal)


def fold_kv(keep, send):
    got = flip(send, "fsdp", 1)
    return total(keep[0], got[0]), total(keep[1], got[1])


def return_kv(keep, send):
    own, across = fold_kv(keep, send)
    return own, flip(across, "fsdp", 2)


def total(*terms):
    result = terms[0].astype(f32)
    for term in terms[1:]:
        result = result + term.astype(f32)
    return result.astype(bf16)


class Order:
    def __init__(self, *token):
        self.token = token

    def tie(self, *values):
        tied = lax.optimization_barrier(self.token + values)[len(self.token) :]
        return tied[0] if len(tied) == 1 else tied

    def done(self, value):
        self.token = (value,)
        return value

    def done_all(self, *values):
        self.token = values
        return values


class Reduction:
    def __init__(self, order, keep, send):
        self.order = order
        self.keep = keep
        self.core = flip(order.tie(send), "fsdp", 1)

    def chip(self):
        self.core = self.order.tie(self.core)
        high = total(self.keep[1, 2:], self.core[1, 2:])
        low = total(self.keep[1, :2], self.core[1, :2])
        high, low = self.order.done_all(high, low)
        self.high = flip(high, "fsdp", 2)
        self.low = flip(low, "fsdp", 2)

    def first(self, both=False):
        if both:
            self.high, self.low = self.order.tie(self.high, self.low)
        else:
            self.high = self.order.tie(self.high)
        out = total(self.keep[0, 2:], self.core[0, 2:], self.high)
        self.got = flip(self.order.done(out), "dp", 1)

    def rest(self):
        self.low = self.order.done(self.order.tie(self.low))

    def second(self):
        self.got, self.low = self.order.tie(self.got, self.low)
        self.terms = (self.keep[0, :2], self.core[0, :2], self.low, self.got)
        self.got = flip(self.order.done(total(*[term[1] for term in self.terms])), "dp", 2)

    def third(self):
        size = lax.axis_size("dp")
        own = total(*[term[0] for term in self.terms], self.order.tie(self.got))
        distance = 4
        while 2 * distance < size:
            own = total(own, flip(own, "dp", distance))
            distance *= 2
        self.own = self.order.done(own)
        self.got = flip(own, "dp", distance) if distance < size else jnp.zeros_like(own)

    def back(self):
        self.own = self.order.done(total(self.own, self.order.tie(self.got)))
        self.beside = flip(self.own, "dp", 2)
        self.pieces = [self.own, self.beside, flip(self.own, "dp", 1)]

    def back_again(self):
        self.beside = self.order.done(self.order.tie(self.beside))
        self.pieces.append(flip(self.beside, "dp", 1))

    def end(self):
        return self.order.tie(*self.pieces)


def rotation(token_positions):
    frequency = rope_base ** (-jnp.arange(HALF, dtype=f32) / HALF)
    angles = frequency[:, None] * token_positions.astype(f32)[None, :]
    return jnp.cos(angles), jnp.sin(angles)


def body(
    tokens,
    cotangent,
    sequence_ids,
    span_position,
    attention_norm,
    query_weight,
    key_matrix,
    value_matrix,
    output_weight,
    feedforward_norm,
    gate_weight,
    up_weight,
    down_weight,
):
    rows, width = tokens.shape
    key_width = key_matrix.shape[1]
    ffn = gate_weight.shape[1]
    itself = lax.axis_index("fsdp")
    outer = lax.axis_index("dp")
    quarter = 2 * (outer % 2) + (outer // 2) % 2
    place = jnp.stack([itself % 2, itself // 2, quarter]).astype(jnp.int32)

    outer = lax.axis_index("dp")
    bits = jnp.stack([outer % 2, (outer // 2) % 2, itself]).astype(jnp.int32)
    packed, *mine = pack(
        bits, query_weight, key_matrix.T, value_matrix.T, output_weight, gate_weight, up_weight
    )
    down_t = down_weight.T
    half = width // 2
    mine.append(pick(outer % 2 == 1, down_t[half:], down_t[:half]))
    gains = jnp.stack([attention_norm, feedforward_norm], axis=0)
    gains = [flip(gains, "fsdp", distance) if distance else gains for distance in range(4)]
    mine = Order(*gains).tie(*mine)
    far = [flip(piece, "fsdp", 2) for piece in mine]
    shards = (packed, gate_weight, up_weight, down_t)
    near = [flip(shard, "fsdp", 1) for shard in shards]
    sequence_ids, span_position = Order(*mine).tie(sequence_ids, span_position)
    places = jnp.arange(rows, dtype=jnp.int32) + span_position[itself] * rows
    cos, sin = rotation(places)
    others = itself ^ jnp.arange(4)
    visible = (
        (sequence_ids[others] == sequence_ids[itself])
        & (span_position[others] <= span_position[itself])
    ).astype(jnp.int32)

    beside = order_by(itself % 2, gains[0], gains[1])
    away = order_by(itself % 2, gains[2], gains[3])
    chip = itself // 2 == 1
    gains = jnp.concatenate(
        [pick(chip, a, n) for a, n in zip(away, beside)]
        + [pick(chip, n, a) for a, n in zip(away, beside)],
        axis=1,
    ).astype(f32)
    attention_gain, ffn_gain = gains[:1], gains[1:]
    order = Order(cos, sin, visible, attention_gain, ffn_gain)
    share = ((1, 0), (1, 0), (2, 1), (1, 0))

    def shared(i):
        got = order.done(order.tie(far[i]))
        return got, flip(got, "dp", share[i][0])

    def gathered(i, got, other):
        return [shards[i], near[i], got, other, flip(got, "fsdp", 1), flip(other, "fsdp", 1)]

    shared_a = shared(0)
    order.done_all(*order.tie(*shared_a))
    shared_gate = shared(1)
    sources_a = gathered(0, *shared_a)
    order.done_all(*order.tie(*near), *sources_a)
    tokens_t = order.tie(tokens.T)
    hidden, normed, q, kv, weights_a = enter_first(
        bits, tokens_t, attention_gain, cos, sin, shared_plan(0, 0, 0), tuple(sources_a)
    )
    order.done(kv)
    shared_up = shared(2)
    shared_gate = order.done_all(*order.tie(*shared_gate))
    kvs = exchange_kv(kv)
    shared_down = shared(3)
    order.done_all(*order.tie(*shared_up))
    sources_gu = gathered(1, *shared_gate) + gathered(2, *shared_up)
    sources_dn = gathered(3, *order.tie(*shared_down))
    plan_gu = shared_plan(0, 0, 0) + shared_plan(6, ffn, 1)
    plan_dn = shared_plan(0, None, 0)
    finished, att, att_t, lse, middle, nf, gating, upward, inner, weights_gu, weights_dn = forward_block(
        visible, bits, hidden, q, kvs, ffn_gain, weights_a, tuple(sources_gu), tuple(sources_dn),
        (plan_gu, plan_dn),
    )
    weights = (weights_a, weights_gu, weights_dn)
    saved = [(hidden, normed, q, kvs, att, att_t, lse, middle, nf, gating, upward, inner)]
    hidden = finished
    normed, q, kv = enter(hidden, attention_gain, cos, sin, weights_a)
    kvs = exchange_kv(kv)
    activations, att, att_t, lse, middle, nf, gating, upward, inner = forward_block(
        visible, bits, hidden, q, kvs, ffn_gain, weights_a, (weights_gu,), (weights_dn,)
    )
    saved.append((hidden, normed, q, kvs, att, att_t, lse, middle, nf, gating, upward, inner))

    hidden, normed2, q, kvs, att2, att_t, lse, middle, nf2, gating, upward, inner2 = saved[1]
    gb2, dgu2, d_middle, gm2, d_out, ffn_gain_grad2 = feed_back(
        cotangent.T, middle, gating, upward, ffn_gain, weights
    )
    dq, *dkvs = attend_back(visible, q, d_out, att_t, lse, cos, sin, kvs)
    own, got = return_kv(*dkvs)
    grad, dqkv2, attention_gain_grad2 = leave(
        hidden, d_middle, dq, own, got, attention_gain, cos, sin, weights_a
    )

    hidden, normed, q, kvs, att, att_t, lse, middle, nf, gating, upward, inner = saved[0]
    order = Order(grad)
    down = Reduction(order, *down_grad_parts(place, gb2, grad, inner2, inner))
    down.chip()
    d_middle, gm, d_out, ffn_gain_grad, *rest = feed_back_gate(
        place, order.tie(grad), middle, gating, upward, ffn_gain, nf2, nf, dgu2, weights
    )
    order.done(d_middle)
    down.first(both=True)
    gate = Reduction(order, *rest[:2])
    gate.chip()
    up = Reduction(order, *rest[2:])
    dq, *dkvs = attend_back(visible, order.tie(q), d_out, att_t, lse, cos, sin, kvs)
    order.done(dq)
    gate.first()
    down.second()
    own, across = fold_kv(*order.tie(*dkvs))
    order.done(across)
    gate.rest()
    down.third()
    across = order.tie(across)
    got = order.done(order.tie(flip(across, "fsdp", 2)))
    gate.second()
    up.chip()
    d_middle = order.tie(d_middle)
    grad, *mixed = leave_mixed(
        place,
        hidden,
        d_middle,
        dq,
        own,
        got,
        attention_gain,
        cos,
        sin,
        (normed2, normed),
        dqkv2,
        (att2, att),
        (gm2, gm),
        (attention_gain_grad2, ffn_gain_grad2, ffn_gain_grad),
        weights_a,
    )
    order.done(grad)
    up.first()
    down.back()
    gate.third()
    mixed = Reduction(order, *mixed)
    mixed.chip()
    up.second()
    gate.back()
    mixed.first()
    up.third()
    down.back_again()
    mixed.rest()
    mixed.second()
    gate.back_again()
    up.back()
    down_grad = order.done(finish(place, down.end(), True))
    mixed.third()
    up.back_again()
    gate_grad = order.done(finish(place, gate.end(), False))
    mixed.back()
    up_grad = order.done(finish(place, up.end(), False))
    mixed.back_again()
    query_grad, key_grad, value_grad, output_grad, gain_grads = finish_mixed(
        place, mixed.end(), width, key_width
    )
    shard_rows = attention_norm.shape[0]
    gain_grads = lax.dynamic_slice_in_dim(gain_grads, itself * shard_rows, shard_rows, axis=1)
    return (
        activations.T,
        grad.T,
        gain_grads[0],
        query_grad,
        key_grad.T,
        value_grad.T,
        output_grad,
        gain_grads[GAIN_ROWS // 2],
        gate_grad,
        up_grad,
        down_grad.T,
    )


def solution(mesh):
    return jax.shard_map(
        body,
        mesh=mesh,
        in_specs=(
            P(("dp", "fsdp"), None),
            P(("dp", "fsdp"), None),
            P("dp"),
            P("dp"),
            P("fsdp"),
            P("fsdp", None),
            P("fsdp", None),
            P("fsdp", None),
            P("fsdp", None),
            P("fsdp"),
            P("fsdp", None),
            P("fsdp", None),
            P("fsdp", None),
        ),
        out_specs=(
            P(("dp", "fsdp"), None),
            P(("dp", "fsdp"), None),
            P("fsdp"),
            P("fsdp", None),
            P("fsdp", None),
            P("fsdp", None),
            P("fsdp", None),
            P("fsdp"),
            P("fsdp", None),
            P("fsdp", None),
            P("fsdp", None),
        ),
        check_vma=False,
    )
```

```python
import functools

import jax
import jax.numpy as jnp
from jax import lax
from jax.experimental import pallas as pl
from jax.experimental.pallas import tpu as pltpu
from jax.sharding import PartitionSpec as P

QUERY_HEADS = 15
KEY_VALUE_HEADS = 5
HEAD_SIZE = 64
SHARING = QUERY_HEADS // KEY_VALUE_HEADS
HALF = HEAD_SIZE // 2

epsilon = 1e-05
rope_base = 10000.0
masked = -1e30
score_scale = HEAD_SIZE ** (-0.5)

bf16 = jnp.bfloat16
f32 = jnp.float32
GAIN_ROWS = 16
FFN_MEBIBYTES = 26


def nn(left, right):
    return jnp.dot(left, right, preferred_element_type=f32)


def nt(left, right):
    return lax.dot_general(left, right, (((1,), (1,)), ((), ())), preferred_element_type=f32)


def in_vmem():
    return pl.BlockSpec(memory_space=pltpu.VMEM)


def in_smem():
    return pl.BlockSpec(memory_space=pltpu.SMEM)


def anywhere():
    return pl.BlockSpec(memory_space=pl.ANY)


def params(mebibytes=14):
    return pltpu.CompilerParams(vmem_limit_bytes=mebibytes * 1024 * 1024)


def shape(dims, dtype):
    return jax.ShapeDtypeStruct(dims, dtype)


def kept(array):
    return pltpu.with_memory_space_constraint(array, pltpu.VMEM)


def in_hbm(array):
    return pltpu.with_memory_space_constraint(array, pltpu.HBM)


def cost(flops, bytes_accessed):
    return pl.CostEstimate(flops=int(flops), bytes_accessed=int(bytes_accessed), transcendentals=0)


def inverse_rms(hidden):
    return lax.rsqrt(jnp.mean(hidden * hidden, axis=-1, keepdims=True) + epsilon)


def pack_kernel(
    bits_ref, query_hbm, key_hbm, value_hbm, out_hbm, gate_hbm, up_hbm, packed_hbm, mine_hbm,
    mine_gate_hbm, mine_up_hbm, query_ref, key_ref, value_ref, out_ref, gate_ref, up_ref, packed_ref,
    mine_ref, sems,
):
    half = gate_ref.shape[1]
    loads = [
        pltpu.make_async_copy(source, target, sems.at[i])
        for i, (source, target) in enumerate(
            (
                (query_hbm, query_ref),
                (key_hbm, key_ref),
                (value_hbm, value_ref),
                (out_hbm, out_ref),
                (gate_hbm.at[:, pl.ds(pl.multiple_of(bits_ref[0] * half, 128), half)], gate_ref),
                (up_hbm.at[:, pl.ds(pl.multiple_of(bits_ref[1] * half, 128), half)], up_ref),
            )
        )
    ]
    for load in loads:
        load.start()
    for load in loads[:4]:
        load.wait()
    packed_ref[...] = jnp.concatenate(
        [
            query_ref[...].astype(f32),
            key_ref[...].astype(f32).T,
            value_ref[...].astype(f32).T,
            out_ref[...].astype(f32),
        ],
        axis=1,
    ).astype(bf16)
    wide = mine_ref.shape[1]
    mine_ref[...] = packed_ref[:, pl.ds(pl.multiple_of(bits_ref[0] * wide, 128), wide)]
    for load in loads[4:]:
        load.wait()
    stores = [
        pltpu.make_async_copy(source, target, sems.at[i])
        for i, (source, target) in enumerate(
            (
                (mine_ref, mine_hbm),
                (gate_ref, mine_gate_hbm),
                (up_ref, mine_up_hbm),
                (packed_ref, packed_hbm),
            )
        )
    ]
    for store in stores:
        store.start()
    for store in stores:
        store.wait()


def pack(bits, query, key_t, value_t, out, gate, up):
    rows, width = query.shape
    columns = 2 * width + 2 * key_t.shape[0]
    ffn = gate.shape[1]
    return pl.pallas_call(
        pack_kernel,
        out_shape=(
            pltpu.HBM((rows, columns), bf16),
            pltpu.HBM((rows, columns // 2), bf16),
            pltpu.HBM((rows, ffn // 2), bf16),
            pltpu.HBM((rows, ffn // 2), bf16),
        ),
        in_specs=[in_smem()] + [anywhere()] * 6,
        out_specs=(anywhere(),) * 4,
        scratch_shapes=[
            pltpu.VMEM((rows, width), bf16),
            pltpu.VMEM(key_t.shape, bf16),
            pltpu.VMEM(value_t.shape, bf16),
            pltpu.VMEM((rows, width), bf16),
            pltpu.VMEM((rows, ffn // 2), bf16),
            pltpu.VMEM((rows, ffn // 2), bf16),
            pltpu.VMEM((rows, columns), bf16),
            pltpu.VMEM((rows, columns // 2), bf16),
            pltpu.SemaphoreType.DMA((6,)),
        ],
        compiler_params=params(),
        cost_estimate=cost(0, 8 * rows * columns),
        name="pack",
    )(bits, *[in_hbm(part) for part in (query, key_t, value_t, out, gate, up)])


def piece_copies(plan, bits_ref, sources, target_ref, sems):
    me = bits_ref[2]
    copies = []
    for i, (which, member, column, part, bit) in enumerate(plan):
        source = sources[which]
        height, width = source.shape
        if column is None:
            turned = pl.ds(pl.multiple_of((me ^ member) * width, 128), width)
            if part is None:
                rows = pl.ds(0, height)
            else:
                rows = pl.ds(pl.multiple_of((bits_ref[bit] ^ part) * height, 16), height)
            target = target_ref.at[rows, turned]
        else:
            rows = pl.ds(pl.multiple_of((me ^ member) * height, 16), height)
            if part is None:
                columns = pl.ds(column, width)
            else:
                columns = pl.ds(
                    pl.multiple_of(column + (bits_ref[bit] ^ part) * width, 128), width
                )
            target = target_ref.at[rows, columns]
        copies.append(pltpu.make_async_copy(source, target, sems.at[i]))
    return copies


def shared_plan(first, column, bit):
    return (
        (first, 0, column, None, bit),
        (first + 1, 1, column, None, bit),
        (first + 2, 2, column, 0, bit),
        (first + 3, 2, column, 1, bit),
        (first + 4, 3, column, 0, bit),
        (first + 5, 3, column, 1, bit),
    )


def enter_body(hidden, gain_ref, cos_ref, sin_ref, ready, normed_ref, q_ref, kv_ref, w_ref):
    width = hidden.shape[1]
    key_width = kv_ref.shape[0] // 2
    mixed_width = width + key_width
    wide = width + 2 * key_width + HEAD_SIZE
    normed = (hidden * inverse_rms(hidden) * gain_ref[...]).astype(bf16)
    normed_ref[...] = normed
    cos, sin = cos_ref[...], sin_ref[...]
    ready()
    mixed = nn(normed, w_ref[:, :mixed_width]).T
    for head in range(QUERY_HEADS + KEY_VALUE_HEADS):
        low = head * HEAD_SIZE
        first = mixed[low : low + HALF]
        second = mixed[low + HALF : low + HEAD_SIZE]
        top = first * cos - second * sin
        bottom = second * cos + first * sin
        if head < QUERY_HEADS:
            q_ref[low : low + HALF, :] = (top * score_scale).astype(bf16)
            q_ref[low + HALF : low + HEAD_SIZE, :] = (bottom * score_scale).astype(bf16)
        else:
            low = low - width
            kv_ref[low : low + HALF, :] = top.astype(bf16)
            kv_ref[low + HALF : low + HEAD_SIZE, :] = bottom.astype(bf16)
    values = nn(normed, w_ref[:, mixed_width:wide]).T
    kv_ref[key_width:, :] = values[:key_width].astype(bf16)


def enter_first_kernel(plan, count, index_ref, h_ref, gain_ref, cos_ref, sin_ref, *refs):
    sources = refs[:count]
    hidden_ref, normed_ref, q_ref, kv_ref, w_ref, sems = refs[count:]
    copies = piece_copies(plan, index_ref, sources, w_ref, sems)
    for copy in copies:
        copy.start()
    hidden = h_ref[...].astype(f32).T
    hidden_ref[...] = hidden

    def ready():
        for copy in copies:
            copy.wait()

    enter_body(hidden, gain_ref, cos_ref, sin_ref, ready, normed_ref, q_ref, kv_ref, w_ref)


def enter_first(index, hidden_t, gain, cos, sin, plan, sources):
    width, rows = hidden_t.shape
    key_width = KEY_VALUE_HEADS * HEAD_SIZE
    columns = 2 * (width + key_width)
    return pl.pallas_call(
        functools.partial(enter_first_kernel, plan, len(sources)),
        out_shape=(
            shape((rows, width), f32),
            shape((rows, width), bf16),
            shape((width, rows), bf16),
            shape((2 * key_width, rows), bf16),
            pltpu.VMEM((width, columns), bf16),
        ),
        in_specs=[in_smem()] + [in_vmem()] * 4 + [anywhere()] * len(sources),
        out_specs=(in_vmem(),) * 5,
        scratch_shapes=[pltpu.SemaphoreType.DMA((len(plan),))],
        compiler_params=params(),
        cost_estimate=cost(4 * rows * width * width, width * columns * 4),
        name="enter_first",
    )(index, hidden_t, gain, cos, sin, *sources)


def enter_kernel(h_ref, gain_ref, cos_ref, sin_ref, w_ref, normed_ref, q_ref, kv_ref):
    enter_body(
        h_ref[...], gain_ref, cos_ref, sin_ref, lambda: None, normed_ref, q_ref, kv_ref, w_ref
    )


def enter(hidden, gain, cos, sin, weights_a):
    rows, width = hidden.shape
    key_width = KEY_VALUE_HEADS * HEAD_SIZE
    wide = width + 2 * key_width + HEAD_SIZE
    return pl.pallas_call(
        enter_kernel,
        out_shape=(
            shape((rows, width), bf16),
            shape((width, rows), bf16),
            shape((2 * key_width, rows), bf16),
        ),
        in_specs=[in_vmem()] * 5,
        out_specs=(in_vmem(),) * 3,
        compiler_params=params(),
        cost_estimate=cost(2 * rows * width * wide, width * wide * 2 + rows * width * 10),
        name="enter",
    )(hidden, gain, cos, sin, kept(weights_a))


def out_weight(a_ref):
    return a_ref[:, a_ref.shape[1] - a_ref.shape[0] - HEAD_SIZE :]


def stacked_heads(ref, group):
    parts = []
    for j in range(SHARING):
        low = (group * SHARING + j) * HEAD_SIZE
        parts.append(ref[low : low + HEAD_SIZE, :])
    return jnp.concatenate(parts, axis=1)


def key_block(ref, group):
    return ref[group * HEAD_SIZE : (group + 1) * HEAD_SIZE, :]


def value_block(ref, group):
    key_width = KEY_VALUE_HEADS * HEAD_SIZE
    return ref[key_width + group * HEAD_SIZE : key_width + (group + 1) * HEAD_SIZE, :]


def causal(rows):
    keys = lax.broadcasted_iota(jnp.int32, (rows, SHARING * rows), 0)
    queries = lax.broadcasted_iota(jnp.int32, (rows, SHARING * rows), 1) % rows
    return keys <= queries


def whole_copies(source_ref, target_ref, sems):
    parts = 4
    height = source_ref.shape[0] // parts
    return [
        pltpu.make_async_copy(
            source_ref.at[pl.ds(i * height, height), :],
            target_ref.at[pl.ds(i * height, height), :],
            sems.at[i],
        )
        for i in range(parts)
    ]


def forward_kernel(plans, counts, *refs):
    (visible_ref, bits_ref, h_ref, q_ref, kv0_ref, kv1_ref, kv2_ref, kv3_ref, gain_ref, a_ref) = refs[:10]
    gu_sources = refs[10 : 10 + counts[0]]
    dn_sources = refs[10 + counts[0] : 10 + counts[0] + counts[1]]
    refs = refs[10 + counts[0] + counts[1] :]
    (out_ref, att_ref, att_t_ref, lse_ref, middle_ref, nf_ref, gating_ref, upward_ref, inner_ref) = refs[:9]
    refs = refs[9:]
    gu_ref, gu_sems, dn_sems = refs[-3:]
    if plans is not None:
        gu_hbm, dn_ref = refs[:2]
        refs = refs[2:]
        gu_loads = piece_copies(plans[0], bits_ref, gu_sources, gu_ref, gu_sems)
        dn_loads = piece_copies(plans[1], bits_ref, dn_sources, dn_ref, dn_sems)
    else:
        (dn_ref,) = dn_sources
        gu_loads, dn_loads = whole_copies(gu_sources[0], gu_ref, gu_sems), []
    acc_ref, m_ref, l_ref, kvs_ref = refs[:4]
    rows, width = h_ref.shape
    ffn = inner_ref.shape[1]
    for load in gu_loads + dn_loads:
        load.start()

    allowed = causal(rows)
    for group in range(KEY_VALUE_HEADS):
        scores = nn(key_block(kv0_ref, group).T, stacked_heads(q_ref, group))
        scores = jnp.where(allowed, scores, masked)
        peak = jnp.max(scores, axis=0, keepdims=True)
        raised = jnp.exp(scores - peak)
        m_ref[group : group + 1, :] = peak
        l_ref[group : group + 1, :] = jnp.sum(raised, axis=0, keepdims=True)
        acc_ref[group] = nn(value_block(kv0_ref, group), raised.astype(bf16))
    for i, kv_ref in enumerate((kv1_ref, kv2_ref, kv3_ref)):
        kvs_ref[i] = kv_ref[...]

    @pl.loop(0, 3)
    def _(member):
        kv_ref = kvs_ref.at[member]

        @pl.when(visible_ref[member + 1] == 1)
        def _():
            for group in range(KEY_VALUE_HEADS):
                scores = nn(key_block(kv_ref, group).T, stacked_heads(q_ref, group))
                old = m_ref[group : group + 1, :]
                peak = jnp.maximum(old, jnp.max(scores, axis=0, keepdims=True))
                raised = jnp.exp(scores - peak)
                fade = jnp.exp(old - peak)
                m_ref[group : group + 1, :] = peak
                l_ref[group : group + 1, :] = l_ref[group : group + 1, :] * fade + jnp.sum(
                    raised, axis=0, keepdims=True
                )
                acc_ref[group] = acc_ref[group] * fade + nn(
                    value_block(kv_ref, group), raised.astype(bf16)
                )

    total = l_ref[...]
    lse_ref[...] = m_ref[...] + jnp.log(total)
    for group in range(KEY_VALUE_HEADS):
        mean = acc_ref[group] / total[group : group + 1, :]
        for j in range(SHARING):
            low = (group * SHARING + j) * HEAD_SIZE
            att_t_ref[low : low + HEAD_SIZE, :] = mean[:, j * rows : (j + 1) * rows].astype(bf16)
    attended = att_t_ref[...].T
    att_ref[...] = attended
    middle = h_ref[...] + nn(attended, out_weight(a_ref))[:, HEAD_SIZE:]
    middle_ref[...] = middle
    normed = (middle * inverse_rms(middle) * gain_ref[...]).astype(bf16)
    nf_ref[...] = normed
    for load in gu_loads:
        load.wait()
    gu_stores = whole_copies(gu_ref, gu_hbm, gu_sems) if plans is not None else []
    for store in gu_stores:
        store.start()
    step = 512
    for low in range(0, ffn, step):
        gating = nn(normed, gu_ref[:, low : low + step])
        upward = nn(normed, gu_ref[:, ffn + low : ffn + low + step])
        gating_ref[:, low : low + step] = gating.astype(bf16)
        upward_ref[:, low : low + step] = upward.astype(bf16)
        inner_ref[:, low : low + step] = (gating * jax.nn.sigmoid(gating) * upward).astype(bf16)
    for load in dn_loads:
        load.wait()
    finished = middle + nt(inner_ref[...], dn_ref[...])
    out_ref[...] = finished if plans is not None else finished.T.astype(bf16)
    for store in gu_stores:
        store.wait()


def forward_block(visible, index, hidden, q, kvs, gain, weights_a, gu, dn, plans=None):
    rows, width = hidden.shape
    ffn = gu[0].shape[1] if plans is not None else gu[0].shape[1] // 2
    lanes = SHARING * rows
    counts = (len(gu), len(dn))
    first = plans is not None
    whole = (pltpu.HBM((width, 2 * ffn), bf16), pltpu.VMEM((width, ffn), bf16))
    return pl.pallas_call(
        functools.partial(forward_kernel, plans, counts),
        out_shape=(
            shape((rows, width), f32) if first else shape((width, rows), bf16),
            shape((rows, width), bf16),
            shape((width, rows), bf16),
            shape((KEY_VALUE_HEADS, lanes), f32),
            shape((rows, width), f32),
            shape((rows, width), bf16),
            shape((rows, ffn), bf16),
            shape((rows, ffn), bf16),
            shape((rows, ffn), bf16),
        )
        + (whole if first else ()),
        in_specs=[in_smem()] * 2
        + [in_vmem()] * 8
        + [anywhere()] * counts[0]
        + [anywhere() if first else in_vmem()] * counts[1],
        out_specs=(in_vmem(),) * 9 + ((anywhere(), in_vmem()) if first else ()),
        scratch_shapes=[
            pltpu.VMEM((KEY_VALUE_HEADS, HEAD_SIZE, lanes), f32),
            pltpu.VMEM((KEY_VALUE_HEADS, lanes), f32),
            pltpu.VMEM((KEY_VALUE_HEADS, lanes), f32),
            pltpu.VMEM((3, *kvs[0].shape), bf16),
            pltpu.VMEM((width, 2 * ffn), bf16),
            pltpu.SemaphoreType.DMA((len(plans[0]) if first else 4,)),
            pltpu.SemaphoreType.DMA((len(plans[1]) if first else 1,)),
        ],
        compiler_params=params(FFN_MEBIBYTES),
        cost_estimate=cost(2 * rows * width * (4 * ffn), 3 * width * ffn * 2 + rows * ffn * 8),
        name="forward_first" if first else "forward_last",
    )(
        visible, index, hidden, q, *kvs, gain, kept(weights_a),
        *([*gu, *dn] if first else [in_hbm(gu[0]), kept(dn[0])]),
    )


def feed_back_kernel(
    g_ref,
    middle_ref,
    gating_ref,
    upward_ref,
    gain_ref,
    a_ref,
    gu_hbm,
    dn_ref,
    gb_ref,
    dgu_ref,
    dmid_ref,
    gm_ref,
    do_ref,
    dgain_ref,
    sum_ref,
    gu_ref,
    gu_sems,
):
    rows, width = middle_ref.shape
    ffn = gating_ref.shape[1]
    loads = whole_copies(gu_hbm, gu_ref, gu_sems)
    for load in loads:
        load.start()
    grad = g_ref[...] if g_ref.shape[0] == rows else g_ref[...].astype(f32).T
    short = grad.astype(bf16)
    gb_ref[...] = short
    step = 512
    for low in range(0, ffn, step):
        part = slice(low, low + step)
        behind = slice(ffn + low, ffn + low + step)
        d_inner = nn(short, dn_ref[:, part])
        gating = gating_ref[:, part].astype(f32)
        upward = upward_ref[:, part].astype(f32)
        gate = jax.nn.sigmoid(gating)
        d_gating = (d_inner * upward * (gate * (1.0 + gating * (1.0 - gate)))).astype(bf16)
        d_upward = (d_inner * (gating * gate)).astype(bf16)
        dgu_ref[:, part] = d_gating
        dgu_ref[:, behind] = d_upward
    for load in loads:
        load.wait()
    sum_ref[...] = nt(dgu_ref[...], gu_ref[...])
    d_normed = sum_ref[...]
    middle = middle_ref[...]
    factor = inverse_rms(middle)
    unit = middle * factor
    dgain_ref[...] = jnp.sum(d_normed * unit, axis=0, keepdims=True)
    scaled = d_normed * gain_ref[...]
    d_middle = grad + factor * (scaled - unit * jnp.mean(scaled * unit, axis=-1, keepdims=True))
    dmid_ref[...] = d_middle
    padded = jnp.concatenate(
        [jnp.zeros((rows, HEAD_SIZE), f32), d_middle], axis=1
    ).astype(bf16)
    gm_ref[...] = padded
    do_ref[...] = nt(padded, out_weight(a_ref)).T.astype(bf16)


def feed_back(grad, middle, gating, upward, gain, weights):
    rows, width = middle.shape
    weights_a, weights_gu, weights_dn = weights
    ffn = weights_dn.shape[1]
    wo_wide = width + HEAD_SIZE
    return pl.pallas_call(
        feed_back_kernel,
        out_shape=(
            shape((rows, width), bf16),
            shape((rows, 2 * ffn), bf16),
            shape((rows, width), f32),
            shape((rows, wo_wide), bf16),
            shape((width, rows), bf16),
            shape((1, width), f32),
        ),
        in_specs=[in_vmem()] * 6 + [anywhere(), in_vmem()],
        out_specs=(in_vmem(),) * 6,
        scratch_shapes=[
            pltpu.VMEM((rows, width), f32),
            pltpu.VMEM((width, 2 * ffn), bf16),
            pltpu.SemaphoreType.DMA((4,)),
        ],
        compiler_params=params(FFN_MEBIBYTES),
        cost_estimate=cost(2 * rows * width * (4 * ffn), 3 * width * ffn * 2 + rows * ffn * 8),
        name="feed_back",
    )(grad, middle, gating, upward, gain, kept(weights_a), in_hbm(weights_gu), kept(weights_dn))


def attend_back_kernel(
    visible_ref,
    q_ref,
    do_ref,
    att_ref,
    lse_ref,
    cos_ref,
    sin_ref,
    kv0_ref,
    kv1_ref,
    kv2_ref,
    kv3_ref,
    dq_ref,
    keep_ref,
    send_ref,
    acc_ref,
    row_ref,
    kvs_ref,
    dkvs_ref,
):
    rows = q_ref.shape[1]
    key_width = KEY_VALUE_HEADS * HEAD_SIZE
    allowed = causal(rows)
    for group in range(KEY_VALUE_HEADS):
        row_ref[group : group + 1, :] = jnp.sum(
            stacked_heads(do_ref, group).astype(f32) * stacked_heads(att_ref, group).astype(f32),
            axis=0,
            keepdims=True,
        )

    def one(group, kv_ref, dkv_ref, own):
        queries = stacked_heads(q_ref, group)
        d_out = stacked_heads(do_ref, group)
        keys = key_block(kv_ref, group)
        scores = nn(keys.T, queries)
        if own:
            scores = jnp.where(allowed, scores, masked)
        probs = jnp.exp(scores - lse_ref[group : group + 1, :])
        d_probs = nn(value_block(kv_ref, group).T, d_out)
        d_scores = (probs * (d_probs - row_ref[group : group + 1, :])).astype(bf16)
        dkv_ref[group * HEAD_SIZE : (group + 1) * HEAD_SIZE, :] = nt(queries, d_scores).astype(bf16)
        dkv_ref[key_width + group * HEAD_SIZE : key_width + (group + 1) * HEAD_SIZE, :] = nt(
            d_out, probs.astype(bf16)
        ).astype(bf16)
        moved = nn(keys, d_scores)
        if own:
            acc_ref[group] = moved
        else:
            acc_ref[group] += moved

    for group in range(KEY_VALUE_HEADS):
        one(group, kv0_ref, keep_ref.at[0], True)
    for i, kv_ref in enumerate((kv1_ref, kv2_ref, kv3_ref)):
        kvs_ref[i] = kv_ref[...]

    @pl.loop(0, 3)
    def _(member):
        kv_ref, dkv_ref = kvs_ref.at[member], dkvs_ref.at[member]

        @pl.when(visible_ref[member + 1] == 1)
        def _():
            for group in range(KEY_VALUE_HEADS):
                one(group, kv_ref, dkv_ref, False)

        @pl.when(visible_ref[member + 1] == 0)
        def _():
            dkv_ref[...] = jnp.zeros(dkv_ref.shape, bf16)

    send_ref[0] = dkvs_ref[0]
    keep_ref[1] = dkvs_ref[1]
    send_ref[1] = dkvs_ref[2]
    cos, sin = cos_ref[...], sin_ref[...]
    for group in range(KEY_VALUE_HEADS):
        for j in range(SHARING):
            low = (group * SHARING + j) * HEAD_SIZE
            lanes = slice(j * rows, (j + 1) * rows)
            first = acc_ref[group, :HALF, lanes] * score_scale
            second = acc_ref[group, HALF:, lanes] * score_scale
            dq_ref[low : low + HALF, :] = (first * cos + second * sin).astype(bf16)
            dq_ref[low + HALF : low + HEAD_SIZE, :] = (second * cos - first * sin).astype(bf16)


def attend_back(visible, q, d_out, att_t, lse, cos, sin, kvs):
    width, rows = q.shape
    key_rows = kvs[0].shape[0]
    lanes = SHARING * rows
    return pl.pallas_call(
        attend_back_kernel,
        out_shape=(shape((width, rows), bf16),) + (shape((2, key_rows, rows), bf16),) * 2,
        in_specs=[in_smem()] + [in_vmem()] * 10,
        out_specs=(in_vmem(),) * 3,
        scratch_shapes=[
            pltpu.VMEM((KEY_VALUE_HEADS, HEAD_SIZE, lanes), f32),
            pltpu.VMEM((KEY_VALUE_HEADS, lanes), f32),
            pltpu.VMEM((3, key_rows, rows), bf16),
            pltpu.VMEM((3, key_rows, rows), bf16),
        ],
        compiler_params=params(),
        cost_estimate=cost(2 * rows * width * 4 * rows * 10, 10 * width * rows * 2),
        name="attend_back",
    )(visible, q, d_out, att_t, lse, cos, sin, *kvs)


def leave_kernel(
    h_ref,
    dmid_ref,
    dq_ref,
    own_ref,
    got_ref,
    gain_ref,
    cos_ref,
    sin_ref,
    w_ref,
    g_ref,
    dqkv_ref,
    dgain_ref,
    turned_ref,
):
    width, rows = dq_ref.shape
    key_width = own_ref.shape[0] // 2
    wide = turned_ref.shape[0]
    cos, sin = cos_ref[...], sin_ref[...]
    turned_ref[:width, :] = dq_ref[...]
    summed = own_ref[...].astype(f32) + got_ref[...].astype(f32)
    for head in range(KEY_VALUE_HEADS):
        low = head * HEAD_SIZE
        first = summed[low : low + HALF]
        second = summed[low + HALF : low + HEAD_SIZE]
        base = width + low
        turned_ref[base : base + HALF, :] = (first * cos + second * sin).astype(bf16)
        turned_ref[base + HALF : base + HEAD_SIZE, :] = (second * cos - first * sin).astype(bf16)
    turned_ref[width + key_width : width + 2 * key_width, :] = summed[key_width:].astype(bf16)
    turned_ref[width + 2 * key_width :, :] = jnp.zeros((wide - width - 2 * key_width, rows), bf16)
    d_mixed = turned_ref[...].T
    dqkv_ref[...] = d_mixed
    d_normed = nt(d_mixed, w_ref[:, :wide])
    hidden = h_ref[...]
    factor = inverse_rms(hidden)
    unit = hidden * factor
    dgain_ref[...] = jnp.sum(d_normed * unit, axis=0, keepdims=True)
    scaled = d_normed * gain_ref[...]
    grad = dmid_ref[...] + factor * (
        scaled - unit * jnp.mean(scaled * unit, axis=-1, keepdims=True)
    )
    g_ref[...] = grad if g_ref.dtype == f32 else grad.T.astype(bf16)


def leave(hidden, d_middle, dq, own, got, gain, cos, sin, weights_a):
    rows, width = hidden.shape
    key_width = KEY_VALUE_HEADS * HEAD_SIZE
    wide = width + 2 * key_width + HEAD_SIZE
    return pl.pallas_call(
        leave_kernel,
        out_shape=(
            shape((rows, width), f32),
            shape((rows, wide), bf16),
            shape((1, width), f32),
        ),
        in_specs=[in_vmem()] * 9,
        out_specs=(in_vmem(),) * 3,
        scratch_shapes=[pltpu.VMEM((wide, rows), bf16)],
        compiler_params=params(),
        cost_estimate=cost(2 * rows * width * wide, width * wide * 2 + rows * width * 14),
        name="leave",
    )(hidden, d_middle, dq, own, got, gain, cos, sin, kept(weights_a))


def grad_parts(place_ref, right, keep_ref, send_ref, xt_ref):
    block, step = keep_ref.shape[2:]
    core, chip, quarter = place_ref[0], place_ref[1], place_ref[2]
    for part in range(4):
        columns = right(part * step, (part + 1) * step)
        for away in range(2):
            for out_ref, which in ((keep_ref, core), (send_ref, 1 - core)):
                start = pl.multiple_of((2 * (chip ^ away) + which) * block, 16)
                out_ref[away, part ^ quarter] = nn(
                    xt_ref[pl.ds(start, block), :], columns
                ).astype(bf16)


def feed_back_gate_kernel(*refs):
    (place_ref, g_ref, middle_ref, gating_ref, upward_ref, gain_ref, nf2_ref, nf_ref, dgu2_ref,
     a_ref, gu_hbm, dn_ref, dmid_ref, gm_ref, do_ref, dgain_ref, keep_ref, send_ref, keep2_ref,
     send2_ref, gb_ref, dgu_ref, sum_ref, xt_ref, gu_ref, gu_sems) = refs
    feed_back_kernel(
        g_ref, middle_ref, gating_ref, upward_ref, gain_ref, a_ref, gu_hbm, dn_ref, gb_ref, dgu_ref,
        dmid_ref, gm_ref, do_ref, dgain_ref, sum_ref, gu_ref, gu_sems,
    )

    rows = nf_ref.shape[0]
    ffn = gating_ref.shape[1]
    xt_ref[:, :rows] = nf2_ref[...].T
    xt_ref[:, rows:] = nf_ref[...].T
    for base, out_refs in ((0, (keep_ref, send_ref)), (ffn, (keep2_ref, send2_ref))):

        def right(low, high, base=base):
            return jnp.concatenate(
                [dgu2_ref[:, base + low : base + high], dgu_ref[:, base + low : base + high]], axis=0
            )

        grad_parts(place_ref, right, *out_refs, xt_ref)


def feed_back_gate(place, grad, middle, gating, upward, gain, nf2, nf, dgu2, weights):
    rows, width = grad.shape
    weights_a, weights_gu, weights_dn = weights
    ffn = weights_dn.shape[1]
    wo_wide = width + HEAD_SIZE
    return pl.pallas_call(
        feed_back_gate_kernel,
        out_shape=(
            shape((rows, width), f32),
            shape((rows, wo_wide), bf16),
            shape((width, rows), bf16),
            shape((1, width), f32),
        )
        + (shape((2, 4, width // 4, ffn // 4), bf16),) * 4,
        in_specs=[in_smem()] + [in_vmem()] * 9 + [anywhere(), in_vmem()],
        out_specs=(in_vmem(),) * 8,
        scratch_shapes=[
            pltpu.VMEM((rows, width), bf16),
            pltpu.VMEM((rows, 2 * ffn), bf16),
            pltpu.VMEM((rows, width), f32),
            pltpu.VMEM((width, 2 * rows), bf16),
            pltpu.VMEM((width, 2 * ffn), bf16),
            pltpu.SemaphoreType.DMA((4,)),
        ],
        compiler_params=params(FFN_MEBIBYTES),
        cost_estimate=cost(2 * rows * width * (8 * ffn), 3 * width * ffn * 2 + rows * ffn * 8),
        name="feed_back_gate",
    )(place, grad, middle, gating, upward, gain, nf2, nf, dgu2, kept(weights_a), in_hbm(weights_gu),
      kept(weights_dn))


def leave_mixed_kernel(*refs):
    (place_ref, h_ref, dmid_ref, dq_ref, own_ref, got_ref, gain_ref, cos_ref, sin_ref, n1_ref, n2_ref,
     d1_ref, a1_ref, a2_ref, m1_ref, m2_ref, attention_gain_ref, ffn_gain_ref, ffn_gain2_ref, w_ref,
     g_ref, keep_ref, send_ref, d2_ref, dgain_ref, turned_ref, nt_ref, at_ref, gains_ref) = refs
    leave_kernel(
        h_ref, dmid_ref, dq_ref, own_ref, got_ref, gain_ref, cos_ref, sin_ref, w_ref, g_ref, d2_ref,
        dgain_ref, turned_ref,
    )
    gains = (attention_gain_ref[...] + dgain_ref[...], ffn_gain_ref[...] + ffn_gain2_ref[...])
    attention_grad_kernel(
        place_ref, n1_ref, n2_ref, d1_ref, d2_ref, a1_ref, a2_ref, m1_ref, m2_ref, gains, keep_ref,
        send_ref, nt_ref, at_ref, gains_ref,
    )


def leave_mixed(
    place, hidden, d_middle, dq, own, got, gain, cos, sin, normed, dqkv2, att, gm, gain_grads, weights_a
):
    rows, width = hidden.shape
    key_width = KEY_VALUE_HEADS * HEAD_SIZE
    wide = width + 2 * key_width + HEAD_SIZE
    block = width // 4 + GAIN_ROWS
    columns = 2 * width + 2 * key_width
    return pl.pallas_call(
        leave_mixed_kernel,
        out_shape=(shape((width, rows), bf16),)
        + (shape((2, 4, block, columns // 4), bf16),) * 2,
        in_specs=[in_smem()] + [in_vmem()] * 19,
        out_specs=(in_vmem(),) * 3,
        scratch_shapes=[
            pltpu.VMEM((rows, wide), bf16),
            pltpu.VMEM((1, width), f32),
            pltpu.VMEM((wide, rows), bf16),
            pltpu.VMEM((width, 2 * rows), bf16),
            pltpu.VMEM((width, 2 * rows), bf16),
            pltpu.VMEM((GAIN_ROWS, columns), f32),
        ],
        compiler_params=params(),
        cost_estimate=cost(6 * rows * width * wide, width * wide * 2 + rows * width * 14),
        name="leave_mixed",
    )(place, hidden, d_middle, dq, own, got, gain, cos, sin, *normed, dqkv2, *att, *gm, *gain_grads,
      kept(weights_a))


def down_grad_kernel(place_ref, g2_ref, g_ref, inner2_ref, inner_ref, keep_ref, send_ref, gt_ref):
    rows = g2_ref.shape[0]
    height, step = keep_ref.shape[2:]
    gt_ref[:, :rows] = g2_ref[...].T
    gt_ref[:, rows:] = g_ref[...].astype(bf16).T
    core, chip, quarter = place_ref[0], place_ref[1], place_ref[2]
    for away in range(2):
        for out_ref, which in ((keep_ref, core), (send_ref, 1 - core)):
            columns = pl.ds(pl.multiple_of((2 * (chip ^ away) + which) * step, 128), step)
            right = jnp.concatenate([inner2_ref[:, columns], inner_ref[:, columns]], axis=0)
            for part in range(4):
                out_ref[away, part ^ quarter] = nn(
                    gt_ref[part * height : (part + 1) * height, :], right
                ).astype(bf16)


def down_grad_parts(place, g2, g, inner2, inner):
    rows, width = g.shape
    ffn = inner.shape[1]
    return pl.pallas_call(
        down_grad_kernel,
        out_shape=(shape((2, 4, width // 4, ffn // 4), bf16),) * 2,
        in_specs=[in_smem()] + [in_vmem()] * 4,
        out_specs=(in_vmem(),) * 2,
        scratch_shapes=[pltpu.VMEM((width, 2 * rows), bf16)],
        compiler_params=params(),
        cost_estimate=cost(4 * rows * width * ffn, width * ffn * 2),
        name="down_grad",
    )(place, in_hbm(g2), g, in_hbm(inner2), in_hbm(inner))


def attention_grad_kernel(
    place_ref, n1_ref, n2_ref, d1_ref, d2_ref, a1_ref, a2_ref, m1_ref, m2_ref, gains,
    keep_ref, send_ref, nt_ref, at_ref, gains_ref,
):
    rows = n1_ref.shape[0]
    block = n1_ref.shape[1] // 4
    wide = d1_ref.shape[1]
    edge = wide - 128
    step = keep_ref.shape[3]
    nt_ref[:, :rows] = n1_ref[...].T
    nt_ref[:, rows:] = n2_ref[...].T
    at_ref[:, :rows] = a1_ref[...].T
    at_ref[:, rows:] = a2_ref[...].T
    half = GAIN_ROWS // 2
    gains_ref[...] = jnp.zeros_like(gains_ref)
    for i, gain in enumerate(gains):
        gains_ref[i * half : (i + 1) * half, : gain.shape[1]] = jnp.broadcast_to(
            gain, (half, gain.shape[1])
        )
    core, chip, quarter = place_ref[0], place_ref[1], place_ref[2]
    d_mixed = jnp.concatenate([d1_ref[...], d2_ref[...]], axis=0)
    d_out = jnp.concatenate([m1_ref[...], m2_ref[...]], axis=0)
    for away in range(2):
        for out_ref, which in ((keep_ref, core), (send_ref, 1 - core)):
            member = 2 * (chip ^ away) + which
            start = pl.multiple_of(member * block, 16)
            normed = nt_ref[pl.ds(start, block), :]
            attended = at_ref[pl.ds(start, block), :]
            for part in range(4):
                low, high = part * step, (part + 1) * step
                pieces = []
                if low < edge:
                    pieces.append(nn(normed, d_mixed[:, low : min(high, edge)]))
                if low <= edge < high:
                    pieces.append(nn(normed, d_mixed[:, edge:]) + nn(attended, d_out[:, :128]))
                if high > wide:
                    base = wide - 128
                    pieces.append(nn(attended, d_out[:, max(low, wide) - base : high - base]))
                piece = pieces[0] if len(pieces) == 1 else jnp.concatenate(pieces, axis=1)
                out_ref[away, part ^ quarter, :block, :] = piece.astype(bf16)
                out_ref[away, part ^ quarter, block:, :] = gains_ref[:, low:high].astype(bf16)


def finish_kernel(place_ref, p0_ref, p1_ref, p2_ref, p3_ref, out_ref):
    part = pl.program_id(0)
    for i, ref in enumerate((p0_ref, p1_ref, p2_ref, p3_ref)):

        @pl.when(part == i)
        def _(ref=ref):
            out_ref[...] = ref[...].astype(f32)


def finish(place, pieces, by_rows):
    height, step = pieces[0].shape
    whole = pl.BlockSpec((height, step), lambda i, place: (0, 0))
    if by_rows:
        dims, index = (4 * height, step), lambda i, place: (i ^ place[2], 0)
    else:
        dims, index = (height, 4 * step), lambda i, place: (0, i ^ place[2])
    return pl.pallas_call(
        finish_kernel,
        grid_spec=pltpu.PrefetchScalarGridSpec(
            num_scalar_prefetch=1,
            grid=(4,),
            in_specs=[whole] * 4,
            out_specs=pl.BlockSpec((height, step), index),
        ),
        out_shape=shape(dims, f32),
        compiler_params=params(),
        cost_estimate=cost(0, 24 * height * step),
        name="finish",
    )(place, *pieces)


def finish_mixed_kernel(
    place_ref, p0_ref, p1_ref, p2_ref, p3_ref, query_ref, key_ref, value_ref, out_ref, gain_ref,
    mixed_ref,
):
    quarter = place_ref[2]
    block, width = query_ref.shape
    key_width = key_ref.shape[0]
    step = p0_ref.shape[1]
    for i, ref in enumerate((p0_ref, p1_ref, p2_ref, p3_ref)):
        start = pl.multiple_of((quarter ^ i) * step, 128)
        mixed_ref[:, pl.ds(start, step)] = ref[...].astype(f32)
    first_end = width + key_width
    second_end = first_end + key_width
    query_ref[...] = mixed_ref[:block, :width]
    key_ref[...] = mixed_ref[:block, width:first_end].T
    value_ref[...] = mixed_ref[:block, first_end:second_end].T
    out_ref[...] = mixed_ref[:block, second_end:]
    gain_ref[...] = mixed_ref[block:, : gain_ref.shape[1]]


def finish_mixed(place, pieces, width, key_width):
    height, step = pieces[0].shape
    block = height - GAIN_ROWS
    return pl.pallas_call(
        finish_mixed_kernel,
        out_shape=(
            shape((block, width), f32),
            shape((key_width, block), f32),
            shape((key_width, block), f32),
            shape((block, width), f32),
            shape((GAIN_ROWS, width + HEAD_SIZE), f32),
        ),
        in_specs=[in_smem()] + [in_vmem()] * 4,
        out_specs=(in_vmem(),) * 5,
        scratch_shapes=[pltpu.VMEM((height, 4 * step), f32)],
        compiler_params=params(),
        cost_estimate=cost(0, 24 * height * step),
        name="finish_mixed",
    )(place, *pieces)


def flip(value, axis_name, distance):
    size = lax.axis_size(axis_name)
    return lax.ppermute(value, axis_name, [(i, i ^ distance) for i in range(size)])


def pick(condition, when_true, when_false):
    return jnp.where(condition, when_true, when_false)


def order_by(bit, own, other):
    return (pick(bit == 1, other, own), pick(bit == 1, own, other))


def exchange_kv(block):
    beside = flip(block, "fsdp", 1)
    across = flip(block, "fsdp", 2)
    diagonal = flip(across, "fsdp", 1)
    return (block, beside, across, diagonal)


def fold_kv(keep, send):
    got = flip(send, "fsdp", 1)
    return total(keep[0], got[0]), total(keep[1], got[1])


def return_kv(keep, send):
    own, across = fold_kv(keep, send)
    return own, flip(across, "fsdp", 2)


def total(*terms):
    result = terms[0].astype(f32)
    for term in terms[1:]:
        result = result + term.astype(f32)
    return result.astype(bf16)


class Order:
    def __init__(self, *token):
        self.token = token

    def tie(self, *values):
        tied = lax.optimization_barrier(self.token + values)[len(self.token) :]
        return tied[0] if len(tied) == 1 else tied

    def done(self, value):
        self.token = (value,)
        return value

    def done_all(self, *values):
        self.token = values
        return values


class Reduction:
    def __init__(self, order, keep, send):
        self.order = order
        self.keep = keep
        self.core = flip(order.tie(send), "fsdp", 1)

    def chip(self):
        self.core = self.order.tie(self.core)
        high = total(self.keep[1, 2:], self.core[1, 2:])
        low = total(self.keep[1, :2], self.core[1, :2])
        high, low = self.order.done_all(high, low)
        self.high = flip(high, "fsdp", 2)
        self.low = flip(low, "fsdp", 2)

    def first(self, both=False):
        if both:
            self.high, self.low = self.order.tie(self.high, self.low)
        else:
            self.high = self.order.tie(self.high)
        out = total(self.keep[0, 2:], self.core[0, 2:], self.high)
        self.got = flip(self.order.done(out), "dp", 1)

    def rest(self):
        self.low = self.order.done(self.order.tie(self.low))

    def second(self):
        self.got, self.low = self.order.tie(self.got, self.low)
        self.terms = (self.keep[0, :2], self.core[0, :2], self.low, self.got)
        self.got = flip(self.order.done(total(*[term[1] for term in self.terms])), "dp", 2)

    def third(self):
        size = lax.axis_size("dp")
        own = total(*[term[0] for term in self.terms], self.order.tie(self.got))
        distance = 4
        while 2 * distance < size:
            own = total(own, flip(own, "dp", distance))
            distance *= 2
        self.own = self.order.done(own)
        self.got = flip(own, "dp", distance) if distance < size else jnp.zeros_like(own)

    def back(self):
        self.own = self.order.done(total(self.own, self.order.tie(self.got)))
        self.beside = flip(self.own, "dp", 2)
        self.pieces = [self.own, self.beside, flip(self.own, "dp", 1)]

    def back_again(self):
        self.beside = self.order.done(self.order.tie(self.beside))
        self.pieces.append(flip(self.beside, "dp", 1))

    def end(self):
        return self.order.tie(*self.pieces)


def rotation(token_positions):
    frequency = rope_base ** (-jnp.arange(HALF, dtype=f32) / HALF)
    angles = frequency[:, None] * token_positions.astype(f32)[None, :]
    return jnp.cos(angles), jnp.sin(angles)


def body(
    tokens,
    cotangent,
    sequence_ids,
    span_position,
    attention_norm,
    query_weight,
    key_matrix,
    value_matrix,
    output_weight,
    feedforward_norm,
    gate_weight,
    up_weight,
    down_weight,
):
    rows, width = tokens.shape
    key_width = key_matrix.shape[1]
    ffn = gate_weight.shape[1]
    itself = lax.axis_index("fsdp")
    outer = lax.axis_index("dp")
    quarter = 2 * (outer % 2) + (outer // 2) % 2
    place = jnp.stack([itself % 2, itself // 2, quarter]).astype(jnp.int32)

    outer = lax.axis_index("dp")
    bits = jnp.stack([outer % 2, (outer // 2) % 2, itself]).astype(jnp.int32)
    packed, *mine = pack(
        bits, query_weight, key_matrix.T, value_matrix.T, output_weight, gate_weight, up_weight
    )
    down_t = down_weight.T
    half = width // 2
    mine.append(pick(outer % 2 == 1, down_t[half:], down_t[:half]))
    gains = jnp.stack([attention_norm, feedforward_norm], axis=0)
    gains = [flip(gains, "fsdp", distance) if distance else gains for distance in range(4)]
    mine = Order(*gains).tie(*mine)
    far = [flip(piece, "fsdp", 2) for piece in mine]
    shards = (packed, gate_weight, up_weight, down_t)
    near = [flip(shard, "fsdp", 1) for shard in shards]
    sequence_ids, span_position = Order(*mine).tie(sequence_ids, span_position)
    places = jnp.arange(rows, dtype=jnp.int32) + span_position[itself] * rows
    cos, sin = rotation(places)
    others = itself ^ jnp.arange(4)
    visible = (
        (sequence_ids[others] == sequence_ids[itself])
        & (span_position[others] <= span_position[itself])
    ).astype(jnp.int32)

    beside = order_by(itself % 2, gains[0], gains[1])
    away = order_by(itself % 2, gains[2], gains[3])
    chip = itself // 2 == 1
    gains = jnp.concatenate(
        [pick(chip, a, n) for a, n in zip(away, beside)]
        + [pick(chip, n, a) for a, n in zip(away, beside)],
        axis=1,
    ).astype(f32)
    attention_gain, ffn_gain = gains[:1], gains[1:]
    order = Order(cos, sin, visible, attention_gain, ffn_gain)
    share = ((1, 0), (1, 0), (2, 1), (1, 0))

    def shared(i):
        got = order.done(order.tie(far[i]))
        return got, flip(got, "dp", share[i][0])

    def gathered(i, got, other):
        return [shards[i], near[i], got, other, flip(got, "fsdp", 1), flip(other, "fsdp", 1)]

    shared_a = shared(0)
    order.done_all(*order.tie(*shared_a))
    shared_gate = shared(1)
    sources_a = gathered(0, *shared_a)
    order.done_all(*order.tie(*near), *sources_a)
    tokens_t = order.tie(tokens.T)
    hidden, normed, q, kv, weights_a = enter_first(
        bits, tokens_t, attention_gain, cos, sin, shared_plan(0, 0, 0), tuple(sources_a)
    )
    order.done(kv)
    shared_up = shared(2)
    shared_gate = order.done_all(*order.tie(*shared_gate))
    kvs = exchange_kv(kv)
    shared_down = shared(3)
    order.done_all(*order.tie(*shared_up))
    sources_gu = gathered(1, *shared_gate) + gathered(2, *shared_up)
    sources_dn = gathered(3, *order.tie(*shared_down))
    plan_gu = shared_plan(0, 0, 0) + shared_plan(6, ffn, 1)
    plan_dn = shared_plan(0, None, 0)
    finished, att, att_t, lse, middle, nf, gating, upward, inner, weights_gu, weights_dn = forward_block(
        visible, bits, hidden, q, kvs, ffn_gain, weights_a, tuple(sources_gu), tuple(sources_dn),
        (plan_gu, plan_dn),
    )
    weights = (weights_a, weights_gu, weights_dn)
    saved = [(hidden, normed, q, kvs, att, att_t, lse, middle, nf, gating, upward, inner)]
    hidden = finished
    normed, q, kv = enter(hidden, attention_gain, cos, sin, weights_a)
    kvs = exchange_kv(kv)
    activations, att, att_t, lse, middle, nf, gating, upward, inner = forward_block(
        visible, bits, hidden, q, kvs, ffn_gain, weights_a, (weights_gu,), (weights_dn,)
    )
    saved.append((hidden, normed, q, kvs, att, att_t, lse, middle, nf, gating, upward, inner))

    hidden, normed2, q, kvs, att2, att_t, lse, middle, nf2, gating, upward, inner2 = saved[1]
    gb2, dgu2, d_middle, gm2, d_out, ffn_gain_grad2 = feed_back(
        cotangent.T, middle, gating, upward, ffn_gain, weights
    )
    dq, *dkvs = attend_back(visible, q, d_out, att_t, lse, cos, sin, kvs)
    own, got = return_kv(*dkvs)
    grad, dqkv2, attention_gain_grad2 = leave(
        hidden, d_middle, dq, own, got, attention_gain, cos, sin, weights_a
    )

    hidden, normed, q, kvs, att, att_t, lse, middle, nf, gating, upward, inner = saved[0]
    order = Order(grad)
    down = Reduction(order, *down_grad_parts(place, gb2, grad, inner2, inner))
    down.chip()
    d_middle, gm, d_out, ffn_gain_grad, *rest = feed_back_gate(
        place, order.tie(grad), middle, gating, upward, ffn_gain, nf2, nf, dgu2, weights
    )
    order.done(d_middle)
    down.first()
    gate = Reduction(order, *rest[:2])
    gate.chip()
    down.rest()
    up = Reduction(order, *rest[2:])
    dq, *dkvs = attend_back(visible, order.tie(q), d_out, att_t, lse, cos, sin, kvs)
    order.done(dq)
    gate.first()
    down.second()
    own, across = fold_kv(*order.tie(*dkvs))
    order.done(across)
    gate.rest()
    down.third()
    across = order.tie(across)
    got = order.done(order.tie(flip(across, "fsdp", 2)))
    gate.second()
    up.chip()
    d_middle = order.tie(d_middle)
    grad, *mixed = leave_mixed(
        place,
        hidden,
        d_middle,
        dq,
        own,
        got,
        attention_gain,
        cos,
        sin,
        (normed2, normed),
        dqkv2,
        (att2, att),
        (gm2, gm),
        (attention_gain_grad2, ffn_gain_grad2, ffn_gain_grad),
        weights_a,
    )
    order.done(grad)
    up.first()
    down.back()
    gate.third()
    mixed = Reduction(order, *mixed)
    mixed.chip()
    up.second()
    down.back_again()
    down_grad = order.done(finish(place, down.end(), True))
    mixed.first()
    gate.back()
    up.third()
    mixed.rest()
    mixed.second()
    gate.back_again()
    gate_grad = order.done(finish(place, gate.end(), False))
    up.back()
    mixed.third()
    up.back_again()
    up_grad = order.done(finish(place, up.end(), False))
    mixed.back()
    mixed.back_again()
    query_grad, key_grad, value_grad, output_grad, gain_grads = finish_mixed(
        place, mixed.end(), width, key_width
    )
    shard_rows = attention_norm.shape[0]
    gain_grads = lax.dynamic_slice_in_dim(gain_grads, itself * shard_rows, shard_rows, axis=1)
    return (
        activations.T,
        grad.T,
        gain_grads[0],
        query_grad,
        key_grad.T,
        value_grad.T,
        output_grad,
        gain_grads[GAIN_ROWS // 2],
        gate_grad,
        up_grad,
        down_grad.T,
    )


def solution(mesh):
    return jax.shard_map(
        body,
        mesh=mesh,
        in_specs=(
            P(("dp", "fsdp"), None),
            P(("dp", "fsdp"), None),
            P("dp"),
            P("dp"),
            P("fsdp"),
            P("fsdp", None),
            P("fsdp", None),
            P("fsdp", None),
            P("fsdp", None),
            P("fsdp"),
            P("fsdp", None),
            P("fsdp", None),
            P("fsdp", None),
        ),
        out_specs=(
            P(("dp", "fsdp"), None),
            P(("dp", "fsdp"), None),
            P("fsdp"),
            P("fsdp", None),
            P("fsdp", None),
            P("fsdp", None),
            P("fsdp", None),
            P("fsdp"),
            P("fsdp", None),
            P("fsdp", None),
            P("fsdp", None),
        ),
        check_vma=False,
    )
```

```python
import functools

import jax
import jax.numpy as jnp
from jax import lax
from jax.experimental import pallas as pl
from jax.experimental.pallas import tpu as pltpu
from jax.sharding import PartitionSpec as P

QUERY_HEADS = 15
KEY_VALUE_HEADS = 5
HEAD_SIZE = 64
SHARING = QUERY_HEADS // KEY_VALUE_HEADS
HALF = HEAD_SIZE // 2

epsilon = 1e-05
rope_base = 10000.0
masked = -1e30
score_scale = HEAD_SIZE ** (-0.5)

bf16 = jnp.bfloat16
f32 = jnp.float32
GAIN_ROWS = 16
FFN_MEBIBYTES = 26


def nn(left, right):
    return jnp.dot(left, right, preferred_element_type=f32)


def nt(left, right):
    return lax.dot_general(left, right, (((1,), (1,)), ((), ())), preferred_element_type=f32)


def in_vmem():
    return pl.BlockSpec(memory_space=pltpu.VMEM)


def in_smem():
    return pl.BlockSpec(memory_space=pltpu.SMEM)


def anywhere():
    return pl.BlockSpec(memory_space=pl.ANY)


def params(mebibytes=14):
    return pltpu.CompilerParams(vmem_limit_bytes=mebibytes * 1024 * 1024)


def shape(dims, dtype):
    return jax.ShapeDtypeStruct(dims, dtype)


def kept(array):
    return pltpu.with_memory_space_constraint(array, pltpu.VMEM)


def in_hbm(array):
    return pltpu.with_memory_space_constraint(array, pltpu.HBM)


def cost(flops, bytes_accessed):
    return pl.CostEstimate(flops=int(flops), bytes_accessed=int(bytes_accessed), transcendentals=0)


def inverse_rms(hidden):
    return lax.rsqrt(jnp.mean(hidden * hidden, axis=-1, keepdims=True) + epsilon)


def pack_kernel(
    bits_ref, query_hbm, key_hbm, value_hbm, out_hbm, gate_hbm, up_hbm, packed_hbm, mine_hbm,
    mine_gate_hbm, mine_up_hbm, query_ref, key_ref, value_ref, out_ref, gate_ref, up_ref, packed_ref,
    mine_ref, sems,
):
    half = gate_ref.shape[1]
    loads = [
        pltpu.make_async_copy(source, target, sems.at[i])
        for i, (source, target) in enumerate(
            (
                (query_hbm, query_ref),
                (key_hbm, key_ref),
                (value_hbm, value_ref),
                (out_hbm, out_ref),
                (gate_hbm.at[:, pl.ds(pl.multiple_of(bits_ref[0] * half, 128), half)], gate_ref),
                (up_hbm.at[:, pl.ds(pl.multiple_of(bits_ref[1] * half, 128), half)], up_ref),
            )
        )
    ]
    for load in loads:
        load.start()
    for load in loads[:4]:
        load.wait()
    packed_ref[...] = jnp.concatenate(
        [
            query_ref[...].astype(f32),
            key_ref[...].astype(f32).T,
            value_ref[...].astype(f32).T,
            out_ref[...].astype(f32),
        ],
        axis=1,
    ).astype(bf16)
    wide = mine_ref.shape[1]
    mine_ref[...] = packed_ref[:, pl.ds(pl.multiple_of(bits_ref[0] * wide, 128), wide)]
    for load in loads[4:]:
        load.wait()
    stores = [
        pltpu.make_async_copy(source, target, sems.at[i])
        for i, (source, target) in enumerate(
            (
                (mine_ref, mine_hbm),
                (gate_ref, mine_gate_hbm),
                (up_ref, mine_up_hbm),
                (packed_ref, packed_hbm),
            )
        )
    ]
    for store in stores:
        store.start()
    for store in stores:
        store.wait()


def pack(bits, query, key_t, value_t, out, gate, up):
    rows, width = query.shape
    columns = 2 * width + 2 * key_t.shape[0]
    ffn = gate.shape[1]
    return pl.pallas_call(
        pack_kernel,
        out_shape=(
            pltpu.HBM((rows, columns), bf16),
            pltpu.HBM((rows, columns // 2), bf16),
            pltpu.HBM((rows, ffn // 2), bf16),
            pltpu.HBM((rows, ffn // 2), bf16),
        ),
        in_specs=[in_smem()] + [anywhere()] * 6,
        out_specs=(anywhere(),) * 4,
        scratch_shapes=[
            pltpu.VMEM((rows, width), bf16),
            pltpu.VMEM(key_t.shape, bf16),
            pltpu.VMEM(value_t.shape, bf16),
            pltpu.VMEM((rows, width), bf16),
            pltpu.VMEM((rows, ffn // 2), bf16),
            pltpu.VMEM((rows, ffn // 2), bf16),
            pltpu.VMEM((rows, columns), bf16),
            pltpu.VMEM((rows, columns // 2), bf16),
            pltpu.SemaphoreType.DMA((6,)),
        ],
        compiler_params=params(),
        cost_estimate=cost(0, 8 * rows * columns),
        name="pack",
    )(bits, *[in_hbm(part) for part in (query, key_t, value_t, out, gate, up)])


def piece_copies(plan, bits_ref, sources, target_ref, sems):
    me = bits_ref[2]
    copies = []
    for i, (which, member, column, part, bit) in enumerate(plan):
        source = sources[which]
        height, width = source.shape
        if column is None:
            turned = pl.ds(pl.multiple_of((me ^ member) * width, 128), width)
            if part is None:
                rows = pl.ds(0, height)
            else:
                rows = pl.ds(pl.multiple_of((bits_ref[bit] ^ part) * height, 16), height)
            target = target_ref.at[rows, turned]
        else:
            rows = pl.ds(pl.multiple_of((me ^ member) * height, 16), height)
            if part is None:
                columns = pl.ds(column, width)
            else:
                columns = pl.ds(
                    pl.multiple_of(column + (bits_ref[bit] ^ part) * width, 128), width
                )
            target = target_ref.at[rows, columns]
        copies.append(pltpu.make_async_copy(source, target, sems.at[i]))
    return copies


def shared_plan(first, column, bit):
    return (
        (first, 0, column, None, bit),
        (first + 1, 1, column, None, bit),
        (first + 2, 2, column, 0, bit),
        (first + 3, 2, column, 1, bit),
        (first + 4, 3, column, 0, bit),
        (first + 5, 3, column, 1, bit),
    )


def enter_body(hidden, gain_ref, cos_ref, sin_ref, ready, normed_ref, q_ref, kv_ref, w_ref):
    width = hidden.shape[1]
    key_width = kv_ref.shape[0] // 2
    mixed_width = width + key_width
    wide = width + 2 * key_width + HEAD_SIZE
    normed = (hidden * inverse_rms(hidden) * gain_ref[...]).astype(bf16)
    normed_ref[...] = normed
    cos, sin = cos_ref[...], sin_ref[...]
    ready()
    mixed = nn(normed, w_ref[:, :mixed_width]).T
    for head in range(QUERY_HEADS + KEY_VALUE_HEADS):
        low = head * HEAD_SIZE
        first = mixed[low : low + HALF]
        second = mixed[low + HALF : low + HEAD_SIZE]
        top = first * cos - second * sin
        bottom = second * cos + first * sin
        if head < QUERY_HEADS:
            q_ref[low : low + HALF, :] = (top * score_scale).astype(bf16)
            q_ref[low + HALF : low + HEAD_SIZE, :] = (bottom * score_scale).astype(bf16)
        else:
            low = low - width
            kv_ref[low : low + HALF, :] = top.astype(bf16)
            kv_ref[low + HALF : low + HEAD_SIZE, :] = bottom.astype(bf16)
    values = nn(normed, w_ref[:, mixed_width:wide]).T
    kv_ref[key_width:, :] = values[:key_width].astype(bf16)


def enter_first_kernel(plan, count, index_ref, h_ref, gain_ref, cos_ref, sin_ref, *refs):
    sources = refs[:count]
    hidden_ref, normed_ref, q_ref, kv_ref, w_ref, sems = refs[count:]
    copies = piece_copies(plan, index_ref, sources, w_ref, sems)
    for copy in copies:
        copy.start()
    hidden = h_ref[...].astype(f32).T
    hidden_ref[...] = hidden

    def ready():
        for copy in copies:
            copy.wait()

    enter_body(hidden, gain_ref, cos_ref, sin_ref, ready, normed_ref, q_ref, kv_ref, w_ref)


def enter_first(index, hidden_t, gain, cos, sin, plan, sources):
    width, rows = hidden_t.shape
    key_width = KEY_VALUE_HEADS * HEAD_SIZE
    columns = 2 * (width + key_width)
    return pl.pallas_call(
        functools.partial(enter_first_kernel, plan, len(sources)),
        out_shape=(
            shape((rows, width), f32),
            shape((rows, width), bf16),
            shape((width, rows), bf16),
            shape((2 * key_width, rows), bf16),
            pltpu.VMEM((width, columns), bf16),
        ),
        in_specs=[in_smem()] + [in_vmem()] * 4 + [anywhere()] * len(sources),
        out_specs=(in_vmem(),) * 5,
        scratch_shapes=[pltpu.SemaphoreType.DMA((len(plan),))],
        compiler_params=params(),
        cost_estimate=cost(4 * rows * width * width, width * columns * 4),
        name="enter_first",
    )(index, hidden_t, gain, cos, sin, *sources)


def enter_kernel(h_ref, gain_ref, cos_ref, sin_ref, w_ref, normed_ref, q_ref, kv_ref):
    enter_body(
        h_ref[...], gain_ref, cos_ref, sin_ref, lambda: None, normed_ref, q_ref, kv_ref, w_ref
    )


def enter(hidden, gain, cos, sin, weights_a):
    rows, width = hidden.shape
    key_width = KEY_VALUE_HEADS * HEAD_SIZE
    wide = width + 2 * key_width + HEAD_SIZE
    return pl.pallas_call(
        enter_kernel,
        out_shape=(
            shape((rows, width), bf16),
            shape((width, rows), bf16),
            shape((2 * key_width, rows), bf16),
        ),
        in_specs=[in_vmem()] * 5,
        out_specs=(in_vmem(),) * 3,
        compiler_params=params(),
        cost_estimate=cost(2 * rows * width * wide, width * wide * 2 + rows * width * 10),
        name="enter",
    )(hidden, gain, cos, sin, kept(weights_a))


def out_weight(a_ref):
    return a_ref[:, a_ref.shape[1] - a_ref.shape[0] - HEAD_SIZE :]


def stacked_heads(ref, group):
    parts = []
    for j in range(SHARING):
        low = (group * SHARING + j) * HEAD_SIZE
        parts.append(ref[low : low + HEAD_SIZE, :])
    return jnp.concatenate(parts, axis=1)


def key_block(ref, group):
    return ref[group * HEAD_SIZE : (group + 1) * HEAD_SIZE, :]


def value_block(ref, group):
    key_width = KEY_VALUE_HEADS * HEAD_SIZE
    return ref[key_width + group * HEAD_SIZE : key_width + (group + 1) * HEAD_SIZE, :]


def causal(rows):
    keys = lax.broadcasted_iota(jnp.int32, (rows, SHARING * rows), 0)
    queries = lax.broadcasted_iota(jnp.int32, (rows, SHARING * rows), 1) % rows
    return keys <= queries


def whole_copies(source_ref, target_ref, sems):
    parts = 4
    height = source_ref.shape[0] // parts
    return [
        pltpu.make_async_copy(
            source_ref.at[pl.ds(i * height, height), :],
            target_ref.at[pl.ds(i * height, height), :],
            sems.at[i],
        )
        for i in range(parts)
    ]


def forward_kernel(plans, counts, *refs):
    (visible_ref, bits_ref, h_ref, q_ref, kv0_ref, kv1_ref, kv2_ref, kv3_ref, gain_ref, a_ref) = refs[:10]
    gu_sources = refs[10 : 10 + counts[0]]
    dn_sources = refs[10 + counts[0] : 10 + counts[0] + counts[1]]
    refs = refs[10 + counts[0] + counts[1] :]
    (out_ref, att_ref, att_t_ref, lse_ref, middle_ref, nf_ref, gating_ref, upward_ref, inner_ref) = refs[:9]
    refs = refs[9:]
    gu_ref, gu_sems, dn_sems = refs[-3:]
    if plans is not None:
        gu_hbm, dn_ref = refs[:2]
        refs = refs[2:]
        gu_loads = piece_copies(plans[0], bits_ref, gu_sources, gu_ref, gu_sems)
        dn_loads = piece_copies(plans[1], bits_ref, dn_sources, dn_ref, dn_sems)
    else:
        (dn_ref,) = dn_sources
        gu_loads, dn_loads = whole_copies(gu_sources[0], gu_ref, gu_sems), []
    acc_ref, m_ref, l_ref, kvs_ref = refs[:4]
    rows, width = h_ref.shape
    ffn = inner_ref.shape[1]
    for load in gu_loads + dn_loads:
        load.start()

    allowed = causal(rows)
    for group in range(KEY_VALUE_HEADS):
        scores = nn(key_block(kv0_ref, group).T, stacked_heads(q_ref, group))
        scores = jnp.where(allowed, scores, masked)
        peak = jnp.max(scores, axis=0, keepdims=True)
        raised = jnp.exp(scores - peak)
        m_ref[group : group + 1, :] = peak
        l_ref[group : group + 1, :] = jnp.sum(raised, axis=0, keepdims=True)
        acc_ref[group] = nn(value_block(kv0_ref, group), raised.astype(bf16))
    for i, kv_ref in enumerate((kv1_ref, kv2_ref, kv3_ref)):
        kvs_ref[i] = kv_ref[...]

    @pl.loop(0, 3)
    def _(member):
        kv_ref = kvs_ref.at[member]

        @pl.when(visible_ref[member + 1] == 1)
        def _():
            for group in range(KEY_VALUE_HEADS):
                scores = nn(key_block(kv_ref, group).T, stacked_heads(q_ref, group))
                old = m_ref[group : group + 1, :]
                peak = jnp.maximum(old, jnp.max(scores, axis=0, keepdims=True))
                raised = jnp.exp(scores - peak)
                fade = jnp.exp(old - peak)
                m_ref[group : group + 1, :] = peak
                l_ref[group : group + 1, :] = l_ref[group : group + 1, :] * fade + jnp.sum(
                    raised, axis=0, keepdims=True
                )
                acc_ref[group] = acc_ref[group] * fade + nn(
                    value_block(kv_ref, group), raised.astype(bf16)
                )

    total = l_ref[...]
    lse_ref[...] = m_ref[...] + jnp.log(total)
    for group in range(KEY_VALUE_HEADS):
        mean = acc_ref[group] / total[group : group + 1, :]
        for j in range(SHARING):
            low = (group * SHARING + j) * HEAD_SIZE
            att_t_ref[low : low + HEAD_SIZE, :] = mean[:, j * rows : (j + 1) * rows].astype(bf16)
    attended = att_t_ref[...].T
    att_ref[...] = attended
    middle = h_ref[...] + nn(attended, out_weight(a_ref))[:, HEAD_SIZE:]
    middle_ref[...] = middle
    normed = (middle * inverse_rms(middle) * gain_ref[...]).astype(bf16)
    nf_ref[...] = normed
    for load in gu_loads:
        load.wait()
    gu_stores = whole_copies(gu_ref, gu_hbm, gu_sems) if plans is not None else []
    for store in gu_stores:
        store.start()
    step = 512
    for low in range(0, ffn, step):
        gating = nn(normed, gu_ref[:, low : low + step])
        upward = nn(normed, gu_ref[:, ffn + low : ffn + low + step])
        gating_ref[:, low : low + step] = gating.astype(bf16)
        upward_ref[:, low : low + step] = upward.astype(bf16)
        inner_ref[:, low : low + step] = (gating * jax.nn.sigmoid(gating) * upward).astype(bf16)
    for load in dn_loads:
        load.wait()
    finished = middle + nt(inner_ref[...], dn_ref[...])
    out_ref[...] = finished if plans is not None else finished.T.astype(bf16)
    for store in gu_stores:
        store.wait()


def forward_block(visible, index, hidden, q, kvs, gain, weights_a, gu, dn, plans=None):
    rows, width = hidden.shape
    ffn = gu[0].shape[1] if plans is not None else gu[0].shape[1] // 2
    lanes = SHARING * rows
    counts = (len(gu), len(dn))
    first = plans is not None
    whole = (pltpu.HBM((width, 2 * ffn), bf16), pltpu.VMEM((width, ffn), bf16))
    return pl.pallas_call(
        functools.partial(forward_kernel, plans, counts),
        out_shape=(
            shape((rows, width), f32) if first else shape((width, rows), bf16),
            shape((rows, width), bf16),
            shape((width, rows), bf16),
            shape((KEY_VALUE_HEADS, lanes), f32),
            shape((rows, width), f32),
            shape((rows, width), bf16),
            shape((rows, ffn), bf16),
            shape((rows, ffn), bf16),
            shape((rows, ffn), bf16),
        )
        + (whole if first else ()),
        in_specs=[in_smem()] * 2
        + [in_vmem()] * 8
        + [anywhere()] * counts[0]
        + [anywhere() if first else in_vmem()] * counts[1],
        out_specs=(in_vmem(),) * 9 + ((anywhere(), in_vmem()) if first else ()),
        scratch_shapes=[
            pltpu.VMEM((KEY_VALUE_HEADS, HEAD_SIZE, lanes), f32),
            pltpu.VMEM((KEY_VALUE_HEADS, lanes), f32),
            pltpu.VMEM((KEY_VALUE_HEADS, lanes), f32),
            pltpu.VMEM((3, *kvs[0].shape), bf16),
            pltpu.VMEM((width, 2 * ffn), bf16),
            pltpu.SemaphoreType.DMA((len(plans[0]) if first else 4,)),
            pltpu.SemaphoreType.DMA((len(plans[1]) if first else 1,)),
        ],
        compiler_params=params(FFN_MEBIBYTES),
        cost_estimate=cost(2 * rows * width * (4 * ffn), 3 * width * ffn * 2 + rows * ffn * 8),
        name="forward_first" if first else "forward_last",
    )(
        visible, index, hidden, q, *kvs, gain, kept(weights_a),
        *([*gu, *dn] if first else [in_hbm(gu[0]), kept(dn[0])]),
    )


def feed_back_kernel(
    g_ref,
    middle_ref,
    gating_ref,
    upward_ref,
    gain_ref,
    a_ref,
    gu_hbm,
    dn_ref,
    gb_ref,
    dgu_ref,
    dmid_ref,
    gm_ref,
    do_ref,
    dgain_ref,
    sum_ref,
    gu_ref,
    gu_sems,
):
    rows, width = middle_ref.shape
    ffn = gating_ref.shape[1]
    loads = whole_copies(gu_hbm, gu_ref, gu_sems)
    for load in loads:
        load.start()
    grad = g_ref[...] if g_ref.shape[0] == rows else g_ref[...].astype(f32).T
    short = grad.astype(bf16)
    gb_ref[...] = short
    step = 512
    for low in range(0, ffn, step):
        part = slice(low, low + step)
        behind = slice(ffn + low, ffn + low + step)
        d_inner = nn(short, dn_ref[:, part])
        gating = gating_ref[:, part].astype(f32)
        upward = upward_ref[:, part].astype(f32)
        gate = jax.nn.sigmoid(gating)
        d_gating = (d_inner * upward * (gate * (1.0 + gating * (1.0 - gate)))).astype(bf16)
        d_upward = (d_inner * (gating * gate)).astype(bf16)
        dgu_ref[:, part] = d_gating
        dgu_ref[:, behind] = d_upward
    for load in loads:
        load.wait()
    sum_ref[...] = nt(dgu_ref[...], gu_ref[...])
    d_normed = sum_ref[...]
    middle = middle_ref[...]
    factor = inverse_rms(middle)
    unit = middle * factor
    dgain_ref[...] = jnp.sum(d_normed * unit, axis=0, keepdims=True)
    scaled = d_normed * gain_ref[...]
    d_middle = grad + factor * (scaled - unit * jnp.mean(scaled * unit, axis=-1, keepdims=True))
    dmid_ref[...] = d_middle
    padded = jnp.concatenate(
        [jnp.zeros((rows, HEAD_SIZE), f32), d_middle], axis=1
    ).astype(bf16)
    gm_ref[...] = padded
    do_ref[...] = nt(padded, out_weight(a_ref)).T.astype(bf16)


def feed_back(grad, middle, gating, upward, gain, weights):
    rows, width = middle.shape
    weights_a, weights_gu, weights_dn = weights
    ffn = weights_dn.shape[1]
    wo_wide = width + HEAD_SIZE
    return pl.pallas_call(
        feed_back_kernel,
        out_shape=(
            shape((rows, width), bf16),
            shape((rows, 2 * ffn), bf16),
            shape((rows, width), f32),
            shape((rows, wo_wide), bf16),
            shape((width, rows), bf16),
            shape((1, width), f32),
        ),
        in_specs=[in_vmem()] * 6 + [anywhere(), in_vmem()],
        out_specs=(in_vmem(),) * 6,
        scratch_shapes=[
            pltpu.VMEM((rows, width), f32),
            pltpu.VMEM((width, 2 * ffn), bf16),
            pltpu.SemaphoreType.DMA((4,)),
        ],
        compiler_params=params(FFN_MEBIBYTES),
        cost_estimate=cost(2 * rows * width * (4 * ffn), 3 * width * ffn * 2 + rows * ffn * 8),
        name="feed_back",
    )(grad, middle, gating, upward, gain, kept(weights_a), in_hbm(weights_gu), kept(weights_dn))


def attend_back_kernel(
    visible_ref,
    q_ref,
    do_ref,
    att_ref,
    lse_ref,
    cos_ref,
    sin_ref,
    kv0_ref,
    kv1_ref,
    kv2_ref,
    kv3_ref,
    dq_ref,
    keep_ref,
    send_ref,
    acc_ref,
    row_ref,
    kvs_ref,
    dkvs_ref,
):
    rows = q_ref.shape[1]
    key_width = KEY_VALUE_HEADS * HEAD_SIZE
    allowed = causal(rows)
    for group in range(KEY_VALUE_HEADS):
        row_ref[group : group + 1, :] = jnp.sum(
            stacked_heads(do_ref, group).astype(f32) * stacked_heads(att_ref, group).astype(f32),
            axis=0,
            keepdims=True,
        )

    def one(group, kv_ref, dkv_ref, own):
        queries = stacked_heads(q_ref, group)
        d_out = stacked_heads(do_ref, group)
        keys = key_block(kv_ref, group)
        scores = nn(keys.T, queries)
        if own:
            scores = jnp.where(allowed, scores, masked)
        probs = jnp.exp(scores - lse_ref[group : group + 1, :])
        d_probs = nn(value_block(kv_ref, group).T, d_out)
        d_scores = (probs * (d_probs - row_ref[group : group + 1, :])).astype(bf16)
        dkv_ref[group * HEAD_SIZE : (group + 1) * HEAD_SIZE, :] = nt(queries, d_scores).astype(bf16)
        dkv_ref[key_width + group * HEAD_SIZE : key_width + (group + 1) * HEAD_SIZE, :] = nt(
            d_out, probs.astype(bf16)
        ).astype(bf16)
        moved = nn(keys, d_scores)
        if own:
            acc_ref[group] = moved
        else:
            acc_ref[group] += moved

    for group in range(KEY_VALUE_HEADS):
        one(group, kv0_ref, keep_ref.at[0], True)
    for i, kv_ref in enumerate((kv1_ref, kv2_ref, kv3_ref)):
        kvs_ref[i] = kv_ref[...]

    @pl.loop(0, 3)
    def _(member):
        kv_ref, dkv_ref = kvs_ref.at[member], dkvs_ref.at[member]

        @pl.when(visible_ref[member + 1] == 1)
        def _():
            for group in range(KEY_VALUE_HEADS):
                one(group, kv_ref, dkv_ref, False)

        @pl.when(visible_ref[member + 1] == 0)
        def _():
            dkv_ref[...] = jnp.zeros(dkv_ref.shape, bf16)

    send_ref[0] = dkvs_ref[0]
    keep_ref[1] = dkvs_ref[1]
    send_ref[1] = dkvs_ref[2]
    cos, sin = cos_ref[...], sin_ref[...]
    for group in range(KEY_VALUE_HEADS):
        for j in range(SHARING):
            low = (group * SHARING + j) * HEAD_SIZE
            lanes = slice(j * rows, (j + 1) * rows)
            first = acc_ref[group, :HALF, lanes] * score_scale
            second = acc_ref[group, HALF:, lanes] * score_scale
            dq_ref[low : low + HALF, :] = (first * cos + second * sin).astype(bf16)
            dq_ref[low + HALF : low + HEAD_SIZE, :] = (second * cos - first * sin).astype(bf16)


def attend_back(visible, q, d_out, att_t, lse, cos, sin, kvs):
    width, rows = q.shape
    key_rows = kvs[0].shape[0]
    lanes = SHARING * rows
    return pl.pallas_call(
        attend_back_kernel,
        out_shape=(shape((width, rows), bf16),) + (shape((2, key_rows, rows), bf16),) * 2,
        in_specs=[in_smem()] + [in_vmem()] * 10,
        out_specs=(in_vmem(),) * 3,
        scratch_shapes=[
            pltpu.VMEM((KEY_VALUE_HEADS, HEAD_SIZE, lanes), f32),
            pltpu.VMEM((KEY_VALUE_HEADS, lanes), f32),
            pltpu.VMEM((3, key_rows, rows), bf16),
            pltpu.VMEM((3, key_rows, rows), bf16),
        ],
        compiler_params=params(),
        cost_estimate=cost(2 * rows * width * 4 * rows * 10, 10 * width * rows * 2),
        name="attend_back",
    )(visible, q, d_out, att_t, lse, cos, sin, *kvs)


def leave_kernel(
    h_ref,
    dmid_ref,
    dq_ref,
    own_ref,
    got_ref,
    gain_ref,
    cos_ref,
    sin_ref,
    w_ref,
    g_ref,
    dqkv_ref,
    dgain_ref,
    turned_ref,
):
    width, rows = dq_ref.shape
    key_width = own_ref.shape[0] // 2
    wide = turned_ref.shape[0]
    cos, sin = cos_ref[...], sin_ref[...]
    turned_ref[:width, :] = dq_ref[...]
    summed = own_ref[...].astype(f32) + got_ref[...].astype(f32)
    for head in range(KEY_VALUE_HEADS):
        low = head * HEAD_SIZE
        first = summed[low : low + HALF]
        second = summed[low + HALF : low + HEAD_SIZE]
        base = width + low
        turned_ref[base : base + HALF, :] = (first * cos + second * sin).astype(bf16)
        turned_ref[base + HALF : base + HEAD_SIZE, :] = (second * cos - first * sin).astype(bf16)
    turned_ref[width + key_width : width + 2 * key_width, :] = summed[key_width:].astype(bf16)
    turned_ref[width + 2 * key_width :, :] = jnp.zeros((wide - width - 2 * key_width, rows), bf16)
    d_mixed = turned_ref[...].T
    dqkv_ref[...] = d_mixed
    d_normed = nt(d_mixed, w_ref[:, :wide])
    hidden = h_ref[...]
    factor = inverse_rms(hidden)
    unit = hidden * factor
    dgain_ref[...] = jnp.sum(d_normed * unit, axis=0, keepdims=True)
    scaled = d_normed * gain_ref[...]
    grad = dmid_ref[...] + factor * (
        scaled - unit * jnp.mean(scaled * unit, axis=-1, keepdims=True)
    )
    g_ref[...] = grad if g_ref.dtype == f32 else grad.T.astype(bf16)


def leave(hidden, d_middle, dq, own, got, gain, cos, sin, weights_a):
    rows, width = hidden.shape
    key_width = KEY_VALUE_HEADS * HEAD_SIZE
    wide = width + 2 * key_width + HEAD_SIZE
    return pl.pallas_call(
        leave_kernel,
        out_shape=(
            shape((rows, width), f32),
            shape((rows, wide), bf16),
            shape((1, width), f32),
        ),
        in_specs=[in_vmem()] * 9,
        out_specs=(in_vmem(),) * 3,
        scratch_shapes=[pltpu.VMEM((wide, rows), bf16)],
        compiler_params=params(),
        cost_estimate=cost(2 * rows * width * wide, width * wide * 2 + rows * width * 14),
        name="leave",
    )(hidden, d_middle, dq, own, got, gain, cos, sin, kept(weights_a))


def grad_parts(place_ref, right, keep_ref, send_ref, xt_ref):
    block, step = keep_ref.shape[2:]
    core, chip, quarter = place_ref[0], place_ref[1], place_ref[2]
    for part in range(4):
        columns = right(part * step, (part + 1) * step)
        for away in range(2):
            for out_ref, which in ((keep_ref, core), (send_ref, 1 - core)):
                start = pl.multiple_of((2 * (chip ^ away) + which) * block, 16)
                out_ref[away, part ^ quarter] = nn(
                    xt_ref[pl.ds(start, block), :], columns
                ).astype(bf16)


def feed_back_gate_kernel(*refs):
    (place_ref, g_ref, middle_ref, gating_ref, upward_ref, gain_ref, nf2_ref, nf_ref, dgu2_ref,
     a_ref, gu_hbm, dn_ref, dmid_ref, gm_ref, do_ref, dgain_ref, keep_ref, send_ref, keep2_ref,
     send2_ref, gb_ref, dgu_ref, sum_ref, xt_ref, gu_ref, gu_sems) = refs
    feed_back_kernel(
        g_ref, middle_ref, gating_ref, upward_ref, gain_ref, a_ref, gu_hbm, dn_ref, gb_ref, dgu_ref,
        dmid_ref, gm_ref, do_ref, dgain_ref, sum_ref, gu_ref, gu_sems,
    )

    rows = nf_ref.shape[0]
    ffn = gating_ref.shape[1]
    xt_ref[:, :rows] = nf2_ref[...].T
    xt_ref[:, rows:] = nf_ref[...].T
    for base, out_refs in ((0, (keep_ref, send_ref)), (ffn, (keep2_ref, send2_ref))):

        def right(low, high, base=base):
            return jnp.concatenate(
                [dgu2_ref[:, base + low : base + high], dgu_ref[:, base + low : base + high]], axis=0
            )

        grad_parts(place_ref, right, *out_refs, xt_ref)


def feed_back_gate(place, grad, middle, gating, upward, gain, nf2, nf, dgu2, weights):
    rows, width = grad.shape
    weights_a, weights_gu, weights_dn = weights
    ffn = weights_dn.shape[1]
    wo_wide = width + HEAD_SIZE
    return pl.pallas_call(
        feed_back_gate_kernel,
        out_shape=(
            shape((rows, width), f32),
            shape((rows, wo_wide), bf16),
            shape((width, rows), bf16),
            shape((1, width), f32),
        )
        + (shape((2, 4, width // 4, ffn // 4), bf16),) * 4,
        in_specs=[in_smem()] + [in_vmem()] * 9 + [anywhere(), in_vmem()],
        out_specs=(in_vmem(),) * 8,
        scratch_shapes=[
            pltpu.VMEM((rows, width), bf16),
            pltpu.VMEM((rows, 2 * ffn), bf16),
            pltpu.VMEM((rows, width), f32),
            pltpu.VMEM((width, 2 * rows), bf16),
            pltpu.VMEM((width, 2 * ffn), bf16),
            pltpu.SemaphoreType.DMA((4,)),
        ],
        compiler_params=params(FFN_MEBIBYTES),
        cost_estimate=cost(2 * rows * width * (8 * ffn), 3 * width * ffn * 2 + rows * ffn * 8),
        name="feed_back_gate",
    )(place, grad, middle, gating, upward, gain, nf2, nf, dgu2, kept(weights_a), in_hbm(weights_gu),
      kept(weights_dn))


def leave_mixed_kernel(*refs):
    (place_ref, h_ref, dmid_ref, dq_ref, own_ref, got_ref, gain_ref, cos_ref, sin_ref, n1_ref, n2_ref,
     d1_ref, a1_ref, a2_ref, m1_ref, m2_ref, attention_gain_ref, ffn_gain_ref, ffn_gain2_ref, w_ref,
     g_ref, keep_ref, send_ref, d2_ref, dgain_ref, turned_ref, nt_ref, at_ref, gains_ref) = refs
    leave_kernel(
        h_ref, dmid_ref, dq_ref, own_ref, got_ref, gain_ref, cos_ref, sin_ref, w_ref, g_ref, d2_ref,
        dgain_ref, turned_ref,
    )
    gains = (attention_gain_ref[...] + dgain_ref[...], ffn_gain_ref[...] + ffn_gain2_ref[...])
    attention_grad_kernel(
        place_ref, n1_ref, n2_ref, d1_ref, d2_ref, a1_ref, a2_ref, m1_ref, m2_ref, gains, keep_ref,
        send_ref, nt_ref, at_ref, gains_ref,
    )


def leave_mixed(
    place, hidden, d_middle, dq, own, got, gain, cos, sin, normed, dqkv2, att, gm, gain_grads, weights_a
):
    rows, width = hidden.shape
    key_width = KEY_VALUE_HEADS * HEAD_SIZE
    wide = width + 2 * key_width + HEAD_SIZE
    block = width // 4 + GAIN_ROWS
    columns = 2 * width + 2 * key_width
    return pl.pallas_call(
        leave_mixed_kernel,
        out_shape=(shape((width, rows), bf16),)
        + (shape((2, 4, block, columns // 4), bf16),) * 2,
        in_specs=[in_smem()] + [in_vmem()] * 19,
        out_specs=(in_vmem(),) * 3,
        scratch_shapes=[
            pltpu.VMEM((rows, wide), bf16),
            pltpu.VMEM((1, width), f32),
            pltpu.VMEM((wide, rows), bf16),
            pltpu.VMEM((width, 2 * rows), bf16),
            pltpu.VMEM((width, 2 * rows), bf16),
            pltpu.VMEM((GAIN_ROWS, columns), f32),
        ],
        compiler_params=params(),
        cost_estimate=cost(6 * rows * width * wide, width * wide * 2 + rows * width * 14),
        name="leave_mixed",
    )(place, hidden, d_middle, dq, own, got, gain, cos, sin, *normed, dqkv2, *att, *gm, *gain_grads,
      kept(weights_a))


def down_grad_kernel(place_ref, g2_ref, g_ref, inner2_ref, inner_ref, keep_ref, send_ref, gt_ref):
    rows = g2_ref.shape[0]
    height, step = keep_ref.shape[2:]
    gt_ref[:, :rows] = g2_ref[...].T
    gt_ref[:, rows:] = g_ref[...].astype(bf16).T
    core, chip, quarter = place_ref[0], place_ref[1], place_ref[2]
    for away in range(2):
        for out_ref, which in ((keep_ref, core), (send_ref, 1 - core)):
            columns = pl.ds(pl.multiple_of((2 * (chip ^ away) + which) * step, 128), step)
            right = jnp.concatenate([inner2_ref[:, columns], inner_ref[:, columns]], axis=0)
            for part in range(4):
                out_ref[away, part ^ quarter] = nn(
                    gt_ref[part * height : (part + 1) * height, :], right
                ).astype(bf16)


def down_grad_parts(place, g2, g, inner2, inner):
    rows, width = g.shape
    ffn = inner.shape[1]
    return pl.pallas_call(
        down_grad_kernel,
        out_shape=(shape((2, 4, width // 4, ffn // 4), bf16),) * 2,
        in_specs=[in_smem()] + [in_vmem()] * 4,
        out_specs=(in_vmem(),) * 2,
        scratch_shapes=[pltpu.VMEM((width, 2 * rows), bf16)],
        compiler_params=params(),
        cost_estimate=cost(4 * rows * width * ffn, width * ffn * 2),
        name="down_grad",
    )(place, in_hbm(g2), g, in_hbm(inner2), in_hbm(inner))


def attention_grad_kernel(
    place_ref, n1_ref, n2_ref, d1_ref, d2_ref, a1_ref, a2_ref, m1_ref, m2_ref, gains,
    keep_ref, send_ref, nt_ref, at_ref, gains_ref,
):
    rows = n1_ref.shape[0]
    block = n1_ref.shape[1] // 4
    wide = d1_ref.shape[1]
    edge = wide - 128
    step = keep_ref.shape[3]
    nt_ref[:, :rows] = n1_ref[...].T
    nt_ref[:, rows:] = n2_ref[...].T
    at_ref[:, :rows] = a1_ref[...].T
    at_ref[:, rows:] = a2_ref[...].T
    half = GAIN_ROWS // 2
    gains_ref[...] = jnp.zeros_like(gains_ref)
    for i, gain in enumerate(gains):
        gains_ref[i * half : (i + 1) * half, : gain.shape[1]] = jnp.broadcast_to(
            gain, (half, gain.shape[1])
        )
    core, chip, quarter = place_ref[0], place_ref[1], place_ref[2]
    d_mixed = jnp.concatenate([d1_ref[...], d2_ref[...]], axis=0)
    d_out = jnp.concatenate([m1_ref[...], m2_ref[...]], axis=0)
    for away in range(2):
        for out_ref, which in ((keep_ref, core), (send_ref, 1 - core)):
            member = 2 * (chip ^ away) + which
            start = pl.multiple_of(member * block, 16)
            normed = nt_ref[pl.ds(start, block), :]
            attended = at_ref[pl.ds(start, block), :]
            for part in range(4):
                low, high = part * step, (part + 1) * step
                pieces = []
                if low < edge:
                    pieces.append(nn(normed, d_mixed[:, low : min(high, edge)]))
                if low <= edge < high:
                    pieces.append(nn(normed, d_mixed[:, edge:]) + nn(attended, d_out[:, :128]))
                if high > wide:
                    base = wide - 128
                    pieces.append(nn(attended, d_out[:, max(low, wide) - base : high - base]))
                piece = pieces[0] if len(pieces) == 1 else jnp.concatenate(pieces, axis=1)
                out_ref[away, part ^ quarter, :block, :] = piece.astype(bf16)
                out_ref[away, part ^ quarter, block:, :] = gains_ref[:, low:high].astype(bf16)


def finish_kernel(place_ref, p0_ref, p1_ref, p2_ref, p3_ref, out_ref):
    part = pl.program_id(0)
    for i, ref in enumerate((p0_ref, p1_ref, p2_ref, p3_ref)):

        @pl.when(part == i)
        def _(ref=ref):
            out_ref[...] = ref[...].astype(f32)


def finish(place, pieces, by_rows):
    height, step = pieces[0].shape
    whole = pl.BlockSpec((height, step), lambda i, place: (0, 0))
    if by_rows:
        dims, index = (4 * height, step), lambda i, place: (i ^ place[2], 0)
    else:
        dims, index = (height, 4 * step), lambda i, place: (0, i ^ place[2])
    return pl.pallas_call(
        finish_kernel,
        grid_spec=pltpu.PrefetchScalarGridSpec(
            num_scalar_prefetch=1,
            grid=(4,),
            in_specs=[whole] * 4,
            out_specs=pl.BlockSpec((height, step), index),
        ),
        out_shape=shape(dims, f32),
        compiler_params=params(),
        cost_estimate=cost(0, 24 * height * step),
        name="finish",
    )(place, *pieces)


def finish_mixed_kernel(
    place_ref, p0_ref, p1_ref, p2_ref, p3_ref, query_ref, key_ref, value_ref, out_ref, gain_ref,
    mixed_ref,
):
    quarter = place_ref[2]
    block, width = query_ref.shape
    key_width = key_ref.shape[0]
    step = p0_ref.shape[1]
    for i, ref in enumerate((p0_ref, p1_ref, p2_ref, p3_ref)):
        start = pl.multiple_of((quarter ^ i) * step, 128)
        mixed_ref[:, pl.ds(start, step)] = ref[...].astype(f32)
    first_end = width + key_width
    second_end = first_end + key_width
    query_ref[...] = mixed_ref[:block, :width]
    key_ref[...] = mixed_ref[:block, width:first_end].T
    value_ref[...] = mixed_ref[:block, first_end:second_end].T
    out_ref[...] = mixed_ref[:block, second_end:]
    gain_ref[...] = mixed_ref[block:, : gain_ref.shape[1]]


def finish_mixed(place, pieces, width, key_width):
    height, step = pieces[0].shape
    block = height - GAIN_ROWS
    return pl.pallas_call(
        finish_mixed_kernel,
        out_shape=(
            shape((block, width), f32),
            shape((key_width, block), f32),
            shape((key_width, block), f32),
            shape((block, width), f32),
            shape((GAIN_ROWS, width + HEAD_SIZE), f32),
        ),
        in_specs=[in_smem()] + [in_vmem()] * 4,
        out_specs=(in_vmem(),) * 5,
        scratch_shapes=[pltpu.VMEM((height, 4 * step), f32)],
        compiler_params=params(),
        cost_estimate=cost(0, 24 * height * step),
        name="finish_mixed",
    )(place, *pieces)


def flip(value, axis_name, distance):
    size = lax.axis_size(axis_name)
    return lax.ppermute(value, axis_name, [(i, i ^ distance) for i in range(size)])


def pick(condition, when_true, when_false):
    return jnp.where(condition, when_true, when_false)


def order_by(bit, own, other):
    return (pick(bit == 1, other, own), pick(bit == 1, own, other))


def exchange_kv(block):
    beside = flip(block, "fsdp", 1)
    across = flip(block, "fsdp", 2)
    diagonal = flip(across, "fsdp", 1)
    return (block, beside, across, diagonal)


def fold_kv(keep, send):
    got = flip(send, "fsdp", 1)
    return total(keep[0], got[0]), total(keep[1], got[1])


def return_kv(keep, send):
    own, across = fold_kv(keep, send)
    return own, flip(across, "fsdp", 2)


def total(*terms):
    result = terms[0].astype(f32)
    for term in terms[1:]:
        result = result + term.astype(f32)
    return result.astype(bf16)


class Order:
    def __init__(self, *token):
        self.token = token

    def tie(self, *values):
        tied = lax.optimization_barrier(self.token + values)[len(self.token) :]
        return tied[0] if len(tied) == 1 else tied

    def done(self, value):
        self.token = (value,)
        return value

    def done_all(self, *values):
        self.token = values
        return values


class Reduction:
    def __init__(self, order, keep, send):
        self.order = order
        self.keep = keep
        self.core = flip(order.tie(send), "fsdp", 1)

    def chip(self):
        self.core = self.order.tie(self.core)
        high = total(self.keep[1, 2:], self.core[1, 2:])
        low = total(self.keep[1, :2], self.core[1, :2])
        high, low = self.order.done_all(high, low)
        self.high = flip(high, "fsdp", 2)
        self.low = flip(low, "fsdp", 2)

    def first(self, both=False):
        if both:
            self.high, self.low = self.order.tie(self.high, self.low)
        else:
            self.high = self.order.tie(self.high)
        out = total(self.keep[0, 2:], self.core[0, 2:], self.high)
        self.got = flip(self.order.done(out), "dp", 1)

    def rest(self):
        self.low = self.order.done(self.order.tie(self.low))

    def second(self):
        self.got, self.low = self.order.tie(self.got, self.low)
        self.terms = (self.keep[0, :2], self.core[0, :2], self.low, self.got)
        self.got = flip(self.order.done(total(*[term[1] for term in self.terms])), "dp", 2)

    def third(self):
        size = lax.axis_size("dp")
        own = total(*[term[0] for term in self.terms], self.order.tie(self.got))
        distance = 4
        while 2 * distance < size:
            own = total(own, flip(own, "dp", distance))
            distance *= 2
        self.own = self.order.done(own)
        self.got = flip(own, "dp", distance) if distance < size else jnp.zeros_like(own)

    def back(self):
        self.own = self.order.done(total(self.own, self.order.tie(self.got)))
        self.beside = flip(self.own, "dp", 2)
        self.pieces = [self.own, self.beside, flip(self.own, "dp", 1)]

    def back_again(self):
        self.beside = self.order.done(self.order.tie(self.beside))
        self.pieces.append(flip(self.beside, "dp", 1))

    def end(self):
        return self.order.tie(*self.pieces)


def rotation(token_positions):
    frequency = rope_base ** (-jnp.arange(HALF, dtype=f32) / HALF)
    angles = frequency[:, None] * token_positions.astype(f32)[None, :]
    return jnp.cos(angles), jnp.sin(angles)


def body(
    tokens,
    cotangent,
    sequence_ids,
    span_position,
    attention_norm,
    query_weight,
    key_matrix,
    value_matrix,
    output_weight,
    feedforward_norm,
    gate_weight,
    up_weight,
    down_weight,
):
    rows, width = tokens.shape
    key_width = key_matrix.shape[1]
    ffn = gate_weight.shape[1]
    itself = lax.axis_index("fsdp")
    outer = lax.axis_index("dp")
    quarter = 2 * (outer % 2) + (outer // 2) % 2
    place = jnp.stack([itself % 2, itself // 2, quarter]).astype(jnp.int32)

    outer = lax.axis_index("dp")
    bits = jnp.stack([outer % 2, (outer // 2) % 2, itself]).astype(jnp.int32)
    packed, *mine = pack(
        bits, query_weight, key_matrix.T, value_matrix.T, output_weight, gate_weight, up_weight
    )
    down_t = down_weight.T
    half = width // 2
    mine.append(pick(outer % 2 == 1, down_t[half:], down_t[:half]))
    gains = jnp.stack([attention_norm, feedforward_norm], axis=0)
    gains = [flip(gains, "fsdp", distance) if distance else gains for distance in range(4)]
    mine = Order(*gains).tie(*mine)
    far = [flip(piece, "fsdp", 2) for piece in mine]
    shards = (packed, gate_weight, up_weight, down_t)
    near = [flip(shard, "fsdp", 1) for shard in shards]
    sequence_ids, span_position = Order(*mine).tie(sequence_ids, span_position)
    places = jnp.arange(rows, dtype=jnp.int32) + span_position[itself] * rows
    cos, sin = rotation(places)
    others = itself ^ jnp.arange(4)
    visible = (
        (sequence_ids[others] == sequence_ids[itself])
        & (span_position[others] <= span_position[itself])
    ).astype(jnp.int32)

    beside = order_by(itself % 2, gains[0], gains[1])
    away = order_by(itself % 2, gains[2], gains[3])
    chip = itself // 2 == 1
    gains = jnp.concatenate(
        [pick(chip, a, n) for a, n in zip(away, beside)]
        + [pick(chip, n, a) for a, n in zip(away, beside)],
        axis=1,
    ).astype(f32)
    attention_gain, ffn_gain = gains[:1], gains[1:]
    order = Order(cos, sin, visible, attention_gain, ffn_gain)
    share = ((1, 0), (1, 0), (2, 1), (1, 0))

    def shared(i):
        got = order.done(order.tie(far[i]))
        return got, flip(got, "dp", share[i][0])

    def gathered(i, got, other):
        return [shards[i], near[i], got, other, flip(got, "fsdp", 1), flip(other, "fsdp", 1)]

    shared_a = shared(0)
    order.done_all(*order.tie(*shared_a))
    shared_gate = shared(1)
    sources_a = gathered(0, *shared_a)
    order.done_all(*order.tie(*near), *sources_a)
    tokens_t = order.tie(tokens.T)
    hidden, normed, q, kv, weights_a = enter_first(
        bits, tokens_t, attention_gain, cos, sin, shared_plan(0, 0, 0), tuple(sources_a)
    )
    order.done(kv)
    shared_up = shared(2)
    shared_gate = order.done_all(*order.tie(*shared_gate))
    kvs = exchange_kv(kv)
    shared_down = shared(3)
    order.done_all(*order.tie(*shared_up))
    sources_gu = gathered(1, *shared_gate) + gathered(2, *shared_up)
    sources_dn = gathered(3, *order.tie(*shared_down))
    plan_gu = shared_plan(0, 0, 0) + shared_plan(6, ffn, 1)
    plan_dn = shared_plan(0, None, 0)
    finished, att, att_t, lse, middle, nf, gating, upward, inner, weights_gu, weights_dn = forward_block(
        visible, bits, hidden, q, kvs, ffn_gain, weights_a, tuple(sources_gu), tuple(sources_dn),
        (plan_gu, plan_dn),
    )
    weights = (weights_a, weights_gu, weights_dn)
    saved = [(hidden, normed, q, kvs, att, att_t, lse, middle, nf, gating, upward, inner)]
    hidden = finished
    normed, q, kv = enter(hidden, attention_gain, cos, sin, weights_a)
    kvs = exchange_kv(kv)
    activations, att, att_t, lse, middle, nf, gating, upward, inner = forward_block(
        visible, bits, hidden, q, kvs, ffn_gain, weights_a, (weights_gu,), (weights_dn,)
    )
    saved.append((hidden, normed, q, kvs, att, att_t, lse, middle, nf, gating, upward, inner))

    hidden, normed2, q, kvs, att2, att_t, lse, middle, nf2, gating, upward, inner2 = saved[1]
    gb2, dgu2, d_middle, gm2, d_out, ffn_gain_grad2 = feed_back(
        cotangent.T, middle, gating, upward, ffn_gain, weights
    )
    dq, *dkvs = attend_back(visible, q, d_out, att_t, lse, cos, sin, kvs)
    own, got = return_kv(*dkvs)
    grad, dqkv2, attention_gain_grad2 = leave(
        hidden, d_middle, dq, own, got, attention_gain, cos, sin, weights_a
    )

    hidden, normed, q, kvs, att, att_t, lse, middle, nf, gating, upward, inner = saved[0]
    order = Order(grad)
    down = Reduction(order, *down_grad_parts(place, gb2, grad, inner2, inner))
    down.chip()
    d_middle, gm, d_out, ffn_gain_grad, *rest = feed_back_gate(
        place, order.tie(grad), middle, gating, upward, ffn_gain, nf2, nf, dgu2, weights
    )
    order.done(d_middle)
    down.first()
    gate = Reduction(order, *rest[:2])
    gate.chip()
    down.rest()
    up = Reduction(order, *rest[2:])
    dq, *dkvs = attend_back(visible, order.tie(q), d_out, att_t, lse, cos, sin, kvs)
    order.done(dq)
    gate.first()
    down.second()
    own, across = fold_kv(*order.tie(*dkvs))
    order.done(across)
    gate.rest()
    down.third()
    across = order.tie(across)
    got = order.done(order.tie(flip(across, "fsdp", 2)))
    gate.second()
    up.chip()
    d_middle = order.tie(d_middle)
    grad, *mixed = leave_mixed(
        place,
        hidden,
        d_middle,
        dq,
        own,
        got,
        attention_gain,
        cos,
        sin,
        (normed2, normed),
        dqkv2,
        (att2, att),
        (gm2, gm),
        (attention_gain_grad2, ffn_gain_grad2, ffn_gain_grad),
        weights_a,
    )
    order.done(grad)
    up.first()
    down.back()
    gate.third()
    mixed = Reduction(order, *mixed)
    mixed.chip()
    up.second()
    down.back_again()
    down_grad = order.done(finish(place, down.end(), True))
    mixed.first()
    gate.back()
    up.third()
    mixed.rest()
    mixed.second()
    gate.back_again()
    up.back()
    mixed.third()
    gate_grad = order.done(finish(place, gate.end(), False))
    up.back_again()
    up_grad = order.done(finish(place, up.end(), False))
    mixed.back()
    mixed.back_again()
    query_grad, key_grad, value_grad, output_grad, gain_grads = finish_mixed(
        place, mixed.end(), width, key_width
    )
    shard_rows = attention_norm.shape[0]
    gain_grads = lax.dynamic_slice_in_dim(gain_grads, itself * shard_rows, shard_rows, axis=1)
    return (
        activations.T,
        grad.T,
        gain_grads[0],
        query_grad,
        key_grad.T,
        value_grad.T,
        output_grad,
        gain_grads[GAIN_ROWS // 2],
        gate_grad,
        up_grad,
        down_grad.T,
    )


def solution(mesh):
    return jax.shard_map(
        body,
        mesh=mesh,
        in_specs=(
            P(("dp", "fsdp"), None),
            P(("dp", "fsdp"), None),
            P("dp"),
            P("dp"),
            P("fsdp"),
            P("fsdp", None),
            P("fsdp", None),
            P("fsdp", None),
            P("fsdp", None),
            P("fsdp"),
            P("fsdp", None),
            P("fsdp", None),
            P("fsdp", None),
        ),
        out_specs=(
            P(("dp", "fsdp"), None),
            P(("dp", "fsdp"), None),
            P("fsdp"),
            P("fsdp", None),
            P("fsdp", None),
            P("fsdp", None),
            P("fsdp", None),
            P("fsdp"),
            P("fsdp", None),
            P("fsdp", None),
            P("fsdp", None),
        ),
        check_vma=False,
    )
```

```python
import functools

import jax
import jax.numpy as jnp
from jax import lax
from jax.experimental import pallas as pl
from jax.experimental.pallas import tpu as pltpu
from jax.sharding import PartitionSpec as P

QUERY_HEADS = 15
KEY_VALUE_HEADS = 5
HEAD_SIZE = 64
SHARING = QUERY_HEADS // KEY_VALUE_HEADS
HALF = HEAD_SIZE // 2

epsilon = 1e-05
rope_base = 10000.0
masked = -1e30
score_scale = HEAD_SIZE ** (-0.5)

bf16 = jnp.bfloat16
f32 = jnp.float32
GAIN_ROWS = 16
FFN_MEBIBYTES = 26


def nn(left, right):
    return jnp.dot(left, right, preferred_element_type=f32)


def nt(left, right):
    return lax.dot_general(left, right, (((1,), (1,)), ((), ())), preferred_element_type=f32)


def in_vmem():
    return pl.BlockSpec(memory_space=pltpu.VMEM)


def in_smem():
    return pl.BlockSpec(memory_space=pltpu.SMEM)


def anywhere():
    return pl.BlockSpec(memory_space=pl.ANY)


def params(mebibytes=14):
    return pltpu.CompilerParams(vmem_limit_bytes=mebibytes * 1024 * 1024)


def shape(dims, dtype):
    return jax.ShapeDtypeStruct(dims, dtype)


def kept(array):
    return pltpu.with_memory_space_constraint(array, pltpu.VMEM)


def in_hbm(array):
    return pltpu.with_memory_space_constraint(array, pltpu.HBM)


def cost(flops, bytes_accessed):
    return pl.CostEstimate(flops=int(flops), bytes_accessed=int(bytes_accessed), transcendentals=0)


def inverse_rms(hidden):
    return lax.rsqrt(jnp.mean(hidden * hidden, axis=-1, keepdims=True) + epsilon)


def pack_kernel(
    bits_ref, query_hbm, key_hbm, value_hbm, out_hbm, gate_hbm, up_hbm, packed_hbm, mine_hbm,
    mine_gate_hbm, mine_up_hbm, query_ref, key_ref, value_ref, out_ref, gate_ref, up_ref, packed_ref,
    mine_ref, sems,
):
    half = gate_ref.shape[1]
    loads = [
        pltpu.make_async_copy(source, target, sems.at[i])
        for i, (source, target) in enumerate(
            (
                (query_hbm, query_ref),
                (key_hbm, key_ref),
                (value_hbm, value_ref),
                (out_hbm, out_ref),
                (gate_hbm.at[:, pl.ds(pl.multiple_of(bits_ref[0] * half, 128), half)], gate_ref),
                (up_hbm.at[:, pl.ds(pl.multiple_of(bits_ref[1] * half, 128), half)], up_ref),
            )
        )
    ]
    for load in loads:
        load.start()
    for load in loads[:4]:
        load.wait()
    packed_ref[...] = jnp.concatenate(
        [
            query_ref[...].astype(f32),
            key_ref[...].astype(f32).T,
            value_ref[...].astype(f32).T,
            out_ref[...].astype(f32),
        ],
        axis=1,
    ).astype(bf16)
    wide = mine_ref.shape[1]
    mine_ref[...] = packed_ref[:, pl.ds(pl.multiple_of(bits_ref[0] * wide, 128), wide)]
    for load in loads[4:]:
        load.wait()
    stores = [
        pltpu.make_async_copy(source, target, sems.at[i])
        for i, (source, target) in enumerate(
            (
                (mine_ref, mine_hbm),
                (gate_ref, mine_gate_hbm),
                (up_ref, mine_up_hbm),
                (packed_ref, packed_hbm),
            )
        )
    ]
    for store in stores:
        store.start()
    for store in stores:
        store.wait()


def pack(bits, query, key_t, value_t, out, gate, up):
    rows, width = query.shape
    columns = 2 * width + 2 * key_t.shape[0]
    ffn = gate.shape[1]
    return pl.pallas_call(
        pack_kernel,
        out_shape=(
            pltpu.HBM((rows, columns), bf16),
            pltpu.HBM((rows, columns // 2), bf16),
            pltpu.HBM((rows, ffn // 2), bf16),
            pltpu.HBM((rows, ffn // 2), bf16),
        ),
        in_specs=[in_smem()] + [anywhere()] * 6,
        out_specs=(anywhere(),) * 4,
        scratch_shapes=[
            pltpu.VMEM((rows, width), bf16),
            pltpu.VMEM(key_t.shape, bf16),
            pltpu.VMEM(value_t.shape, bf16),
            pltpu.VMEM((rows, width), bf16),
            pltpu.VMEM((rows, ffn // 2), bf16),
            pltpu.VMEM((rows, ffn // 2), bf16),
            pltpu.VMEM((rows, columns), bf16),
            pltpu.VMEM((rows, columns // 2), bf16),
            pltpu.SemaphoreType.DMA((6,)),
        ],
        compiler_params=params(),
        cost_estimate=cost(0, 8 * rows * columns),
        name="pack",
    )(bits, *[in_hbm(part) for part in (query, key_t, value_t, out, gate, up)])


def piece_copies(plan, bits_ref, sources, target_ref, sems):
    me = bits_ref[2]
    copies = []
    for i, (which, member, column, part, bit) in enumerate(plan):
        source = sources[which]
        height, width = source.shape
        if column is None:
            turned = pl.ds(pl.multiple_of((me ^ member) * width, 128), width)
            if part is None:
                rows = pl.ds(0, height)
            else:
                rows = pl.ds(pl.multiple_of((bits_ref[bit] ^ part) * height, 16), height)
            target = target_ref.at[rows, turned]
        else:
            rows = pl.ds(pl.multiple_of((me ^ member) * height, 16), height)
            if part is None:
                columns = pl.ds(column, width)
            else:
                columns = pl.ds(
                    pl.multiple_of(column + (bits_ref[bit] ^ part) * width, 128), width
                )
            target = target_ref.at[rows, columns]
        copies.append(pltpu.make_async_copy(source, target, sems.at[i]))
    return copies


def shared_plan(first, column, bit):
    return (
        (first, 0, column, None, bit),
        (first + 1, 1, column, None, bit),
        (first + 2, 2, column, 0, bit),
        (first + 3, 2, column, 1, bit),
        (first + 4, 3, column, 0, bit),
        (first + 5, 3, column, 1, bit),
    )


def enter_body(hidden, gain_ref, cos_ref, sin_ref, ready, normed_ref, q_ref, kv_ref, w_ref):
    width = hidden.shape[1]
    key_width = kv_ref.shape[0] // 2
    mixed_width = width + key_width
    wide = width + 2 * key_width + HEAD_SIZE
    normed = (hidden * inverse_rms(hidden) * gain_ref[...]).astype(bf16)
    normed_ref[...] = normed
    cos, sin = cos_ref[...], sin_ref[...]
    ready()
    mixed = nn(normed, w_ref[:, :mixed_width]).T
    for head in range(QUERY_HEADS + KEY_VALUE_HEADS):
        low = head * HEAD_SIZE
        first = mixed[low : low + HALF]
        second = mixed[low + HALF : low + HEAD_SIZE]
        top = first * cos - second * sin
        bottom = second * cos + first * sin
        if head < QUERY_HEADS:
            q_ref[low : low + HALF, :] = (top * score_scale).astype(bf16)
            q_ref[low + HALF : low + HEAD_SIZE, :] = (bottom * score_scale).astype(bf16)
        else:
            low = low - width
            kv_ref[low : low + HALF, :] = top.astype(bf16)
            kv_ref[low + HALF : low + HEAD_SIZE, :] = bottom.astype(bf16)
    values = nn(normed, w_ref[:, mixed_width:wide]).T
    kv_ref[key_width:, :] = values[:key_width].astype(bf16)


def enter_first_kernel(plan, count, index_ref, h_ref, gain_ref, cos_ref, sin_ref, *refs):
    sources = refs[:count]
    hidden_ref, normed_ref, q_ref, kv_ref, w_ref, sems = refs[count:]
    copies = piece_copies(plan, index_ref, sources, w_ref, sems)
    for copy in copies:
        copy.start()
    hidden = h_ref[...].astype(f32).T
    hidden_ref[...] = hidden

    def ready():
        for copy in copies:
            copy.wait()

    enter_body(hidden, gain_ref, cos_ref, sin_ref, ready, normed_ref, q_ref, kv_ref, w_ref)


def enter_first(index, hidden_t, gain, cos, sin, plan, sources):
    width, rows = hidden_t.shape
    key_width = KEY_VALUE_HEADS * HEAD_SIZE
    columns = 2 * (width + key_width)
    return pl.pallas_call(
        functools.partial(enter_first_kernel, plan, len(sources)),
        out_shape=(
            shape((rows, width), f32),
            shape((rows, width), bf16),
            shape((width, rows), bf16),
            shape((2 * key_width, rows), bf16),
            pltpu.VMEM((width, columns), bf16),
        ),
        in_specs=[in_smem()] + [in_vmem()] * 4 + [anywhere()] * len(sources),
        out_specs=(in_vmem(),) * 5,
        scratch_shapes=[pltpu.SemaphoreType.DMA((len(plan),))],
        compiler_params=params(),
        cost_estimate=cost(4 * rows * width * width, width * columns * 4),
        name="enter_first",
    )(index, hidden_t, gain, cos, sin, *sources)


def enter_kernel(h_ref, gain_ref, cos_ref, sin_ref, w_ref, normed_ref, q_ref, kv_ref):
    enter_body(
        h_ref[...], gain_ref, cos_ref, sin_ref, lambda: None, normed_ref, q_ref, kv_ref, w_ref
    )


def enter(hidden, gain, cos, sin, weights_a):
    rows, width = hidden.shape
    key_width = KEY_VALUE_HEADS * HEAD_SIZE
    wide = width + 2 * key_width + HEAD_SIZE
    return pl.pallas_call(
        enter_kernel,
        out_shape=(
            shape((rows, width), bf16),
            shape((width, rows), bf16),
            shape((2 * key_width, rows), bf16),
        ),
        in_specs=[in_vmem()] * 5,
        out_specs=(in_vmem(),) * 3,
        compiler_params=params(),
        cost_estimate=cost(2 * rows * width * wide, width * wide * 2 + rows * width * 10),
        name="enter",
    )(hidden, gain, cos, sin, kept(weights_a))


def out_weight(a_ref):
    return a_ref[:, a_ref.shape[1] - a_ref.shape[0] - HEAD_SIZE :]


def stacked_heads(ref, group):
    parts = []
    for j in range(SHARING):
        low = (group * SHARING + j) * HEAD_SIZE
        parts.append(ref[low : low + HEAD_SIZE, :])
    return jnp.concatenate(parts, axis=1)


def key_block(ref, group):
    return ref[group * HEAD_SIZE : (group + 1) * HEAD_SIZE, :]


def value_block(ref, group):
    key_width = KEY_VALUE_HEADS * HEAD_SIZE
    return ref[key_width + group * HEAD_SIZE : key_width + (group + 1) * HEAD_SIZE, :]


def causal(rows):
    keys = lax.broadcasted_iota(jnp.int32, (rows, SHARING * rows), 0)
    queries = lax.broadcasted_iota(jnp.int32, (rows, SHARING * rows), 1) % rows
    return keys <= queries


def whole_copies(source_ref, target_ref, sems):
    parts = 4
    height = source_ref.shape[0] // parts
    return [
        pltpu.make_async_copy(
            source_ref.at[pl.ds(i * height, height), :],
            target_ref.at[pl.ds(i * height, height), :],
            sems.at[i],
        )
        for i in range(parts)
    ]


def forward_kernel(plans, counts, *refs):
    (visible_ref, bits_ref, h_ref, q_ref, kv0_ref, kv1_ref, kv2_ref, kv3_ref, gain_ref, a_ref) = refs[:10]
    gu_sources = refs[10 : 10 + counts[0]]
    dn_sources = refs[10 + counts[0] : 10 + counts[0] + counts[1]]
    refs = refs[10 + counts[0] + counts[1] :]
    (out_ref, att_ref, att_t_ref, lse_ref, middle_ref, nf_ref, gating_ref, upward_ref, inner_ref) = refs[:9]
    refs = refs[9:]
    gu_ref, gu_sems, dn_sems = refs[-3:]
    if plans is not None:
        gu_hbm, dn_ref = refs[:2]
        refs = refs[2:]
        gu_loads = piece_copies(plans[0], bits_ref, gu_sources, gu_ref, gu_sems)
        dn_loads = piece_copies(plans[1], bits_ref, dn_sources, dn_ref, dn_sems)
    else:
        (dn_ref,) = dn_sources
        gu_loads, dn_loads = whole_copies(gu_sources[0], gu_ref, gu_sems), []
    acc_ref, m_ref, l_ref, kvs_ref = refs[:4]
    rows, width = h_ref.shape
    ffn = inner_ref.shape[1]
    for load in gu_loads + dn_loads:
        load.start()

    allowed = causal(rows)
    for group in range(KEY_VALUE_HEADS):
        scores = nn(key_block(kv0_ref, group).T, stacked_heads(q_ref, group))
        scores = jnp.where(allowed, scores, masked)
        peak = jnp.max(scores, axis=0, keepdims=True)
        raised = jnp.exp(scores - peak)
        m_ref[group : group + 1, :] = peak
        l_ref[group : group + 1, :] = jnp.sum(raised, axis=0, keepdims=True)
        acc_ref[group] = nn(value_block(kv0_ref, group), raised.astype(bf16))
    for i, kv_ref in enumerate((kv1_ref, kv2_ref, kv3_ref)):
        kvs_ref[i] = kv_ref[...]

    @pl.loop(0, 3)
    def _(member):
        kv_ref = kvs_ref.at[member]

        @pl.when(visible_ref[member + 1] == 1)
        def _():
            for group in range(KEY_VALUE_HEADS):
                scores = nn(key_block(kv_ref, group).T, stacked_heads(q_ref, group))
                old = m_ref[group : group + 1, :]
                peak = jnp.maximum(old, jnp.max(scores, axis=0, keepdims=True))
                raised = jnp.exp(scores - peak)
                fade = jnp.exp(old - peak)
                m_ref[group : group + 1, :] = peak
                l_ref[group : group + 1, :] = l_ref[group : group + 1, :] * fade + jnp.sum(
                    raised, axis=0, keepdims=True
                )
                acc_ref[group] = acc_ref[group] * fade + nn(
                    value_block(kv_ref, group), raised.astype(bf16)
                )

    total = l_ref[...]
    lse_ref[...] = m_ref[...] + jnp.log(total)
    for group in range(KEY_VALUE_HEADS):
        mean = acc_ref[group] / total[group : group + 1, :]
        for j in range(SHARING):
            low = (group * SHARING + j) * HEAD_SIZE
            att_t_ref[low : low + HEAD_SIZE, :] = mean[:, j * rows : (j + 1) * rows].astype(bf16)
    attended = att_t_ref[...].T
    att_ref[...] = attended
    middle = h_ref[...] + nn(attended, out_weight(a_ref))[:, HEAD_SIZE:]
    middle_ref[...] = middle
    normed = (middle * inverse_rms(middle) * gain_ref[...]).astype(bf16)
    nf_ref[...] = normed
    for load in gu_loads:
        load.wait()
    gu_stores = whole_copies(gu_ref, gu_hbm, gu_sems) if plans is not None else []
    for store in gu_stores:
        store.start()
    step = 512
    for low in range(0, ffn, step):
        gating = nn(normed, gu_ref[:, low : low + step])
        upward = nn(normed, gu_ref[:, ffn + low : ffn + low + step])
        gating_ref[:, low : low + step] = gating.astype(bf16)
        upward_ref[:, low : low + step] = upward.astype(bf16)
        inner_ref[:, low : low + step] = (gating * jax.nn.sigmoid(gating) * upward).astype(bf16)
    for load in dn_loads:
        load.wait()
    finished = middle + nt(inner_ref[...], dn_ref[...])
    out_ref[...] = finished if plans is not None else finished.T.astype(bf16)
    for store in gu_stores:
        store.wait()


def forward_block(visible, index, hidden, q, kvs, gain, weights_a, gu, dn, plans=None):
    rows, width = hidden.shape
    ffn = gu[0].shape[1] if plans is not None else gu[0].shape[1] // 2
    lanes = SHARING * rows
    counts = (len(gu), len(dn))
    first = plans is not None
    whole = (pltpu.HBM((width, 2 * ffn), bf16), pltpu.VMEM((width, ffn), bf16))
    return pl.pallas_call(
        functools.partial(forward_kernel, plans, counts),
        out_shape=(
            shape((rows, width), f32) if first else shape((width, rows), bf16),
            shape((rows, width), bf16),
            shape((width, rows), bf16),
            shape((KEY_VALUE_HEADS, lanes), f32),
            shape((rows, width), f32),
            shape((rows, width), bf16),
            shape((rows, ffn), bf16),
            shape((rows, ffn), bf16),
            shape((rows, ffn), bf16),
        )
        + (whole if first else ()),
        in_specs=[in_smem()] * 2
        + [in_vmem()] * 8
        + [anywhere()] * counts[0]
        + [anywhere() if first else in_vmem()] * counts[1],
        out_specs=(in_vmem(),) * 9 + ((anywhere(), in_vmem()) if first else ()),
        scratch_shapes=[
            pltpu.VMEM((KEY_VALUE_HEADS, HEAD_SIZE, lanes), f32),
            pltpu.VMEM((KEY_VALUE_HEADS, lanes), f32),
            pltpu.VMEM((KEY_VALUE_HEADS, lanes), f32),
            pltpu.VMEM((3, *kvs[0].shape), bf16),
            pltpu.VMEM((width, 2 * ffn), bf16),
            pltpu.SemaphoreType.DMA((len(plans[0]) if first else 4,)),
            pltpu.SemaphoreType.DMA((len(plans[1]) if first else 1,)),
        ],
        compiler_params=params(FFN_MEBIBYTES),
        cost_estimate=cost(2 * rows * width * (4 * ffn), 3 * width * ffn * 2 + rows * ffn * 8),
        name="forward_first" if first else "forward_last",
    )(
        visible, index, hidden, q, *kvs, gain, kept(weights_a),
        *([*gu, *dn] if first else [in_hbm(gu[0]), kept(dn[0])]),
    )


def feed_back_kernel(
    g_ref,
    middle_ref,
    gating_ref,
    upward_ref,
    gain_ref,
    a_ref,
    gu_hbm,
    dn_ref,
    gb_ref,
    dgu_ref,
    dmid_ref,
    gm_ref,
    do_ref,
    dgain_ref,
    sum_ref,
    gu_ref,
    gu_sems,
):
    rows, width = middle_ref.shape
    ffn = gating_ref.shape[1]
    loads = whole_copies(gu_hbm, gu_ref, gu_sems)
    for load in loads:
        load.start()
    grad = g_ref[...] if g_ref.shape[0] == rows else g_ref[...].astype(f32).T
    short = grad.astype(bf16)
    gb_ref[...] = short
    step = 512
    for low in range(0, ffn, step):
        part = slice(low, low + step)
        behind = slice(ffn + low, ffn + low + step)
        d_inner = nn(short, dn_ref[:, part])
        gating = gating_ref[:, part].astype(f32)
        upward = upward_ref[:, part].astype(f32)
        gate = jax.nn.sigmoid(gating)
        d_gating = (d_inner * upward * (gate * (1.0 + gating * (1.0 - gate)))).astype(bf16)
        d_upward = (d_inner * (gating * gate)).astype(bf16)
        dgu_ref[:, part] = d_gating
        dgu_ref[:, behind] = d_upward
    for load in loads:
        load.wait()
    sum_ref[...] = nt(dgu_ref[...], gu_ref[...])
    d_normed = sum_ref[...]
    middle = middle_ref[...]
    factor = inverse_rms(middle)
    unit = middle * factor
    dgain_ref[...] = jnp.sum(d_normed * unit, axis=0, keepdims=True)
    scaled = d_normed * gain_ref[...]
    d_middle = grad + factor * (scaled - unit * jnp.mean(scaled * unit, axis=-1, keepdims=True))
    dmid_ref[...] = d_middle
    padded = jnp.concatenate(
        [jnp.zeros((rows, HEAD_SIZE), f32), d_middle], axis=1
    ).astype(bf16)
    gm_ref[...] = padded
    do_ref[...] = nt(padded, out_weight(a_ref)).T.astype(bf16)


def feed_back(grad, middle, gating, upward, gain, weights):
    rows, width = middle.shape
    weights_a, weights_gu, weights_dn = weights
    ffn = weights_dn.shape[1]
    wo_wide = width + HEAD_SIZE
    return pl.pallas_call(
        feed_back_kernel,
        out_shape=(
            shape((rows, width), bf16),
            shape((rows, 2 * ffn), bf16),
            shape((rows, width), f32),
            shape((rows, wo_wide), bf16),
            shape((width, rows), bf16),
            shape((1, width), f32),
        ),
        in_specs=[in_vmem()] * 6 + [anywhere(), in_vmem()],
        out_specs=(in_vmem(),) * 6,
        scratch_shapes=[
            pltpu.VMEM((rows, width), f32),
            pltpu.VMEM((width, 2 * ffn), bf16),
            pltpu.SemaphoreType.DMA((4,)),
        ],
        compiler_params=params(FFN_MEBIBYTES),
        cost_estimate=cost(2 * rows * width * (4 * ffn), 3 * width * ffn * 2 + rows * ffn * 8),
        name="feed_back",
    )(grad, middle, gating, upward, gain, kept(weights_a), in_hbm(weights_gu), kept(weights_dn))


def attend_back_kernel(
    visible_ref,
    q_ref,
    do_ref,
    att_ref,
    lse_ref,
    cos_ref,
    sin_ref,
    kv0_ref,
    kv1_ref,
    kv2_ref,
    kv3_ref,
    dq_ref,
    keep_ref,
    send_ref,
    acc_ref,
    row_ref,
    kvs_ref,
    dkvs_ref,
):
    rows = q_ref.shape[1]
    key_width = KEY_VALUE_HEADS * HEAD_SIZE
    allowed = causal(rows)
    for group in range(KEY_VALUE_HEADS):
        row_ref[group : group + 1, :] = jnp.sum(
            stacked_heads(do_ref, group).astype(f32) * stacked_heads(att_ref, group).astype(f32),
            axis=0,
            keepdims=True,
        )

    def one(group, kv_ref, dkv_ref, own):
        queries = stacked_heads(q_ref, group)
        d_out = stacked_heads(do_ref, group)
        keys = key_block(kv_ref, group)
        scores = nn(keys.T, queries)
        if own:
            scores = jnp.where(allowed, scores, masked)
        probs = jnp.exp(scores - lse_ref[group : group + 1, :])
        d_probs = nn(value_block(kv_ref, group).T, d_out)
        d_scores = (probs * (d_probs - row_ref[group : group + 1, :])).astype(bf16)
        dkv_ref[group * HEAD_SIZE : (group + 1) * HEAD_SIZE, :] = nt(queries, d_scores).astype(bf16)
        dkv_ref[key_width + group * HEAD_SIZE : key_width + (group + 1) * HEAD_SIZE, :] = nt(
            d_out, probs.astype(bf16)
        ).astype(bf16)
        moved = nn(keys, d_scores)
        if own:
            acc_ref[group] = moved
        else:
            acc_ref[group] += moved

    for group in range(KEY_VALUE_HEADS):
        one(group, kv0_ref, keep_ref.at[0], True)
    for i, kv_ref in enumerate((kv1_ref, kv2_ref, kv3_ref)):
        kvs_ref[i] = kv_ref[...]

    @pl.loop(0, 3)
    def _(member):
        kv_ref, dkv_ref = kvs_ref.at[member], dkvs_ref.at[member]

        @pl.when(visible_ref[member + 1] == 1)
        def _():
            for group in range(KEY_VALUE_HEADS):
                one(group, kv_ref, dkv_ref, False)

        @pl.when(visible_ref[member + 1] == 0)
        def _():
            dkv_ref[...] = jnp.zeros(dkv_ref.shape, bf16)

    send_ref[0] = dkvs_ref[0]
    keep_ref[1] = dkvs_ref[1]
    send_ref[1] = dkvs_ref[2]
    cos, sin = cos_ref[...], sin_ref[...]
    for group in range(KEY_VALUE_HEADS):
        for j in range(SHARING):
            low = (group * SHARING + j) * HEAD_SIZE
            lanes = slice(j * rows, (j + 1) * rows)
            first = acc_ref[group, :HALF, lanes] * score_scale
            second = acc_ref[group, HALF:, lanes] * score_scale
            dq_ref[low : low + HALF, :] = (first * cos + second * sin).astype(bf16)
            dq_ref[low + HALF : low + HEAD_SIZE, :] = (second * cos - first * sin).astype(bf16)


def attend_back(visible, q, d_out, att_t, lse, cos, sin, kvs):
    width, rows = q.shape
    key_rows = kvs[0].shape[0]
    lanes = SHARING * rows
    return pl.pallas_call(
        attend_back_kernel,
        out_shape=(shape((width, rows), bf16),) + (shape((2, key_rows, rows), bf16),) * 2,
        in_specs=[in_smem()] + [in_vmem()] * 10,
        out_specs=(in_vmem(),) * 3,
        scratch_shapes=[
            pltpu.VMEM((KEY_VALUE_HEADS, HEAD_SIZE, lanes), f32),
            pltpu.VMEM((KEY_VALUE_HEADS, lanes), f32),
            pltpu.VMEM((3, key_rows, rows), bf16),
            pltpu.VMEM((3, key_rows, rows), bf16),
        ],
        compiler_params=params(),
        cost_estimate=cost(2 * rows * width * 4 * rows * 10, 10 * width * rows * 2),
        name="attend_back",
    )(visible, q, d_out, att_t, lse, cos, sin, *kvs)


def leave_kernel(
    h_ref,
    dmid_ref,
    dq_ref,
    own_ref,
    got_ref,
    gain_ref,
    cos_ref,
    sin_ref,
    w_ref,
    g_ref,
    dqkv_ref,
    dgain_ref,
    turned_ref,
):
    width, rows = dq_ref.shape
    key_width = own_ref.shape[0] // 2
    wide = turned_ref.shape[0]
    cos, sin = cos_ref[...], sin_ref[...]
    turned_ref[:width, :] = dq_ref[...]
    summed = own_ref[...].astype(f32) + got_ref[...].astype(f32)
    for head in range(KEY_VALUE_HEADS):
        low = head * HEAD_SIZE
        first = summed[low : low + HALF]
        second = summed[low + HALF : low + HEAD_SIZE]
        base = width + low
        turned_ref[base : base + HALF, :] = (first * cos + second * sin).astype(bf16)
        turned_ref[base + HALF : base + HEAD_SIZE, :] = (second * cos - first * sin).astype(bf16)
    turned_ref[width + key_width : width + 2 * key_width, :] = summed[key_width:].astype(bf16)
    turned_ref[width + 2 * key_width :, :] = jnp.zeros((wide - width - 2 * key_width, rows), bf16)
    d_mixed = turned_ref[...].T
    dqkv_ref[...] = d_mixed
    d_normed = nt(d_mixed, w_ref[:, :wide])
    hidden = h_ref[...]
    factor = inverse_rms(hidden)
    unit = hidden * factor
    dgain_ref[...] = jnp.sum(d_normed * unit, axis=0, keepdims=True)
    scaled = d_normed * gain_ref[...]
    grad = dmid_ref[...] + factor * (
        scaled - unit * jnp.mean(scaled * unit, axis=-1, keepdims=True)
    )
    g_ref[...] = grad if g_ref.dtype == f32 else grad.T.astype(bf16)


def leave(hidden, d_middle, dq, own, got, gain, cos, sin, weights_a):
    rows, width = hidden.shape
    key_width = KEY_VALUE_HEADS * HEAD_SIZE
    wide = width + 2 * key_width + HEAD_SIZE
    return pl.pallas_call(
        leave_kernel,
        out_shape=(
            shape((rows, width), f32),
            shape((rows, wide), bf16),
            shape((1, width), f32),
        ),
        in_specs=[in_vmem()] * 9,
        out_specs=(in_vmem(),) * 3,
        scratch_shapes=[pltpu.VMEM((wide, rows), bf16)],
        compiler_params=params(),
        cost_estimate=cost(2 * rows * width * wide, width * wide * 2 + rows * width * 14),
        name="leave",
    )(hidden, d_middle, dq, own, got, gain, cos, sin, in_hbm(weights_a))


def grad_parts(place_ref, right, keep_ref, send_ref, xt_ref):
    block, step = keep_ref.shape[2:]
    core, chip, quarter = place_ref[0], place_ref[1], place_ref[2]
    for part in range(4):
        columns = right(part * step, (part + 1) * step)
        for away in range(2):
            for out_ref, which in ((keep_ref, core), (send_ref, 1 - core)):
                start = pl.multiple_of((2 * (chip ^ away) + which) * block, 16)
                out_ref[away, part ^ quarter] = nn(
                    xt_ref[pl.ds(start, block), :], columns
                ).astype(bf16)


def feed_back_gate_kernel(*refs):
    (place_ref, g_ref, middle_ref, gating_ref, upward_ref, gain_ref, nf2_ref, nf_ref, dgu2_ref,
     a_ref, gu_hbm, dn_ref, dmid_ref, gm_ref, do_ref, dgain_ref, keep_ref, send_ref, keep2_ref,
     send2_ref, gb_ref, dgu_ref, sum_ref, xt_ref, gu_ref, gu_sems) = refs
    feed_back_kernel(
        g_ref, middle_ref, gating_ref, upward_ref, gain_ref, a_ref, gu_hbm, dn_ref, gb_ref, dgu_ref,
        dmid_ref, gm_ref, do_ref, dgain_ref, sum_ref, gu_ref, gu_sems,
    )

    rows = nf_ref.shape[0]
    ffn = gating_ref.shape[1]
    xt_ref[:, :rows] = nf2_ref[...].T
    xt_ref[:, rows:] = nf_ref[...].T
    for base, out_refs in ((0, (keep_ref, send_ref)), (ffn, (keep2_ref, send2_ref))):

        def right(low, high, base=base):
            return jnp.concatenate(
                [dgu2_ref[:, base + low : base + high], dgu_ref[:, base + low : base + high]], axis=0
            )

        grad_parts(place_ref, right, *out_refs, xt_ref)


def feed_back_gate(place, grad, middle, gating, upward, gain, nf2, nf, dgu2, weights):
    rows, width = grad.shape
    weights_a, weights_gu, weights_dn = weights
    ffn = weights_dn.shape[1]
    wo_wide = width + HEAD_SIZE
    return pl.pallas_call(
        feed_back_gate_kernel,
        out_shape=(
            shape((rows, width), f32),
            shape((rows, wo_wide), bf16),
            shape((width, rows), bf16),
            shape((1, width), f32),
        )
        + (shape((2, 4, width // 4, ffn // 4), bf16),) * 4,
        in_specs=[in_smem()] + [in_vmem()] * 9 + [anywhere(), in_vmem()],
        out_specs=(in_vmem(),) * 8,
        scratch_shapes=[
            pltpu.VMEM((rows, width), bf16),
            pltpu.VMEM((rows, 2 * ffn), bf16),
            pltpu.VMEM((rows, width), f32),
            pltpu.VMEM((width, 2 * rows), bf16),
            pltpu.VMEM((width, 2 * ffn), bf16),
            pltpu.SemaphoreType.DMA((4,)),
        ],
        compiler_params=params(FFN_MEBIBYTES),
        cost_estimate=cost(2 * rows * width * (8 * ffn), 3 * width * ffn * 2 + rows * ffn * 8),
        name="feed_back_gate",
    )(place, grad, middle, gating, upward, gain, nf2, nf, dgu2, kept(weights_a), in_hbm(weights_gu),
      kept(weights_dn))


def leave_mixed_kernel(*refs):
    (place_ref, h_ref, dmid_ref, dq_ref, own_ref, got_ref, gain_ref, cos_ref, sin_ref, n1_ref, n2_ref,
     d1_ref, a1_ref, a2_ref, m1_ref, m2_ref, attention_gain_ref, ffn_gain_ref, ffn_gain2_ref, w_ref,
     g_ref, keep_ref, send_ref, d2_ref, dgain_ref, turned_ref, nt_ref, at_ref, gains_ref) = refs
    leave_kernel(
        h_ref, dmid_ref, dq_ref, own_ref, got_ref, gain_ref, cos_ref, sin_ref, w_ref, g_ref, d2_ref,
        dgain_ref, turned_ref,
    )
    gains = (attention_gain_ref[...] + dgain_ref[...], ffn_gain_ref[...] + ffn_gain2_ref[...])
    attention_grad_kernel(
        place_ref, n1_ref, n2_ref, d1_ref, d2_ref, a1_ref, a2_ref, m1_ref, m2_ref, gains, keep_ref,
        send_ref, nt_ref, at_ref, gains_ref,
    )


def leave_mixed(
    place, hidden, d_middle, dq, own, got, gain, cos, sin, normed, dqkv2, att, gm, gain_grads, weights_a
):
    rows, width = hidden.shape
    key_width = KEY_VALUE_HEADS * HEAD_SIZE
    wide = width + 2 * key_width + HEAD_SIZE
    block = width // 4 + GAIN_ROWS
    columns = 2 * width + 2 * key_width
    return pl.pallas_call(
        leave_mixed_kernel,
        out_shape=(shape((width, rows), bf16),)
        + (shape((2, 4, block, columns // 4), bf16),) * 2,
        in_specs=[in_smem()] + [in_vmem()] * 19,
        out_specs=(in_vmem(),) * 3,
        scratch_shapes=[
            pltpu.VMEM((rows, wide), bf16),
            pltpu.VMEM((1, width), f32),
            pltpu.VMEM((wide, rows), bf16),
            pltpu.VMEM((width, 2 * rows), bf16),
            pltpu.VMEM((width, 2 * rows), bf16),
            pltpu.VMEM((GAIN_ROWS, columns), f32),
        ],
        compiler_params=params(),
        cost_estimate=cost(6 * rows * width * wide, width * wide * 2 + rows * width * 14),
        name="leave_mixed",
    )(place, hidden, d_middle, dq, own, got, gain, cos, sin, *normed, dqkv2, *att, *gm, *gain_grads,
      kept(weights_a))


def down_grad_kernel(place_ref, g2_ref, g_ref, inner2_ref, inner_ref, keep_ref, send_ref, gt_ref):
    rows = g2_ref.shape[0]
    height, step = keep_ref.shape[2:]
    gt_ref[:, :rows] = g2_ref[...].T
    gt_ref[:, rows:] = g_ref[...].astype(bf16).T
    core, chip, quarter = place_ref[0], place_ref[1], place_ref[2]
    for away in range(2):
        for out_ref, which in ((keep_ref, core), (send_ref, 1 - core)):
            columns = pl.ds(pl.multiple_of((2 * (chip ^ away) + which) * step, 128), step)
            right = jnp.concatenate([inner2_ref[:, columns], inner_ref[:, columns]], axis=0)
            for part in range(4):
                out_ref[away, part ^ quarter] = nn(
                    gt_ref[part * height : (part + 1) * height, :], right
                ).astype(bf16)


def down_grad_parts(place, g2, g, inner2, inner):
    rows, width = g.shape
    ffn = inner.shape[1]
    return pl.pallas_call(
        down_grad_kernel,
        out_shape=(shape((2, 4, width // 4, ffn // 4), bf16),) * 2,
        in_specs=[in_smem()] + [in_vmem()] * 4,
        out_specs=(in_vmem(),) * 2,
        scratch_shapes=[pltpu.VMEM((width, 2 * rows), bf16)],
        compiler_params=params(),
        cost_estimate=cost(4 * rows * width * ffn, width * ffn * 2),
        name="down_grad",
    )(place, in_hbm(g2), g, in_hbm(inner2), in_hbm(inner))


def attention_grad_kernel(
    place_ref, n1_ref, n2_ref, d1_ref, d2_ref, a1_ref, a2_ref, m1_ref, m2_ref, gains,
    keep_ref, send_ref, nt_ref, at_ref, gains_ref,
):
    rows = n1_ref.shape[0]
    block = n1_ref.shape[1] // 4
    wide = d1_ref.shape[1]
    edge = wide - 128
    step = keep_ref.shape[3]
    nt_ref[:, :rows] = n1_ref[...].T
    nt_ref[:, rows:] = n2_ref[...].T
    at_ref[:, :rows] = a1_ref[...].T
    at_ref[:, rows:] = a2_ref[...].T
    half = GAIN_ROWS // 2
    gains_ref[...] = jnp.zeros_like(gains_ref)
    for i, gain in enumerate(gains):
        gains_ref[i * half : (i + 1) * half, : gain.shape[1]] = jnp.broadcast_to(
            gain, (half, gain.shape[1])
        )
    core, chip, quarter = place_ref[0], place_ref[1], place_ref[2]
    d_mixed = jnp.concatenate([d1_ref[...], d2_ref[...]], axis=0)
    d_out = jnp.concatenate([m1_ref[...], m2_ref[...]], axis=0)
    for away in range(2):
        for out_ref, which in ((keep_ref, core), (send_ref, 1 - core)):
            member = 2 * (chip ^ away) + which
            start = pl.multiple_of(member * block, 16)
            normed = nt_ref[pl.ds(start, block), :]
            attended = at_ref[pl.ds(start, block), :]
            for part in range(4):
                low, high = part * step, (part + 1) * step
                pieces = []
                if low < edge:
                    pieces.append(nn(normed, d_mixed[:, low : min(high, edge)]))
                if low <= edge < high:
                    pieces.append(nn(normed, d_mixed[:, edge:]) + nn(attended, d_out[:, :128]))
                if high > wide:
                    base = wide - 128
                    pieces.append(nn(attended, d_out[:, max(low, wide) - base : high - base]))
                piece = pieces[0] if len(pieces) == 1 else jnp.concatenate(pieces, axis=1)
                out_ref[away, part ^ quarter, :block, :] = piece.astype(bf16)
                out_ref[away, part ^ quarter, block:, :] = gains_ref[:, low:high].astype(bf16)


def finish_kernel(place_ref, p0_ref, p1_ref, p2_ref, p3_ref, out_ref):
    part = pl.program_id(0)
    for i, ref in enumerate((p0_ref, p1_ref, p2_ref, p3_ref)):

        @pl.when(part == i)
        def _(ref=ref):
            out_ref[...] = ref[...].astype(f32)


def finish(place, pieces, by_rows):
    height, step = pieces[0].shape
    whole = pl.BlockSpec((height, step), lambda i, place: (0, 0))
    if by_rows:
        dims, index = (4 * height, step), lambda i, place: (i ^ place[2], 0)
    else:
        dims, index = (height, 4 * step), lambda i, place: (0, i ^ place[2])
    return pl.pallas_call(
        finish_kernel,
        grid_spec=pltpu.PrefetchScalarGridSpec(
            num_scalar_prefetch=1,
            grid=(4,),
            in_specs=[whole] * 4,
            out_specs=pl.BlockSpec((height, step), index),
        ),
        out_shape=shape(dims, f32),
        compiler_params=params(),
        cost_estimate=cost(0, 24 * height * step),
        name="finish",
    )(place, *pieces)


def finish_mixed_kernel(
    place_ref, p0_ref, p1_ref, p2_ref, p3_ref, query_ref, key_ref, value_ref, out_ref, gain_ref,
    mixed_ref,
):
    quarter = place_ref[2]
    block, width = query_ref.shape
    key_width = key_ref.shape[0]
    step = p0_ref.shape[1]
    for i, ref in enumerate((p0_ref, p1_ref, p2_ref, p3_ref)):
        start = pl.multiple_of((quarter ^ i) * step, 128)
        mixed_ref[:, pl.ds(start, step)] = ref[...].astype(f32)
    first_end = width + key_width
    second_end = first_end + key_width
    query_ref[...] = mixed_ref[:block, :width]
    key_ref[...] = mixed_ref[:block, width:first_end].T
    value_ref[...] = mixed_ref[:block, first_end:second_end].T
    out_ref[...] = mixed_ref[:block, second_end:]
    gain_ref[...] = mixed_ref[block:, : gain_ref.shape[1]]


def finish_mixed(place, pieces, width, key_width):
    height, step = pieces[0].shape
    block = height - GAIN_ROWS
    return pl.pallas_call(
        finish_mixed_kernel,
        out_shape=(
            shape((block, width), f32),
            shape((key_width, block), f32),
            shape((key_width, block), f32),
            shape((block, width), f32),
            shape((GAIN_ROWS, width + HEAD_SIZE), f32),
        ),
        in_specs=[in_smem()] + [in_vmem()] * 4,
        out_specs=(in_vmem(),) * 5,
        scratch_shapes=[pltpu.VMEM((height, 4 * step), f32)],
        compiler_params=params(),
        cost_estimate=cost(0, 24 * height * step),
        name="finish_mixed",
    )(place, *pieces)


def flip(value, axis_name, distance):
    size = lax.axis_size(axis_name)
    return lax.ppermute(value, axis_name, [(i, i ^ distance) for i in range(size)])


def pick(condition, when_true, when_false):
    return jnp.where(condition, when_true, when_false)


def order_by(bit, own, other):
    return (pick(bit == 1, other, own), pick(bit == 1, own, other))


def exchange_kv(block):
    beside = flip(block, "fsdp", 1)
    across = flip(block, "fsdp", 2)
    diagonal = flip(across, "fsdp", 1)
    return (block, beside, across, diagonal)


def fold_kv(keep, send):
    got = flip(send, "fsdp", 1)
    return total(keep[0], got[0]), total(keep[1], got[1])


def return_kv(keep, send):
    own, across = fold_kv(keep, send)
    return own, flip(across, "fsdp", 2)


def total(*terms):
    result = terms[0].astype(f32)
    for term in terms[1:]:
        result = result + term.astype(f32)
    return result.astype(bf16)


class Order:
    def __init__(self, *token):
        self.token = token

    def tie(self, *values):
        tied = lax.optimization_barrier(self.token + values)[len(self.token) :]
        return tied[0] if len(tied) == 1 else tied

    def done(self, value):
        self.token = (value,)
        return value

    def done_all(self, *values):
        self.token = values
        return values


class Reduction:
    def __init__(self, order, keep, send):
        self.order = order
        self.keep = keep
        self.core = flip(order.tie(send), "fsdp", 1)

    def chip(self):
        self.core = self.order.tie(self.core)
        high = total(self.keep[1, 2:], self.core[1, 2:])
        low = total(self.keep[1, :2], self.core[1, :2])
        high, low = self.order.done_all(high, low)
        self.high = flip(high, "fsdp", 2)
        self.low = flip(low, "fsdp", 2)

    def first(self, both=False):
        if both:
            self.high, self.low = self.order.tie(self.high, self.low)
        else:
            self.high = self.order.tie(self.high)
        out = total(self.keep[0, 2:], self.core[0, 2:], self.high)
        self.got = flip(self.order.done(out), "dp", 1)

    def rest(self):
        self.low = self.order.done(self.order.tie(self.low))

    def second(self):
        self.got, self.low = self.order.tie(self.got, self.low)
        self.terms = (self.keep[0, :2], self.core[0, :2], self.low, self.got)
        self.got = flip(self.order.done(total(*[term[1] for term in self.terms])), "dp", 2)

    def third(self):
        size = lax.axis_size("dp")
        own = total(*[term[0] for term in self.terms], self.order.tie(self.got))
        distance = 4
        while 2 * distance < size:
            own = total(own, flip(own, "dp", distance))
            distance *= 2
        self.own = self.order.done(own)
        self.got = flip(own, "dp", distance) if distance < size else jnp.zeros_like(own)

    def back(self):
        self.own = self.order.done(total(self.own, self.order.tie(self.got)))
        self.beside = flip(self.own, "dp", 2)
        self.pieces = [self.own, self.beside, flip(self.own, "dp", 1)]

    def back_again(self):
        self.beside = self.order.done(self.order.tie(self.beside))
        self.pieces.append(flip(self.beside, "dp", 1))

    def end(self):
        return self.order.tie(*self.pieces)


def rotation(token_positions):
    frequency = rope_base ** (-jnp.arange(HALF, dtype=f32) / HALF)
    angles = frequency[:, None] * token_positions.astype(f32)[None, :]
    return jnp.cos(angles), jnp.sin(angles)


def body(
    tokens,
    cotangent,
    sequence_ids,
    span_position,
    attention_norm,
    query_weight,
    key_matrix,
    value_matrix,
    output_weight,
    feedforward_norm,
    gate_weight,
    up_weight,
    down_weight,
):
    rows, width = tokens.shape
    key_width = key_matrix.shape[1]
    ffn = gate_weight.shape[1]
    itself = lax.axis_index("fsdp")
    outer = lax.axis_index("dp")
    quarter = 2 * (outer % 2) + (outer // 2) % 2
    place = jnp.stack([itself % 2, itself // 2, quarter]).astype(jnp.int32)

    outer = lax.axis_index("dp")
    bits = jnp.stack([outer % 2, (outer // 2) % 2, itself]).astype(jnp.int32)
    packed, *mine = pack(
        bits, query_weight, key_matrix.T, value_matrix.T, output_weight, gate_weight, up_weight
    )
    down_t = down_weight.T
    half = width // 2
    mine.append(pick(outer % 2 == 1, down_t[half:], down_t[:half]))
    gains = jnp.stack([attention_norm, feedforward_norm], axis=0)
    gains = [flip(gains, "fsdp", distance) if distance else gains for distance in range(4)]
    mine = Order(*gains).tie(*mine)
    far = [flip(piece, "fsdp", 2) for piece in mine]
    shards = (packed, gate_weight, up_weight, down_t)
    near = [flip(shard, "fsdp", 1) for shard in shards]
    sequence_ids, span_position = Order(*mine).tie(sequence_ids, span_position)
    places = jnp.arange(rows, dtype=jnp.int32) + span_position[itself] * rows
    cos, sin = rotation(places)
    others = itself ^ jnp.arange(4)
    visible = (
        (sequence_ids[others] == sequence_ids[itself])
        & (span_position[others] <= span_position[itself])
    ).astype(jnp.int32)

    beside = order_by(itself % 2, gains[0], gains[1])
    away = order_by(itself % 2, gains[2], gains[3])
    chip = itself // 2 == 1
    gains = jnp.concatenate(
        [pick(chip, a, n) for a, n in zip(away, beside)]
        + [pick(chip, n, a) for a, n in zip(away, beside)],
        axis=1,
    ).astype(f32)
    attention_gain, ffn_gain = gains[:1], gains[1:]
    order = Order(cos, sin, visible, attention_gain, ffn_gain)
    share = ((1, 0), (1, 0), (2, 1), (1, 0))

    def shared(i):
        got = order.done(order.tie(far[i]))
        return got, flip(got, "dp", share[i][0])

    def gathered(i, got, other):
        return [shards[i], near[i], got, other, flip(got, "fsdp", 1), flip(other, "fsdp", 1)]

    shared_a = shared(0)
    order.done_all(*order.tie(*shared_a))
    shared_gate = shared(1)
    sources_a = gathered(0, *shared_a)
    order.done_all(*order.tie(*near), *sources_a)
    tokens_t = order.tie(tokens.T)
    hidden, normed, q, kv, weights_a = enter_first(
        bits, tokens_t, attention_gain, cos, sin, shared_plan(0, 0, 0), tuple(sources_a)
    )
    order.done(kv)
    shared_up = shared(2)
    shared_gate = order.done_all(*order.tie(*shared_gate))
    kvs = exchange_kv(kv)
    shared_down = shared(3)
    order.done_all(*order.tie(*shared_up))
    sources_gu = gathered(1, *shared_gate) + gathered(2, *shared_up)
    sources_dn = gathered(3, *order.tie(*shared_down))
    plan_gu = shared_plan(0, 0, 0) + shared_plan(6, ffn, 1)
    plan_dn = shared_plan(0, None, 0)
    finished, att, att_t, lse, middle, nf, gating, upward, inner, weights_gu, weights_dn = forward_block(
        visible, bits, hidden, q, kvs, ffn_gain, weights_a, tuple(sources_gu), tuple(sources_dn),
        (plan_gu, plan_dn),
    )
    weights = (weights_a, weights_gu, weights_dn)
    saved = [(hidden, normed, q, kvs, att, att_t, lse, middle, nf, gating, upward, inner)]
    hidden = finished
    normed, q, kv = enter(hidden, attention_gain, cos, sin, weights_a)
    kvs = exchange_kv(kv)
    activations, att, att_t, lse, middle, nf, gating, upward, inner = forward_block(
        visible, bits, hidden, q, kvs, ffn_gain, weights_a, (weights_gu,), (weights_dn,)
    )
    saved.append((hidden, normed, q, kvs, att, att_t, lse, middle, nf, gating, upward, inner))

    hidden, normed2, q, kvs, att2, att_t, lse, middle, nf2, gating, upward, inner2 = saved[1]
    gb2, dgu2, d_middle, gm2, d_out, ffn_gain_grad2 = feed_back(
        cotangent.T, middle, gating, upward, ffn_gain, weights
    )
    dq, *dkvs = attend_back(visible, q, d_out, att_t, lse, cos, sin, kvs)
    own, got = return_kv(*dkvs)
    grad, dqkv2, attention_gain_grad2 = leave(
        hidden, d_middle, dq, own, got, attention_gain, cos, sin, weights_a
    )

    hidden, normed, q, kvs, att, att_t, lse, middle, nf, gating, upward, inner = saved[0]
    order = Order(grad)
    down = Reduction(order, *down_grad_parts(place, gb2, grad, inner2, inner))
    down.chip()
    d_middle, gm, d_out, ffn_gain_grad, *rest = feed_back_gate(
        place, order.tie(grad), middle, gating, upward, ffn_gain, nf2, nf, dgu2, weights
    )
    order.done(d_middle)
    down.first()
    gate = Reduction(order, *rest[:2])
    gate.chip()
    down.rest()
    up = Reduction(order, *rest[2:])
    dq, *dkvs = attend_back(visible, order.tie(q), d_out, att_t, lse, cos, sin, kvs)
    order.done(dq)
    gate.first()
    down.second()
    own, across = fold_kv(*order.tie(*dkvs))
    order.done(across)
    gate.rest()
    down.third()
    across = order.tie(across)
    got = order.done(order.tie(flip(across, "fsdp", 2)))
    gate.second()
    up.chip()
    d_middle = order.tie(d_middle)
    grad, *mixed = leave_mixed(
        place,
        hidden,
        d_middle,
        dq,
        own,
        got,
        attention_gain,
        cos,
        sin,
        (normed2, normed),
        dqkv2,
        (att2, att),
        (gm2, gm),
        (attention_gain_grad2, ffn_gain_grad2, ffn_gain_grad),
        weights_a,
    )
    order.done(grad)
    up.first()
    down.back()
    gate.third()
    mixed = Reduction(order, *mixed)
    mixed.chip()
    up.second()
    down.back_again()
    down_grad = order.done(finish(place, down.end(), True))
    mixed.first()
    gate.back()
    up.third()
    mixed.rest()
    mixed.second()
    gate.back_again()
    up.back()
    mixed.third()
    gate_grad = order.done(finish(place, gate.end(), False))
    up.back_again()
    up_grad = order.done(finish(place, up.end(), False))
    mixed.back()
    mixed.back_again()
    query_grad, key_grad, value_grad, output_grad, gain_grads = finish_mixed(
        place, mixed.end(), width, key_width
    )
    shard_rows = attention_norm.shape[0]
    gain_grads = lax.dynamic_slice_in_dim(gain_grads, itself * shard_rows, shard_rows, axis=1)
    return (
        activations.T,
        grad.T,
        gain_grads[0],
        query_grad,
        key_grad.T,
        value_grad.T,
        output_grad,
        gain_grads[GAIN_ROWS // 2],
        gate_grad,
        up_grad,
        down_grad.T,
    )


def solution(mesh):
    return jax.shard_map(
        body,
        mesh=mesh,
        in_specs=(
            P(("dp", "fsdp"), None),
            P(("dp", "fsdp"), None),
            P("dp"),
            P("dp"),
            P("fsdp"),
            P("fsdp", None),
            P("fsdp", None),
            P("fsdp", None),
            P("fsdp", None),
            P("fsdp"),
            P("fsdp", None),
            P("fsdp", None),
            P("fsdp", None),
        ),
        out_specs=(
            P(("dp", "fsdp"), None),
            P(("dp", "fsdp"), None),
            P("fsdp"),
            P("fsdp", None),
            P("fsdp", None),
            P("fsdp", None),
            P("fsdp", None),
            P("fsdp"),
            P("fsdp", None),
            P("fsdp", None),
            P("fsdp", None),
        ),
        check_vma=False,
    )
```
